32 devices in a mesh: cuts: 8 (over z, x), stem: 4 (over y, core).
Axes of the slice: x: 2, y: 2, z: 4, core: 2. Of those that a mesh axis runs over, the one named last changes fastest.
Arguments:
- stem_tensor: bfloat16 [8, 64, 1024], P('stem'), may hold values from -6 to 6
- mid_tensors: bfloat16 [512, 512, 128], P(('cuts', 'stem')), may hold values from -0.1875 to 0.1875
- right_tensors: bfloat16 [8, 512, 64, 128], P(None, ('cuts', 'stem')), may hold values from -0.0078125 to 0.0078125
Outputs:
- amplitudes: float32 [8192], P('cuts')
The draws below stay inside these ranges and needn't reach their ends.
All inputs are finite; a program needn't handle non-finite values.
Results may differ from the reference program's by a relative error of at most 0.0029.
Values may be sent and summed in bfloat16 or wider, within the bound.
No kernel may reach another device: no remote copies, remote signals or barrier semaphores. Data moves between devices by JAX's collectives and lax.ppermute only.
A program may use at most 64 MiB of HBM per device.

```python
import jax
import jax.numpy as jnp
from jax import lax

A = 64
B = 64
K = 512
R = 64
C = 8
MT = 16
BRANCHES = 512
TERMS = 524288


def block_scale(stream_key, shape, shards, smallest, high):
    gain, own = 1.0, jax.random.fold_in(stream_key, 6)
    for axis_at, shards_of in shards:
        heights = jnp.exp(jax.random.uniform(jax.random.fold_in(own, axis_at), (shards_of,), jnp.float32, smallest / len(shards), high / len(shards)))
        gain = gain * jnp.repeat(heights, shape[axis_at] // shards_of).reshape([-1 if axis == axis_at else 1 for axis in range(len(shape))])
    return gain


def bell_draw(own_key, dims, width, limit, split=(), held_as=jnp.bfloat16):
    level = block_scale(own_key, dims, split, -0.22, 0.18) if split else 1.0
    array = jax.random.normal(own_key, dims, jnp.float32) * width * level
    return jnp.minimum(jnp.maximum(array, -limit), limit).astype(held_as)


def setup_inputs(seed: int = 0) -> dict:
    key_of = jax.random.split(jax.random.key(seed), 4)
    return {
        "stem_tensor": bell_draw(key_of[0], (C, A, 2 * K), 1.0, 6.0, ((0, 4),)),
        "mid_tensors": bell_draw(key_of[1], (BRANCHES, K, 2 * R), (2 * K) ** -0.5, 0.1875, ((0, 32),)),
        "right_tensors": bell_draw(key_of[2], (C, BRANCHES, R, 2 * B), TERMS ** -0.5, 0.0078125, ((1, 32),)),
    }


def widen(tensor):
    half_width = tensor.shape[-1] // 2
    real_part = tensor[..., :half_width]
    imag_part = tensor[..., half_width:]
    upper_rows = jnp.concatenate([real_part, imag_part], axis=-1)
    lower_rows = jnp.concatenate([-imag_part, real_part], axis=-1)
    return jnp.concatenate([upper_rows, lower_rows], axis=-2)


def reference(stem_tensor, mid_tensors, right_tensors):
    group_count = mid_tensors.shape[0] // MT
    stem_rows = stem_tensor.reshape(C * A, 2 * K)
    mid_groups = mid_tensors.reshape(group_count, MT, K, 2 * R)
    right_groups = jnp.moveaxis(right_tensors.reshape(C, group_count, MT, R, 2 * B), 1, 0)

    def accumulate(running, paired):
        mid_block, right_block = paired
        widened = jnp.moveaxis(widen(mid_block), 0, 1).reshape(2 * K, MT * 2 * R)
        first_step = jnp.dot(stem_rows, widened, preferred_element_type=jnp.float32).astype(jnp.bfloat16)
        first_step = lax.optimization_barrier(first_step).astype(jnp.float32).reshape(C, A, MT * 2 * R)
        right_wide = widen(right_block).reshape(C, MT * 2 * R, 2 * B).astype(jnp.float32)
        update = jnp.einsum("iaq,iqb->ab", first_step, right_wide, precision=lax.Precision.HIGHEST)
        return running + update, None

    running, _ = lax.scan(accumulate, jnp.zeros((A, 2 * B), jnp.float32), (mid_groups, right_groups))
    return running.reshape(2 * A * B)
```

```python
import functools

import jax
import jax.numpy as jnp
from jax import lax
from jax.experimental import pallas as pl
from jax.experimental.pallas import tpu as pltpu
from jax.sharding import PartitionSpec as P


def turn(x):
    half = x.shape[-1] // 2
    lane = lax.broadcasted_iota(jnp.int32, x.shape, x.ndim - 1)
    rolled = pltpu.roll(x, half, x.ndim - 1)
    return jnp.where(lane < half, -rolled, rolled)


def branch_kernel(place_ref, mid_ref, right_ref, out_ref):
    pairs, _, width = mid_ref.shape
    blocks = right_ref.shape[0]
    left = jnp.concatenate([mid_ref[j] for j in range(pairs)], axis=1)
    columns = []
    for i in range(blocks):
        rows = []
        for j in range(pairs):
            w = right_ref[i, j]
            rows += [w, turn(w.astype(jnp.float32)).astype(w.dtype)]
        columns.append(jnp.concatenate(rows, axis=0))
    wide = jnp.concatenate(columns, axis=1)
    full = jnp.dot(left, wide, preferred_element_type=jnp.float32)
    high = full.astype(jnp.bfloat16)
    low = (full - high.astype(jnp.float32)).astype(jnp.bfloat16)
    for i in range(blocks):
        cols = slice(i * width, (i + 1) * width)
        out_ref[i] = jnp.concatenate([high[:, cols], low[:, cols]], axis=1)


def branch_sums(place, mid, right, stems):
    pairs, depth, width = mid.shape
    blocks = right.shape[0] // stems
    flops = 2 * depth * pairs * width * right.shape[0] * width
    return pl.pallas_call(
        branch_kernel,
        grid_spec=pltpu.PrefetchScalarGridSpec(
            num_scalar_prefetch=1,
            grid=(stems,),
            in_specs=[
                pl.BlockSpec(mid.shape, lambda p, place: (0, 0, 0)),
                pl.BlockSpec((blocks,) + right.shape[1:], lambda p, place: (place[0] ^ p, 0, 0, 0)),
            ],
            out_specs=pl.BlockSpec((blocks, depth, 2 * width), lambda p, place: (p, 0, 0)),
        ),
        out_shape=jax.ShapeDtypeStruct((right.shape[0], depth, 2 * width), jnp.bfloat16),
        compiler_params=pltpu.CompilerParams(vmem_limit_bytes=40 * 1024 * 1024),
        cost_estimate=pl.CostEstimate(flops=flops, bytes_accessed=6 << 20, transcendentals=0),
        name="branch_sums",
    )(place, mid, right)


def close_kernel(*refs):
    *stem_refs, sums_ref, out_ref = refs
    total = None
    at = 0
    for ref in stem_refs:
        for i in range(ref.shape[0]):
            block = ref[i]
            half = block.shape[-1] // 2
            rows = jnp.concatenate([block[:, :half], block[:, half:]], axis=0)
            term = jnp.dot(rows, sums_ref[at], preferred_element_type=jnp.float32)
            total = term if total is None else total + term
            at += 1
    width = total.shape[-1] // 2
    total = total[:, :width] + total[:, width:]
    half = total.shape[0] // 2
    out_ref[...] = total[:half] + turn(total[half:])


def close(stem_pieces, sums):
    rows = stem_pieces[0].shape[1]
    width = sums.shape[-1] // 2
    return pl.pallas_call(
        close_kernel,
        out_shape=jax.ShapeDtypeStruct((rows, width), jnp.float32),
        compiler_params=pltpu.CompilerParams(vmem_limit_bytes=40 * 1024 * 1024),
        cost_estimate=pl.CostEstimate(flops=4 * rows * sums.size, bytes_accessed=3 << 20, transcendentals=0),
        name="close",
    )(*stem_pieces, sums)


def on_device(stem_tensor, mid_tensors, right_tensors):
    stems = lax.axis_size("stem")
    cuts = lax.axis_size("cuts")

    def swap(x, p):
        return lax.ppermute(x, "stem", [(s, s ^ p) for s in range(stems)])

    pieces = [stem_tensor]
    step = stems // 2
    pieces = {0: stem_tensor}
    while step:
        for p in list(pieces):
            pieces[p ^ step] = swap(pieces[p], step)
        step //= 2
    place = lax.axis_index("stem").astype(jnp.int32).reshape(1)
    sums = branch_sums(place, mid_tensors, right_tensors, stems)
    partial_sum = close([pieces[p] for p in range(stems)], sums)
    blocks = partial_sum.reshape(cuts, 1, -1)
    spread = jnp.broadcast_to(blocks, (cuts, stems, blocks.shape[-1])).reshape(cuts * stems, -1)
    got = lax.all_to_all(spread, ("cuts", "stem"), 0, 0, tiled=True)
    return jnp.sum(got, axis=0)


def solution(mesh):
    return jax.shard_map(
        on_device,
        mesh=mesh,
        in_specs=(
            P("stem", None, None),
            P(("cuts", "stem"), None, None),
            P(None, ("cuts", "stem"), None, None),
        ),
        out_specs=P("cuts"),
        check_vma=False,
    )
```

```python
import jax
import jax.numpy as jnp
from jax import lax
from jax.experimental import pallas as pl
from jax.experimental.pallas import tpu as pltpu
from jax.sharding import PartitionSpec as P

VMEM_LIMIT = 52 * 1024 * 1024


def turn(x):
    half = x.shape[-1] // 2
    lane = lax.broadcasted_iota(jnp.int32, x.shape, x.ndim - 1)
    rolled = pltpu.roll(x, half, x.ndim - 1)
    return jnp.where(lane < half, -rolled, rolled)


def two_parts(full):
    high = full.astype(jnp.bfloat16)
    low = (full - high.astype(jnp.float32)).astype(jnp.bfloat16)
    return jnp.concatenate([high, low], axis=1)


def apply_stem(block, sums):
    half = block.shape[-1] // 2
    rows = jnp.concatenate([block[:, :half], block[:, half:]], axis=0)
    both = jnp.dot(rows, two_parts(sums), preferred_element_type=jnp.float32)
    width = both.shape[-1] // 2
    return both[:, :width] + both[:, width:]


def branch_kernel(mid_hbm, right_hbm, own_ref, near_ref, kept_ref, sent_ref, part_ref,
                  mid_ref, right_ref, mid_sem, right_sem):
    pairs, depth, width = mid_ref.shape
    blocks = own_ref.shape[0]
    groups = right_ref.shape[0] // blocks
    me = lax.axis_index("stem")
    mid_copies = [
        pltpu.make_async_copy(mid_hbm.at[pl.ds(j, 4)], mid_ref.at[pl.ds(j, 4)], mid_sem.at[j // 4])
        for j in range(0, pairs, 4)
    ]
    right_copies = [
        pltpu.make_async_copy(
            right_hbm.at[pl.ds((me ^ p) * blocks, blocks)], right_ref.at[pl.ds(p * blocks, blocks)], right_sem.at[p]
        )
        for p in range(groups)
    ]
    order = list(range(groups - 1, -1, -1))
    right_copies[order[0]].start()
    for copy in mid_copies:
        copy.start()
    for p in order[1:]:
        right_copies[p].start()
    for copy in mid_copies:
        copy.wait()
    part = None
    for p in order:
        right_copies[p].wait()
        left = jnp.concatenate([mid_ref[j] for j in range(pairs)], axis=1)
        columns = []
        for b in range(blocks):
            rows = []
            for j in range(pairs):
                w = right_ref[p * blocks + b, j]
                rows += [w, turn(w.astype(jnp.float32)).astype(w.dtype)]
            columns.append(jnp.concatenate(rows, axis=0))
        sums = jnp.dot(left, jnp.concatenate(columns, axis=1), preferred_element_type=jnp.float32)
        for b in range(blocks):
            one = sums[:, b * width:(b + 1) * width]
            if p < 2:
                term = apply_stem((own_ref, near_ref)[p][b], one)
                part = term if part is None else part + term
            elif p % 2:
                sent_ref[(p // 2 - 1) * blocks + b] = one.astype(jnp.bfloat16)
            else:
                kept_ref[(p // 2 - 1) * blocks + b] = one
    part_ref[...] = part


def branch_sums(mid, right, own, near):
    pairs, depth, width = mid.shape
    total = right.shape[0]
    blocks, rows, _ = own.shape
    groups = total // blocks
    far = (groups // 2 - 1) * blocks
    vmem = pl.BlockSpec(memory_space=pltpu.VMEM)
    hbm = pl.BlockSpec(memory_space=pltpu.HBM)
    return pl.pallas_call(
        branch_kernel,
        in_specs=[hbm, hbm, vmem, vmem],
        out_specs=[vmem, vmem, vmem],
        out_shape=[
            jax.ShapeDtypeStruct((far, depth, width), jnp.float32),
            jax.ShapeDtypeStruct((far, depth, width), jnp.bfloat16),
            jax.ShapeDtypeStruct((2 * rows, width), jnp.float32),
        ],
        scratch_shapes=[
            pltpu.VMEM(mid.shape, mid.dtype),
            pltpu.VMEM(right.shape, right.dtype),
            pltpu.SemaphoreType.DMA((pairs // 4,)),
            pltpu.SemaphoreType.DMA((groups,)),
        ],
        compiler_params=pltpu.CompilerParams(vmem_limit_bytes=VMEM_LIMIT),
        cost_estimate=pl.CostEstimate(
            flops=2 * depth * pairs * width * total * width, bytes_accessed=6 << 20, transcendentals=0
        ),
        name="branch_sums",
    )(mid, right, own, near)


def close_kernel(*refs):
    *far_refs, kept_ref, got_ref, part_ref, out_ref = refs
    part = part_ref[...]
    at = 0
    for ref in far_refs:
        for b in range(ref.shape[0]):
            part += apply_stem(ref[b], kept_ref[at] + got_ref[at].astype(jnp.float32))
            at += 1
    half = part.shape[0] // 2
    out_ref[...] = part[:half] + turn(part[half:])


def close(far, kept, got, part):
    rows, width = part.shape[0] // 2, part.shape[1]
    return pl.pallas_call(
        close_kernel,
        out_shape=jax.ShapeDtypeStruct((rows, width), jnp.float32),
        compiler_params=pltpu.CompilerParams(vmem_limit_bytes=VMEM_LIMIT // 2),
        cost_estimate=pl.CostEstimate(flops=8 * rows * kept.size, bytes_accessed=1 << 20, transcendentals=0),
        name="close",
    )(*far, kept, got, part)


def on_device(stem_tensor, mid_tensors, right_tensors):
    stems = lax.axis_size("stem")
    cuts = lax.axis_size("cuts")

    def swap(x, p):
        return lax.ppermute(x, "stem", [(s, s ^ p) for s in range(stems)])

    far = [swap(stem_tensor, p) for p in range(2, stems, 2)]
    near = swap(stem_tensor, 1)
    kept, sent, part = branch_sums(mid_tensors, right_tensors, stem_tensor, near)
    got = swap(sent, 1)
    partial_sum = close(far, kept, got, part)
    spread = lax.all_to_all(partial_sum.reshape(cuts, -1), "cuts", 0, 0, tiled=True)
    amplitudes = jnp.sum(spread, axis=0)
    step = 1
    while step < stems:
        amplitudes = amplitudes + swap(amplitudes, step)
        step *= 2
    return amplitudes


def solution(mesh):
    return jax.shard_map(
        on_device,
        mesh=mesh,
        in_specs=(
            P("stem", None, None),
            P(("cuts", "stem"), None, None),
            P(None, ("cuts", "stem"), None, None),
        ),
        out_specs=P("cuts"),
        check_vma=False,
    )
```

```python
import jax
import jax.numpy as jnp
from jax import lax
from jax.experimental import pallas as pl
from jax.experimental.pallas import tpu as pltpu
from jax.sharding import PartitionSpec as P

MIB = 1024 * 1024


def turn(x):
    half = x.shape[-1] // 2
    lane = lax.broadcasted_iota(jnp.int32, x.shape, x.ndim - 1)
    rolled = pltpu.roll(x, half, x.ndim - 1)
    return jnp.where(lane < half, -rolled, rolled)


def branch_kernel(mid_hbm, right_hbm, kept_ref, *refs):
    *sent_refs, mid_ref, right_ref, mid_sem, right_sem = refs
    pairs, depth, width = mid_ref.shape
    groups = right_sem.shape[0]
    half = groups // 2
    blocks = right_ref.shape[0] // groups
    me = lax.axis_index("stem")
    chunk = pairs // mid_sem.shape[0]

    def mid_copy(n):
        at = pl.ds(n * chunk, chunk)
        return pltpu.make_async_copy(mid_hbm.at[at], mid_ref.at[at], mid_sem.at[n])

    def right_copy(q):
        p = jnp.where(q < half, 2 * q + 1, 2 * q - groups)
        source = right_hbm.at[pl.ds((me ^ p) * blocks, blocks)]
        return pltpu.make_async_copy(source, right_ref.at[pl.ds(q * blocks, blocks)], right_sem.at[q])

    for n in range(mid_sem.shape[0]):
        mid_copy(n).start()
    for q in range(groups):
        right_copy(q).start()
    for n in range(mid_sem.shape[0]):
        mid_copy(n).wait()

    def group(q, carry):
        right_copy(q).wait()
        left = jnp.concatenate([mid_ref[j] for j in range(pairs)], axis=1)
        columns = []
        for b in range(blocks):
            rows = []
            for j in range(pairs):
                w = right_ref[q * blocks + b, j]
                rows += [w, turn(w.astype(jnp.float32)).astype(w.dtype)]
            columns.append(jnp.concatenate(rows, axis=0))
        sums = jnp.dot(left, jnp.concatenate(columns, axis=1), preferred_element_type=jnp.float32)

        for at in range(half):
            @pl.when(q == at)
            def _():
                for b in range(blocks):
                    part = sums[:, b * width:(b + 1) * width]
                    sent_refs[at * blocks + b][...] = part.astype(jnp.bfloat16)

        @pl.when(q >= half)
        def _():
            for b in range(blocks):
                kept_ref[(q - half) * blocks + b] = sums[:, b * width:(b + 1) * width]

        return carry

    lax.fori_loop(0, groups, group, 0)


def branch_sums(mid, right, groups):
    pairs, depth, width = mid.shape
    total = right.shape[0]
    vmem = pl.BlockSpec(memory_space=pltpu.VMEM)
    hbm = pl.BlockSpec(memory_space=pltpu.HBM)
    return pl.pallas_call(
        branch_kernel,
        in_specs=[hbm, hbm],
        out_specs=[vmem] * (1 + total // 2),
        out_shape=[
            jax.ShapeDtypeStruct((total // 2, depth, width), jnp.float32),
        ] + [jax.ShapeDtypeStruct((depth, width), jnp.bfloat16)] * (total // 2),
        scratch_shapes=[
            pltpu.VMEM(mid.shape, mid.dtype),
            pltpu.VMEM(right.shape, right.dtype),
            pltpu.SemaphoreType.DMA((4,)),
            pltpu.SemaphoreType.DMA((groups,)),
        ],
        compiler_params=pltpu.CompilerParams(vmem_limit_bytes=52 * MIB),
        cost_estimate=pl.CostEstimate(
            flops=2 * depth * pairs * width * total * width, bytes_accessed=6 * MIB, transcendentals=0
        ),
        name="branch_sums",
    )(mid, right)


def close_kernel(*refs):
    *more, kept_ref, out_ref = refs
    stem_refs, got_refs = more[:-kept_ref.shape[0]], more[-kept_ref.shape[0]:]
    part = None
    at = 0
    for ref in stem_refs:
        for b in range(ref.shape[0]):
            block = ref[b]
            half = block.shape[-1] // 2
            rows = jnp.concatenate([block[:, :half], block[:, half:]], axis=0)
            sums = kept_ref[at] + got_refs[at][...].astype(jnp.float32)
            high = sums.astype(jnp.bfloat16)
            low = (sums - high.astype(jnp.float32)).astype(jnp.bfloat16)
            term = jnp.dot(rows, jnp.concatenate([high, low], axis=1), preferred_element_type=jnp.float32)
            part = term if part is None else part + term
            at += 1
    width = part.shape[1] // 2
    part = part[:, :width] + part[:, width:]
    half = part.shape[0] // 2
    total = part[:half] + turn(part[half:])
    if len(out_ref.shape) == 2:
        out_ref[...] = total
    else:
        cuts, copies, rows, _ = out_ref.shape
        for c in range(cuts):
            for s in range(copies):
                out_ref[c, s] = total[c * rows:(c + 1) * rows]


def close(stems, kept, got, cuts, copies):
    rows, width = stems[0].shape[1], kept.shape[2]
    whole_tiles = rows % (8 * cuts) == 0
    shape = (cuts, copies, rows // cuts, width) if whole_tiles else (rows, width)
    out = pl.pallas_call(
        close_kernel,
        out_shape=jax.ShapeDtypeStruct(shape, jnp.float32),
        compiler_params=pltpu.CompilerParams(vmem_limit_bytes=24 * MIB),
        cost_estimate=pl.CostEstimate(flops=8 * rows * kept.size, bytes_accessed=MIB, transcendentals=0),
        name="close",
    )(*stems, *got, kept)
    if whole_tiles:
        return out.reshape(cuts * copies, rows // cuts, width)
    out = out.reshape(cuts, 1, -1)
    return jnp.broadcast_to(out, (cuts, copies, out.shape[-1])).reshape(cuts * copies, -1)


def on_device(stem_tensor, mid_tensors, right_tensors):
    stems = lax.axis_size("stem")
    cuts = lax.axis_size("cuts")

    def swap(x, p):
        return lax.ppermute(x, "stem", [(s, s ^ p) for s in range(stems)])

    pieces = [stem_tensor] + [swap(stem_tensor, p) for p in range(2, stems, 2)]
    kept, *sent = branch_sums(mid_tensors, right_tensors, stems)
    got = [swap(x, 1) for x in sent]
    spread = close(pieces, kept, got, cuts, stems)
    parts = lax.all_to_all(spread, ("cuts", "stem"), 0, 0, tiled=True)
    return jnp.sum(parts, axis=0).reshape(-1)


def solution(mesh):
    return jax.shard_map(
        on_device,
        mesh=mesh,
        in_specs=(
            P("stem", None, None),
            P(("cuts", "stem"), None, None),
            P(None, ("cuts", "stem"), None, None),
        ),
        out_specs=P("cuts"),
        check_vma=False,
    )
```

```python
import jax
import jax.numpy as jnp
from jax import lax
from jax.experimental import pallas as pl
from jax.experimental.pallas import tpu as pltpu
from jax.sharding import PartitionSpec as P

MIB = 1024 * 1024


def turn(x):
    half = x.shape[-1] // 2
    lane = lax.broadcasted_iota(jnp.int32, x.shape, x.ndim - 1)
    rolled = pltpu.roll(x, half, x.ndim - 1)
    return jnp.where(lane < half, -rolled, rolled)


def branch_kernel(mid_hbm, right_hbm, kept_ref, *refs):
    *sent_refs, mid_ref, right_ref, mid_sem, right_sem = refs
    pairs, depth, width = mid_ref.shape
    groups = right_sem.shape[0]
    half = groups // 2
    blocks = right_ref.shape[0] // groups
    me = lax.axis_index("stem")
    chunk = pairs // mid_sem.shape[0]

    def mid_copy(n):
        at = pl.ds(n * chunk, chunk)
        return pltpu.make_async_copy(mid_hbm.at[at], mid_ref.at[at], mid_sem.at[n])

    def right_copy(q):
        p = jnp.where(q < half, 2 * q + 1, 2 * q - groups)
        source = right_hbm.at[pl.ds((me ^ p) * blocks, blocks)]
        return pltpu.make_async_copy(source, right_ref.at[pl.ds(q * blocks, blocks)], right_sem.at[q])

    for n in range(mid_sem.shape[0]):
        mid_copy(n).start()
    for q in range(groups):
        right_copy(q).start()
    for n in range(mid_sem.shape[0]):
        mid_copy(n).wait()

    def group(q, carry):
        right_copy(q).wait()
        left = jnp.concatenate([mid_ref[j] for j in range(pairs)], axis=1)
        columns = []
        for b in range(blocks):
            rows = []
            for j in range(pairs):
                w = right_ref[q * blocks + b, j]
                rows += [w, turn(w.astype(jnp.float32)).astype(w.dtype)]
            columns.append(jnp.concatenate(rows, axis=0))
        sums = jnp.dot(left, jnp.concatenate(columns, axis=1), preferred_element_type=jnp.float32)

        for at in range(half):
            @pl.when(q == at)
            def _():
                for b in range(blocks):
                    part = sums[:, b * width:(b + 1) * width]
                    sent_refs[at * blocks + b][...] = part.astype(jnp.bfloat16)

        @pl.when(q >= half)
        def _():
            for b in range(blocks):
                kept_ref[(q - half) * blocks + b] = sums[:, b * width:(b + 1) * width]

        return carry

    lax.fori_loop(0, groups, group, 0)


def branch_sums(mid, right, groups):
    pairs, depth, width = mid.shape
    total = right.shape[0]
    vmem = pl.BlockSpec(memory_space=pltpu.VMEM)
    hbm = pl.BlockSpec(memory_space=pltpu.HBM)
    return pl.pallas_call(
        branch_kernel,
        in_specs=[hbm, hbm],
        out_specs=[vmem] * (1 + total // 2),
        out_shape=[
            jax.ShapeDtypeStruct((total // 2, depth, width), jnp.float32),
        ] + [jax.ShapeDtypeStruct((depth, width), jnp.bfloat16)] * (total // 2),
        scratch_shapes=[
            pltpu.VMEM(mid.shape, mid.dtype),
            pltpu.VMEM(right.shape, right.dtype),
            pltpu.SemaphoreType.DMA((4,)),
            pltpu.SemaphoreType.DMA((groups,)),
        ],
        compiler_params=pltpu.CompilerParams(vmem_limit_bytes=52 * MIB),
        cost_estimate=pl.CostEstimate(
            flops=2 * depth * pairs * width * total * width, bytes_accessed=6 * MIB, transcendentals=0
        ),
        name="branch_sums",
    )(mid, right)


def close_kernel(*refs):
    *more, kept_ref, out_ref = refs
    stem_refs, got_refs = more[:-kept_ref.shape[0]], more[-kept_ref.shape[0]:]
    part = None
    at = 0
    for ref in stem_refs:
        for b in range(ref.shape[0]):
            block = ref[b]
            half = block.shape[-1] // 2
            rows = jnp.concatenate([block[:, :half], block[:, half:]], axis=0)
            sums = kept_ref[at] + got_refs[at][...].astype(jnp.float32)
            high = sums.astype(jnp.bfloat16)
            low = (sums - high.astype(jnp.float32)).astype(jnp.bfloat16)
            term = jnp.dot(rows, jnp.concatenate([high, low], axis=1), preferred_element_type=jnp.float32)
            part = term if part is None else part + term
            at += 1
    width = part.shape[1] // 2
    part = part[:, :width] + part[:, width:]
    half = part.shape[0] // 2
    total = part[:half] + turn(part[half:])
    if len(out_ref.shape) == 2:
        out_ref[...] = total
    else:
        cuts, copies, rows, _ = out_ref.shape
        for c in range(cuts):
            for s in range(copies):
                out_ref[c, s] = total[c * rows:(c + 1) * rows].astype(out_ref.dtype)


def close(stems, kept, got, cuts, copies):
    rows, width = stems[0].shape[1], kept.shape[2]
    whole_tiles = rows % (8 * cuts) == 0
    shape = (cuts, copies, rows // cuts, width) if whole_tiles else (rows, width)
    out = pl.pallas_call(
        close_kernel,
        out_shape=jax.ShapeDtypeStruct(shape, jnp.bfloat16 if whole_tiles else jnp.float32),
        compiler_params=pltpu.CompilerParams(vmem_limit_bytes=24 * MIB),
        cost_estimate=pl.CostEstimate(flops=8 * rows * kept.size, bytes_accessed=MIB, transcendentals=0),
        name="close",
    )(*stems, *got, kept)
    if whole_tiles:
        return out.reshape(cuts * copies, rows // cuts, width)
    out = out.reshape(cuts, 1, -1)
    return jnp.broadcast_to(out, (cuts, copies, out.shape[-1])).reshape(cuts * copies, -1)


def on_device(stem_tensor, mid_tensors, right_tensors):
    stems = lax.axis_size("stem")
    cuts = lax.axis_size("cuts")

    def swap(x, p):
        return lax.ppermute(x, "stem", [(s, s ^ p) for s in range(stems)])

    pieces = [stem_tensor] + [swap(stem_tensor, p) for p in range(2, stems, 2)]
    kept, *sent = branch_sums(mid_tensors, right_tensors, stems)
    got = [swap(x, 1) for x in sent]
    spread = close(pieces, kept, got, cuts, stems)
    parts = lax.all_to_all(spread, ("cuts", "stem"), 0, 0, tiled=True)
    return jnp.sum(parts.astype(jnp.float32), axis=0).reshape(-1)


def solution(mesh):
    return jax.shard_map(
        on_device,
        mesh=mesh,
        in_specs=(
            P("stem", None, None),
            P(("cuts", "stem"), None, None),
            P(None, ("cuts", "stem"), None, None),
        ),
        out_specs=P("cuts"),
        check_vma=False,
    )
```

```python
import jax
import jax.numpy as jnp
from jax import lax
from jax.experimental import pallas as pl
from jax.experimental.pallas import tpu as pltpu
from jax.sharding import PartitionSpec as P

MIB = 1024 * 1024


def turn(x):
    half = x.shape[-1] // 2
    lane = lax.broadcasted_iota(jnp.int32, x.shape, x.ndim - 1)
    rolled = pltpu.roll(x, half, x.ndim - 1)
    return jnp.where(lane < half, -rolled, rolled)


def branch_kernel(mid_hbm, right_hbm, kept_ref, *refs):
    *sent_refs, mid_ref, right_ref, mid_sem, right_sem = refs
    pairs, depth, width = mid_ref.shape
    groups = right_sem.shape[0]
    half = groups // 2
    blocks = right_ref.shape[0] // groups
    me = lax.axis_index("stem")
    chunk = pairs // mid_sem.shape[0]

    def mid_copy(n):
        at = pl.ds(n * chunk, chunk)
        return pltpu.make_async_copy(mid_hbm.at[at], mid_ref.at[at], mid_sem.at[n])

    def right_copy(q):
        p = jnp.where(q < half, 2 * q + 1, 2 * q - groups)
        source = right_hbm.at[pl.ds((me ^ p) * blocks, blocks)]
        return pltpu.make_async_copy(source, right_ref.at[pl.ds(q * blocks, blocks)], right_sem.at[q])

    for n in range(mid_sem.shape[0]):
        mid_copy(n).start()
    for q in range(groups):
        right_copy(q).start()
    for n in range(mid_sem.shape[0]):
        mid_copy(n).wait()

    def group(q, carry):
        right_copy(q).wait()
        left = jnp.concatenate([mid_ref[j] for j in range(pairs)], axis=1)
        columns = []
        for b in range(blocks):
            rows = []
            for j in range(pairs):
                w = right_ref[q * blocks + b, j]
                rows += [w, turn(w.astype(jnp.float32)).astype(w.dtype)]
            columns.append(jnp.concatenate(rows, axis=0))
        sums = jnp.dot(left, jnp.concatenate(columns, axis=1), preferred_element_type=jnp.float32)

        for at in range(half):
            @pl.when(q == at)
            def _():
                for b in range(blocks):
                    part = sums[:, b * width:(b + 1) * width]
                    sent_refs[at * blocks + b][...] = part.astype(jnp.bfloat16)

        @pl.when(q >= half)
        def _():
            for b in range(blocks):
                kept_ref[(q - half) * blocks + b] = sums[:, b * width:(b + 1) * width]

        return carry

    lax.fori_loop(0, groups, group, 0)


def branch_sums(mid, right, groups):
    pairs, depth, width = mid.shape
    total = right.shape[0]
    vmem = pl.BlockSpec(memory_space=pltpu.VMEM)
    hbm = pl.BlockSpec(memory_space=pltpu.HBM)
    return pl.pallas_call(
        branch_kernel,
        in_specs=[hbm, hbm],
        out_specs=[vmem] * (1 + total // 2),
        out_shape=[
            jax.ShapeDtypeStruct((total // 2, depth, width), jnp.float32),
        ] + [jax.ShapeDtypeStruct((depth, width), jnp.bfloat16)] * (total // 2),
        scratch_shapes=[
            pltpu.VMEM(mid.shape, mid.dtype),
            pltpu.VMEM(right.shape, right.dtype),
            pltpu.SemaphoreType.DMA((4,)),
            pltpu.SemaphoreType.DMA((groups,)),
        ],
        compiler_params=pltpu.CompilerParams(vmem_limit_bytes=52 * MIB),
        cost_estimate=pl.CostEstimate(
            flops=2 * depth * pairs * width * total * width, bytes_accessed=6 * MIB, transcendentals=0
        ),
        name="branch_sums",
    )(mid, right)


def close_kernel(*refs):
    *more, kept_ref, out_ref = refs
    stem_refs, got_refs = more[:-kept_ref.shape[0]], more[-kept_ref.shape[0]:]
    part = None
    at = 0
    for ref in stem_refs:
        for b in range(ref.shape[0]):
            block = ref[b]
            half = block.shape[-1] // 2
            rows = jnp.concatenate([block[:, :half], block[:, half:]], axis=0)
            sums = kept_ref[at] + got_refs[at][...].astype(jnp.float32)
            high = sums.astype(jnp.bfloat16)
            low = (sums - high.astype(jnp.float32)).astype(jnp.bfloat16)
            term = jnp.dot(rows, jnp.concatenate([high, low], axis=1), preferred_element_type=jnp.float32)
            part = term if part is None else part + term
            at += 1
    width = part.shape[1] // 2
    part = part[:, :width] + part[:, width:]
    half = part.shape[0] // 2
    out_ref[...] = part[:half] + turn(part[half:])


def close(stems, kept, got):
    rows, width = stems[0].shape[1], kept.shape[2]
    return pl.pallas_call(
        close_kernel,
        out_shape=jax.ShapeDtypeStruct((rows, width), jnp.float32),
        compiler_params=pltpu.CompilerParams(vmem_limit_bytes=24 * MIB),
        cost_estimate=pl.CostEstimate(flops=8 * rows * kept.size, bytes_accessed=MIB, transcendentals=0),
        name="close",
    )(*stems, *got, kept)


def deal(terms, sections, place):
    rows, width = terms[0].shape
    size = rows // sections

    def kernel(*refs):
        for m, out_ref in enumerate(refs[len(terms):]):
            at = pl.ds(pl.multiple_of((place() ^ m) * size, size), size)
            total = refs[0][at]
            for ref in refs[1:len(terms)]:
                total += ref[at]
            out_ref[...] = total

    return pl.pallas_call(
        kernel,
        out_shape=[jax.ShapeDtypeStruct((size, width), jnp.float32)] * sections,
        compiler_params=pltpu.CompilerParams(vmem_limit_bytes=24 * MIB),
        cost_estimate=pl.CostEstimate(flops=4 * rows * width, bytes_accessed=8 * rows * width, transcendentals=0),
        name="deal",
    )(*terms)


def on_device(stem_tensor, mid_tensors, right_tensors):
    stems = lax.axis_size("stem")
    cuts = lax.axis_size("cuts")

    def swap(x, p):
        return lax.ppermute(x, "stem", [(s, s ^ p) for s in range(stems)])

    pieces = [stem_tensor] + [swap(stem_tensor, p) for p in range(2, stems, 2)]
    kept, *sent = branch_sums(mid_tensors, right_tensors, stems)
    got = [swap(x, 1) for x in sent]
    partial_sum = close(pieces, kept, got)
    if partial_sum.shape[0] % (8 * cuts) or cuts % 2:
        parts = partial_sum.reshape(cuts, 1, -1)
        parts = jnp.broadcast_to(parts, (cuts, stems, parts.shape[-1])).reshape(cuts * stems, -1)
        return jnp.sum(lax.all_to_all(parts, ("cuts", "stem"), 0, 0, tiled=True), axis=0)

    def send(x, c, s):
        pairs = [(i * stems + j, (i ^ c) * stems + (j ^ s)) for i in range(cuts) for j in range(stems)]
        return lax.ppermute(x, ("cuts", "stem"), pairs)

    high, low = cuts // 2, 2
    chip = [partial_sum, send(partial_sum, 0, 1)]
    own, *away = deal(chip, high, lambda: lax.axis_index("cuts") // low)
    line = [own] + [send(x, low * m, 0) for m, x in enumerate(away, 1)]
    own, away = deal(line, low, lambda: lax.axis_index("cuts") % low)
    total = own
    for s in range(0, stems, 2):
        total = total + send(away, 1, s)
        if s:
            total = total + send(own, 0, s)
    return total.reshape(-1)


def solution(mesh):
    return jax.shard_map(
        on_device,
        mesh=mesh,
        in_specs=(
            P("stem", None, None),
            P(("cuts", "stem"), None, None),
            P(None, ("cuts", "stem"), None, None),
        ),
        out_specs=P("cuts"),
        check_vma=False,
    )
```

```python
import jax
import jax.numpy as jnp
from jax import lax
from jax.experimental import pallas as pl
from jax.experimental.pallas import tpu as pltpu
from jax.sharding import PartitionSpec as P

MIB = 1024 * 1024


def turn(x):
    half = x.shape[-1] // 2
    lane = lax.broadcasted_iota(jnp.int32, x.shape, x.ndim - 1)
    rolled = pltpu.roll(x, half, x.ndim - 1)
    return jnp.where(lane < half, -rolled, rolled)


def branch_kernel(mid_hbm, right_hbm, kept_ref, *refs):
    *sent_refs, mid_ref, right_ref, mid_sem, right_sem = refs
    pairs, depth, width = mid_ref.shape
    groups = right_sem.shape[0]
    half = groups // 2
    blocks = right_ref.shape[0] // groups
    me = lax.axis_index("stem")
    chunk = pairs // mid_sem.shape[0]

    def mid_copy(n):
        at = pl.ds(n * chunk, chunk)
        return pltpu.make_async_copy(mid_hbm.at[at], mid_ref.at[at], mid_sem.at[n])

    def right_copy(q):
        p = jnp.where(q < half, 2 * q + 1, 2 * q - groups)
        source = right_hbm.at[pl.ds((me ^ p) * blocks, blocks)]
        return pltpu.make_async_copy(source, right_ref.at[pl.ds(q * blocks, blocks)], right_sem.at[q])

    for n in range(mid_sem.shape[0]):
        mid_copy(n).start()
    for q in range(groups):
        right_copy(q).start()
    for n in range(mid_sem.shape[0]):
        mid_copy(n).wait()

    def group(q, carry):
        right_copy(q).wait()
        left = jnp.concatenate([mid_ref[j] for j in range(pairs)], axis=1)
        columns = []
        for b in range(blocks):
            rows = []
            for j in range(pairs):
                w = right_ref[q * blocks + b, j]
                rows += [w, turn(w.astype(jnp.float32)).astype(w.dtype)]
            columns.append(jnp.concatenate(rows, axis=0))
        sums = jnp.dot(left, jnp.concatenate(columns, axis=1), preferred_element_type=jnp.float32)

        for at in range(half):
            @pl.when(q == at)
            def _():
                for b in range(blocks):
                    part = sums[:, b * width:(b + 1) * width]
                    sent_refs[at * blocks + b][...] = part.astype(jnp.bfloat16)

        @pl.when(q >= half)
        def _():
            for b in range(blocks):
                kept_ref[(q - half) * blocks + b] = sums[:, b * width:(b + 1) * width]

        return carry

    lax.fori_loop(0, groups, group, 0)


def branch_sums(mid, right, groups):
    pairs, depth, width = mid.shape
    total = right.shape[0]
    vmem = pl.BlockSpec(memory_space=pltpu.VMEM)
    hbm = pl.BlockSpec(memory_space=pltpu.HBM)
    return pl.pallas_call(
        branch_kernel,
        in_specs=[hbm, hbm],
        out_specs=[vmem] * (1 + total // 2),
        out_shape=[
            jax.ShapeDtypeStruct((total // 2, depth, width), jnp.float32),
        ] + [jax.ShapeDtypeStruct((depth, width), jnp.bfloat16)] * (total // 2),
        scratch_shapes=[
            pltpu.VMEM(mid.shape, mid.dtype),
            pltpu.VMEM(right.shape, right.dtype),
            pltpu.SemaphoreType.DMA((4,)),
            pltpu.SemaphoreType.DMA((groups,)),
        ],
        compiler_params=pltpu.CompilerParams(vmem_limit_bytes=52 * MIB),
        cost_estimate=pl.CostEstimate(
            flops=2 * depth * pairs * width * total * width, bytes_accessed=6 * MIB, transcendentals=0
        ),
        name="branch_sums",
    )(mid, right)


def close_kernel(*refs):
    *more, kept_ref, out_ref = refs
    stem_refs, got_refs = more[:-kept_ref.shape[0]], more[-kept_ref.shape[0]:]
    part = None
    at = 0
    for ref in stem_refs:
        for b in range(ref.shape[0]):
            block = ref[b]
            half = block.shape[-1] // 2
            rows = jnp.concatenate([block[:, :half], block[:, half:]], axis=0)
            sums = kept_ref[at] + got_refs[at][...].astype(jnp.float32)
            high = sums.astype(jnp.bfloat16)
            low = (sums - high.astype(jnp.float32)).astype(jnp.bfloat16)
            term = jnp.dot(rows, jnp.concatenate([high, low], axis=1), preferred_element_type=jnp.float32)
            part = term if part is None else part + term
            at += 1
    width = part.shape[1] // 2
    part = part[:, :width] + part[:, width:]
    half = part.shape[0] // 2
    out_ref[...] = part[:half] + turn(part[half:])


def close(stems, kept, got):
    rows, width = stems[0].shape[1], kept.shape[2]
    return pl.pallas_call(
        close_kernel,
        out_shape=jax.ShapeDtypeStruct((rows, width), jnp.float32),
        compiler_params=pltpu.CompilerParams(vmem_limit_bytes=24 * MIB),
        cost_estimate=pl.CostEstimate(flops=8 * rows * kept.size, bytes_accessed=MIB, transcendentals=0),
        name="close",
    )(*stems, *got, kept)


def deal(terms, sections, place):
    rows, width = terms[0].shape
    size = rows // sections

    def kernel(*refs):
        for m, out_ref in enumerate(refs[len(terms):]):
            at = pl.ds(pl.multiple_of((place() ^ m) * size, size), size)
            total = refs[0][at]
            for ref in refs[1:len(terms)]:
                total += ref[at]
            out_ref[...] = total

    return pl.pallas_call(
        kernel,
        out_shape=[jax.ShapeDtypeStruct((size, width), jnp.float32)] * sections,
        compiler_params=pltpu.CompilerParams(vmem_limit_bytes=24 * MIB),
        cost_estimate=pl.CostEstimate(flops=4 * rows * width, bytes_accessed=8 * rows * width, transcendentals=0),
        name="deal",
    )(*terms)


def on_device(stem_tensor, mid_tensors, right_tensors):
    stems = lax.axis_size("stem")
    cuts = lax.axis_size("cuts")

    def swap(x, p):
        return lax.ppermute(x, "stem", [(s, s ^ p) for s in range(stems)])

    pieces = [stem_tensor] + [swap(stem_tensor, p) for p in range(2, stems, 2)]
    kept, *sent = branch_sums(mid_tensors, right_tensors, stems)
    got = [swap(x, 1) for x in sent]
    partial_sum = close(pieces, kept, got)
    if partial_sum.shape[0] % (8 * cuts) or cuts % 2:
        parts = partial_sum.reshape(cuts, 1, -1)
        parts = jnp.broadcast_to(parts, (cuts, stems, parts.shape[-1])).reshape(cuts * stems, -1)
        return jnp.sum(lax.all_to_all(parts, ("cuts", "stem"), 0, 0, tiled=True), axis=0)

    def send(x, c, s, cores=(1,)):
        pairs = [
            (i * stems + j, (i ^ c) * stems + (j ^ s)) for i in range(cuts) for j in range(stems) if j % 2 in cores
        ]
        return lax.ppermute(x, ("cuts", "stem"), pairs)

    high, low = cuts // 2, 2
    chip = [partial_sum, send(partial_sum, 0, 1, (0,))]
    own, *away = deal(chip, high, lambda: lax.axis_index("cuts") // low)
    line = [own] + [send(x, low * m, 0) for m, x in reversed(list(enumerate(away, 1)))]
    own, away = deal(line, low, lambda: lax.axis_index("cuts") % low)
    total = own
    for s in range(0, stems, 2):
        total = total + send(away, 1, s)
        if s:
            total = total + send(own, 0, s)
    shared = send(total, 0, 1)
    return jnp.where(lax.axis_index("stem") % 2 == 1, total, shared).reshape(-1)


def solution(mesh):
    return jax.shard_map(
        on_device,
        mesh=mesh,
        in_specs=(
            P("stem", None, None),
            P(("cuts", "stem"), None, None),
            P(None, ("cuts", "stem"), None, None),
        ),
        out_specs=P("cuts"),
        check_vma=False,
    )
```

```python
import jax
import jax.numpy as jnp
from jax import lax
from jax.experimental import pallas as pl
from jax.experimental.pallas import tpu as pltpu
from jax.sharding import PartitionSpec as P

MIB = 1024 * 1024


def turn(x):
    half = x.shape[-1] // 2
    lane = lax.broadcasted_iota(jnp.int32, x.shape, x.ndim - 1)
    rolled = pltpu.roll(x, half, x.ndim - 1)
    return jnp.where(lane < half, -rolled, rolled)


def branch_kernel(mid_hbm, right_hbm, kept_ref, *refs):
    *sent_refs, mid_ref, right_ref, mid_sem, right_sem = refs
    pairs, depth, width = mid_ref.shape
    groups = right_sem.shape[0]
    half = groups // 2
    blocks = right_ref.shape[0] // groups
    me = lax.axis_index("stem")
    chunk = pairs // mid_sem.shape[0]

    def mid_copy(n):
        at = pl.ds(n * chunk, chunk)
        return pltpu.make_async_copy(mid_hbm.at[at], mid_ref.at[at], mid_sem.at[n])

    def right_copy(q):
        p = jnp.where(q < half, 2 * q + 1, 2 * q - groups)
        source = right_hbm.at[pl.ds((me ^ p) * blocks, blocks)]
        return pltpu.make_async_copy(source, right_ref.at[pl.ds(q * blocks, blocks)], right_sem.at[q])

    for n in range(mid_sem.shape[0]):
        mid_copy(n).start()
    for q in range(groups):
        right_copy(q).start()
    for n in range(mid_sem.shape[0]):
        mid_copy(n).wait()

    def group(q, carry):
        right_copy(q).wait()
        left = jnp.concatenate([mid_ref[j] for j in range(pairs)], axis=1)
        columns = []
        for b in range(blocks):
            rows = []
            for j in range(pairs):
                w = right_ref[q * blocks + b, j]
                rows += [w, turn(w.astype(jnp.float32)).astype(w.dtype)]
            columns.append(jnp.concatenate(rows, axis=0))
        sums = jnp.dot(left, jnp.concatenate(columns, axis=1), preferred_element_type=jnp.float32)

        for at in range(half):
            @pl.when(q == at)
            def _():
                for b in range(blocks):
                    part = sums[:, b * width:(b + 1) * width]
                    sent_refs[at * blocks + b][...] = part.astype(jnp.bfloat16)

        @pl.when(q >= half)
        def _():
            for b in range(blocks):
                kept_ref[(q - half) * blocks + b] = sums[:, b * width:(b + 1) * width]

        return carry

    lax.fori_loop(0, groups, group, 0)


def branch_sums(mid, right, groups):
    pairs, depth, width = mid.shape
    total = right.shape[0]
    vmem = pl.BlockSpec(memory_space=pltpu.VMEM)
    hbm = pl.BlockSpec(memory_space=pltpu.HBM)
    return pl.pallas_call(
        branch_kernel,
        in_specs=[hbm, hbm],
        out_specs=[vmem] * (1 + total // 2),
        out_shape=[
            jax.ShapeDtypeStruct((total // 2, depth, width), jnp.float32),
        ] + [jax.ShapeDtypeStruct((depth, width), jnp.bfloat16)] * (total // 2),
        scratch_shapes=[
            pltpu.VMEM(mid.shape, mid.dtype),
            pltpu.VMEM(right.shape, right.dtype),
            pltpu.SemaphoreType.DMA((4,)),
            pltpu.SemaphoreType.DMA((groups,)),
        ],
        compiler_params=pltpu.CompilerParams(vmem_limit_bytes=52 * MIB),
        cost_estimate=pl.CostEstimate(
            flops=2 * depth * pairs * width * total * width, bytes_accessed=6 * MIB, transcendentals=0
        ),
        name="branch_sums",
    )(mid, right)


def close_kernel(*refs):
    *more, kept_ref, out_ref = refs
    stem_refs, got_refs = more[:-kept_ref.shape[0]], more[-kept_ref.shape[0]:]
    part = None
    at = 0
    for ref in stem_refs:
        for b in range(ref.shape[0]):
            block = ref[b]
            half = block.shape[-1] // 2
            rows = jnp.concatenate([block[:, :half], block[:, half:]], axis=0)
            sums = kept_ref[at] + got_refs[at][...].astype(jnp.float32)
            high = sums.astype(jnp.bfloat16)
            low = (sums - high.astype(jnp.float32)).astype(jnp.bfloat16)
            term = jnp.dot(rows, jnp.concatenate([high, low], axis=1), preferred_element_type=jnp.float32)
            part = term if part is None else part + term
            at += 1
    width = part.shape[1] // 2
    part = part[:, :width] + part[:, width:]
    half = part.shape[0] // 2
    out_ref[...] = part[:half] + turn(part[half:])


def close(stems, kept, got):
    rows, width = stems[0].shape[1], kept.shape[2]
    return pl.pallas_call(
        close_kernel,
        out_shape=jax.ShapeDtypeStruct((rows, width), jnp.float32),
        compiler_params=pltpu.CompilerParams(vmem_limit_bytes=24 * MIB),
        cost_estimate=pl.CostEstimate(flops=8 * rows * kept.size, bytes_accessed=MIB, transcendentals=0),
        name="close",
    )(*stems, *got, kept)


def deal(terms, sections, place):
    rows, width = terms[0].shape
    size = rows // sections

    def kernel(*refs):
        for m, out_ref in enumerate(refs[len(terms):]):
            at = pl.ds(pl.multiple_of((place() ^ m) * size, size), size)
            total = refs[0][at]
            for ref in refs[1:len(terms)]:
                total += ref[at]
            out_ref[...] = total

    return pl.pallas_call(
        kernel,
        out_shape=[jax.ShapeDtypeStruct((size, width), jnp.float32)] * sections,
        compiler_params=pltpu.CompilerParams(vmem_limit_bytes=24 * MIB),
        cost_estimate=pl.CostEstimate(flops=4 * rows * width, bytes_accessed=8 * rows * width, transcendentals=0),
        name="deal",
    )(*terms)


def on_device(stem_tensor, mid_tensors, right_tensors):
    stems = lax.axis_size("stem")
    cuts = lax.axis_size("cuts")

    def swap(x, p):
        return lax.ppermute(x, "stem", [(s, s ^ p) for s in range(stems)])

    pieces = [stem_tensor] + [swap(stem_tensor, p) for p in range(2, stems, 2)]
    kept, *sent = branch_sums(mid_tensors, right_tensors, stems)
    got = [swap(x, 1) for x in sent]
    partial_sum = close(pieces, kept, got)
    if partial_sum.shape[0] % (8 * cuts) or cuts % 2:
        parts = partial_sum.reshape(cuts, 1, -1)
        parts = jnp.broadcast_to(parts, (cuts, stems, parts.shape[-1])).reshape(cuts * stems, -1)
        return jnp.sum(lax.all_to_all(parts, ("cuts", "stem"), 0, 0, tiled=True), axis=0)

    def send(x, c, s):
        pairs = [
            (i * stems + j, (i ^ c) * stems + (j ^ s) if s % 2 or j % 2 else i * stems + j)
            for i in range(cuts) for j in range(stems)
        ]
        return lax.ppermute(x, ("cuts", "stem"), pairs)

    high, low = cuts // 2, 2
    chip = [partial_sum, send(partial_sum, 0, 1)]
    own, *away = deal(chip, high, lambda: lax.axis_index("cuts") // low)
    line = [own] + [send(x, low * m, 0) for m, x in reversed(list(enumerate(away, 1)))]
    own, away = deal(line, low, lambda: lax.axis_index("cuts") % low)
    total = own
    for s in range(0, stems, 2):
        total = total + send(away, 1, s)
        if s:
            total = total + send(own, 0, s)
    shared = send(total, 0, 1)
    return jnp.where(lax.axis_index("stem") % 2 == 1, total, shared).reshape(-1)


def solution(mesh):
    return jax.shard_map(
        on_device,
        mesh=mesh,
        in_specs=(
            P("stem", None, None),
            P(("cuts", "stem"), None, None),
            P(None, ("cuts", "stem"), None, None),
        ),
        out_specs=P("cuts"),
        check_vma=False,
    )
```

```python
import jax
import jax.numpy as jnp
from jax import lax
from jax.experimental import pallas as pl
from jax.experimental.pallas import tpu as pltpu
from jax.sharding import PartitionSpec as P

MIB = 1024 * 1024


def turn(x):
    half = x.shape[-1] // 2
    lane = lax.broadcasted_iota(jnp.int32, x.shape, x.ndim - 1)
    rolled = pltpu.roll(x, half, x.ndim - 1)
    return jnp.where(lane < half, -rolled, rolled)


def branch_kernel(mid_hbm, right_hbm, kept_ref, *refs):
    *sent_refs, mid_ref, right_ref, mid_sem, right_sem = refs
    pairs, depth, width = mid_ref.shape
    groups = right_sem.shape[0]
    half = groups // 2
    blocks = right_ref.shape[0] // groups
    me = lax.axis_index("stem")
    chunk = pairs // mid_sem.shape[0]

    def mid_copy(n):
        at = pl.ds(n * chunk, chunk)
        return pltpu.make_async_copy(mid_hbm.at[at], mid_ref.at[at], mid_sem.at[n])

    def right_copy(q):
        p = jnp.where(q < half, 2 * q + 1, 2 * q - groups)
        source = right_hbm.at[pl.ds((me ^ p) * blocks, blocks)]
        return pltpu.make_async_copy(source, right_ref.at[pl.ds(q * blocks, blocks)], right_sem.at[q])

    for n in range(mid_sem.shape[0]):
        mid_copy(n).start()
    for q in range(groups):
        right_copy(q).start()
    for n in range(mid_sem.shape[0]):
        mid_copy(n).wait()

    def group(q, carry):
        right_copy(q).wait()
        left = jnp.concatenate([mid_ref[j] for j in range(pairs)], axis=1)
        columns = []
        for b in range(blocks):
            rows = []
            for j in range(pairs):
                w = right_ref[q * blocks + b, j]
                rows += [w, turn(w.astype(jnp.float32)).astype(w.dtype)]
            columns.append(jnp.concatenate(rows, axis=0))
        sums = jnp.dot(left, jnp.concatenate(columns, axis=1), preferred_element_type=jnp.float32)

        for at in range(half):
            @pl.when(q == at)
            def _():
                for b in range(blocks):
                    part = sums[:, b * width:(b + 1) * width]
                    sent_refs[at * blocks + b][...] = part.astype(jnp.bfloat16)

        @pl.when(q >= half)
        def _():
            for b in range(blocks):
                kept_ref[(q - half) * blocks + b] = sums[:, b * width:(b + 1) * width]

        return carry

    lax.fori_loop(0, groups, group, 0)


def branch_sums(mid, right, groups):
    pairs, depth, width = mid.shape
    total = right.shape[0]
    vmem = pl.BlockSpec(memory_space=pltpu.VMEM)
    hbm = pl.BlockSpec(memory_space=pltpu.HBM)
    return pl.pallas_call(
        branch_kernel,
        in_specs=[hbm, hbm],
        out_specs=[vmem] * (1 + total // 2),
        out_shape=[
            jax.ShapeDtypeStruct((total // 2, depth, width), jnp.float32),
        ] + [jax.ShapeDtypeStruct((depth, width), jnp.bfloat16)] * (total // 2),
        scratch_shapes=[
            pltpu.VMEM(mid.shape, mid.dtype),
            pltpu.VMEM(right.shape, right.dtype),
            pltpu.SemaphoreType.DMA((4,)),
            pltpu.SemaphoreType.DMA((groups,)),
        ],
        compiler_params=pltpu.CompilerParams(vmem_limit_bytes=52 * MIB),
        cost_estimate=pl.CostEstimate(
            flops=2 * depth * pairs * width * total * width, bytes_accessed=6 * MIB, transcendentals=0
        ),
        name="branch_sums",
    )(mid, right)


def close_kernel(*refs):
    *more, kept_ref, out_ref = refs
    stem_refs, got_refs = more[:-kept_ref.shape[0]], more[-kept_ref.shape[0]:]
    part = None
    at = 0
    for ref in stem_refs:
        for b in range(ref.shape[0]):
            block = ref[b]
            half = block.shape[-1] // 2
            rows = jnp.concatenate([block[:, :half], block[:, half:]], axis=0)
            sums = kept_ref[at] + got_refs[at][...].astype(jnp.float32)
            high = sums.astype(jnp.bfloat16)
            low = (sums - high.astype(jnp.float32)).astype(jnp.bfloat16)
            term = jnp.dot(rows, jnp.concatenate([high, low], axis=1), preferred_element_type=jnp.float32)
            part = term if part is None else part + term
            at += 1
    width = part.shape[1] // 2
    part = part[:, :width] + part[:, width:]
    half = part.shape[0] // 2
    out_ref[...] = part[:half] + turn(part[half:])


def close(stems, kept, got):
    rows, width = stems[0].shape[1], kept.shape[2]
    return pl.pallas_call(
        close_kernel,
        out_shape=jax.ShapeDtypeStruct((rows, width), jnp.float32),
        compiler_params=pltpu.CompilerParams(vmem_limit_bytes=24 * MIB),
        cost_estimate=pl.CostEstimate(flops=8 * rows * kept.size, bytes_accessed=MIB, transcendentals=0),
        name="close",
    )(*stems, *got, kept)


def on_device(stem_tensor, mid_tensors, right_tensors):
    stems = lax.axis_size("stem")
    cuts = lax.axis_size("cuts")

    def swap(x, p):
        return lax.ppermute(x, "stem", [(s, s ^ p) for s in range(stems)])

    pieces = [stem_tensor] + [swap(stem_tensor, p) for p in range(2, stems, 2)]
    kept, *sent = branch_sums(mid_tensors, right_tensors, stems)
    got = [swap(x, 1) for x in sent]
    partial_sum = close(pieces, kept, got).reshape(cuts, -1)
    own = lax.psum_scatter(partial_sum, "cuts", scatter_dimension=0)
    return lax.psum(own, "stem")


def solution(mesh):
    return jax.shard_map(
        on_device,
        mesh=mesh,
        in_specs=(
            P("stem", None, None),
            P(("cuts", "stem"), None, None),
            P(None, ("cuts", "stem"), None, None),
        ),
        out_specs=P("cuts"),
        check_vma=False,
    )
```

```python
import jax
import jax.numpy as jnp
from jax import lax
from jax.experimental import pallas as pl
from jax.experimental.pallas import tpu as pltpu
from jax.sharding import PartitionSpec as P

MIB = 1024 * 1024


def turn(x):
    half = x.shape[-1] // 2
    lane = lax.broadcasted_iota(jnp.int32, x.shape, x.ndim - 1)
    rolled = pltpu.roll(x, half, x.ndim - 1)
    return jnp.where(lane < half, -rolled, rolled)


def branch_kernel(mid_hbm, right_hbm, kept_ref, *refs):
    *sent_refs, mid_ref, right_ref, mid_sem, right_sem = refs
    pairs, depth, width = mid_ref.shape
    groups = right_sem.shape[0]
    half = groups // 2
    blocks = right_ref.shape[0] // groups
    me = lax.axis_index("stem")
    chunk = pairs // mid_sem.shape[0]

    def mid_copy(n):
        at = pl.ds(n * chunk, chunk)
        return pltpu.make_async_copy(mid_hbm.at[at], mid_ref.at[at], mid_sem.at[n])

    def right_copy(q):
        k = jnp.where(q < half, q, q - half)
        p = jnp.where(k == 0, 0, 2 * k + 1) ^ jnp.where(q < half, 1, 0)
        source = right_hbm.at[pl.ds((me ^ p) * blocks, blocks)]
        return pltpu.make_async_copy(source, right_ref.at[pl.ds(q * blocks, blocks)], right_sem.at[q])

    for n in range(mid_sem.shape[0]):
        mid_copy(n).start()
    for q in range(groups):
        right_copy(q).start()
    for n in range(mid_sem.shape[0]):
        mid_copy(n).wait()

    def group(q, carry):
        right_copy(q).wait()
        left = jnp.concatenate([mid_ref[j] for j in range(pairs)], axis=1)
        columns = []
        for b in range(blocks):
            rows = []
            for j in range(pairs):
                w = right_ref[q * blocks + b, j]
                rows += [w, turn(w.astype(jnp.float32)).astype(w.dtype)]
            columns.append(jnp.concatenate(rows, axis=0))
        sums = jnp.dot(left, jnp.concatenate(columns, axis=1), preferred_element_type=jnp.float32)

        for at in range(half):
            @pl.when(q == at)
            def _():
                for b in range(blocks):
                    part = sums[:, b * width:(b + 1) * width]
                    sent_refs[at * blocks + b][...] = part.astype(jnp.bfloat16)

        @pl.when(q >= half)
        def _():
            for b in range(blocks):
                kept_ref[(q - half) * blocks + b] = sums[:, b * width:(b + 1) * width]

        return carry

    lax.fori_loop(0, groups, group, 0)


def branch_sums(mid, right, groups):
    pairs, depth, width = mid.shape
    total = right.shape[0]
    vmem = pl.BlockSpec(memory_space=pltpu.VMEM)
    hbm = pl.BlockSpec(memory_space=pltpu.HBM)
    return pl.pallas_call(
        branch_kernel,
        in_specs=[hbm, hbm],
        out_specs=[vmem] * (1 + total // 2),
        out_shape=[
            jax.ShapeDtypeStruct((total // 2, depth, width), jnp.float32),
        ] + [jax.ShapeDtypeStruct((depth, width), jnp.bfloat16)] * (total // 2),
        scratch_shapes=[
            pltpu.VMEM(mid.shape, mid.dtype),
            pltpu.VMEM(right.shape, right.dtype),
            pltpu.SemaphoreType.DMA((4,)),
            pltpu.SemaphoreType.DMA((groups,)),
        ],
        compiler_params=pltpu.CompilerParams(vmem_limit_bytes=52 * MIB),
        cost_estimate=pl.CostEstimate(
            flops=2 * depth * pairs * width * total * width, bytes_accessed=6 * MIB, transcendentals=0
        ),
        name="branch_sums",
    )(mid, right)


def close_kernel(*refs):
    *more, kept_ref, out_ref = refs
    stem_refs, got_refs = more[:-kept_ref.shape[0]], more[-kept_ref.shape[0]:]
    part = None
    at = 0
    for ref in stem_refs:
        for b in range(ref.shape[0]):
            block = ref[b]
            half = block.shape[-1] // 2
            rows = jnp.concatenate([block[:, :half], block[:, half:]], axis=0)
            sums = kept_ref[at] + got_refs[at][...].astype(jnp.float32)
            high = sums.astype(jnp.bfloat16)
            low = (sums - high.astype(jnp.float32)).astype(jnp.bfloat16)
            term = jnp.dot(rows, jnp.concatenate([high, low], axis=1), preferred_element_type=jnp.float32)
            part = term if part is None else part + term
            at += 1
    width = part.shape[1] // 2
    part = part[:, :width] + part[:, width:]
    half = part.shape[0] // 2
    out_ref[...] = part[:half] + turn(part[half:])


def close(stems, kept, got):
    rows, width = stems[0].shape[1], kept.shape[2]
    return pl.pallas_call(
        close_kernel,
        out_shape=jax.ShapeDtypeStruct((rows, width), jnp.float32),
        compiler_params=pltpu.CompilerParams(vmem_limit_bytes=24 * MIB),
        cost_estimate=pl.CostEstimate(flops=8 * rows * kept.size, bytes_accessed=MIB, transcendentals=0),
        name="close",
    )(*stems, *got, kept)


def deal(terms, sections, place):
    rows, width = terms[0].shape
    size = rows // sections

    def kernel(*refs):
        for m, out_ref in enumerate(refs[len(terms):]):
            at = pl.ds(pl.multiple_of((place() ^ m) * size, size), size)
            total = refs[0][at]
            for ref in refs[1:len(terms)]:
                total += ref[at]
            out_ref[...] = total

    return pl.pallas_call(
        kernel,
        out_shape=[jax.ShapeDtypeStruct((size, width), jnp.float32)] * sections,
        compiler_params=pltpu.CompilerParams(vmem_limit_bytes=24 * MIB),
        cost_estimate=pl.CostEstimate(flops=4 * rows * width, bytes_accessed=8 * rows * width, transcendentals=0),
        name="deal",
    )(*terms)


def on_device(stem_tensor, mid_tensors, right_tensors):
    stems = lax.axis_size("stem")
    cuts = lax.axis_size("cuts")

    def swap(x, p):
        return lax.ppermute(x, "stem", [(s, s ^ p) for s in range(stems)])

    pieces = [stem_tensor] + [swap(stem_tensor, p) for p in range(3, stems, 2)]
    kept, *sent = branch_sums(mid_tensors, right_tensors, stems)
    got = [swap(x, 1) for x in sent]
    partial_sum = close(pieces, kept, got)
    if partial_sum.shape[0] % (8 * cuts) or cuts % 2:
        parts = partial_sum.reshape(cuts, 1, -1)
        parts = jnp.broadcast_to(parts, (cuts, stems, parts.shape[-1])).reshape(cuts * stems, -1)
        return jnp.sum(lax.all_to_all(parts, ("cuts", "stem"), 0, 0, tiled=True), axis=0)

    def send(x, c, s):
        pairs = [(i * stems + j, (i ^ c) * stems + (j ^ s)) for i in range(cuts) for j in range(stems)]
        return lax.ppermute(x, ("cuts", "stem"), pairs)

    high, low = cuts // 2, 2
    chip = [partial_sum, send(partial_sum, 0, 1)]
    own, *away = deal(chip, high, lambda: lax.axis_index("cuts") // low)
    line = [own] + [send(x, low * m, 1) for m, x in reversed(list(enumerate(away, 1)))]
    own, away = deal(line, low, lambda: lax.axis_index("cuts") % low)
    total = own
    for s in range(0, stems, 2):
        total = total + send(away, 1, s ^ 1)
        if s:
            total = total + send(own, 0, s ^ 1)
    return total.reshape(-1)


def solution(mesh):
    return jax.shard_map(
        on_device,
        mesh=mesh,
        in_specs=(
            P("stem", None, None),
            P(("cuts", "stem"), None, None),
            P(None, ("cuts", "stem"), None, None),
        ),
        out_specs=P("cuts"),
        check_vma=False,
    )
```

```python
import functools

import jax
import jax.numpy as jnp
from jax import lax
from jax.experimental import pallas as pl
from jax.experimental.pallas import tpu as pltpu
from jax.sharding import PartitionSpec as P

MIB = 1024 * 1024


def turn(x):
    half = x.shape[-1] // 2
    lane = lax.broadcasted_iota(jnp.int32, x.shape, x.ndim - 1)
    rolled = pltpu.roll(x, half, x.ndim - 1)
    return jnp.where(lane < half, -rolled, rolled)


def branch_kernel(blocks, mid_hbm, right_hbm, kept_ref, *refs):
    *sent_refs, mid_ref, wide_ref, mid_sem, right_sem = refs
    pairs, _, width = mid_ref.shape
    total, _, inner, _ = right_hbm.shape
    groups = total // blocks
    leaving = len(sent_refs) // blocks
    me = lax.axis_index("stem")
    chunk = pairs // mid_sem.shape[0]

    def mid_copy(n):
        at = pl.ds(n * chunk, chunk)
        return pltpu.make_async_copy(mid_hbm.at[at], mid_ref.at[at], mid_sem.at[n])

    def right_copy(q):
        stays = q - leaving
        p = jnp.where(stays < 0, 2 * q + 3, jnp.where(stays < 2, stays, 2 * stays - 2))
        source = right_hbm.at[pl.ds((me ^ p) * blocks, blocks)]
        target = wide_ref.at[pl.ds(q * blocks, blocks), :, pl.ds(0, inner)]
        return pltpu.make_async_copy(source, target, right_sem.at[q])

    for q in range(groups):
        right_copy(q).start()
    for n in range(mid_sem.shape[0]):
        mid_copy(n).start()

    def widen(q, carry):
        right_copy(q).wait()
        for b in range(blocks):
            for j in range(pairs):
                upper = wide_ref[q * blocks + b, j, :inner]
                wide_ref[q * blocks + b, j, inner:] = turn(upper.astype(jnp.float32)).astype(upper.dtype)
        return carry

    lax.fori_loop(0, groups, widen, 0)
    for n in range(mid_sem.shape[0]):
        mid_copy(n).wait()

    def group(q, carry):
        left = jnp.concatenate([mid_ref[j] for j in range(pairs)], axis=1)
        right = [wide_ref[q * blocks + b].reshape(pairs * 2 * inner, width) for b in range(blocks)]
        sums = jnp.dot(left, jnp.concatenate(right, axis=1), preferred_element_type=jnp.float32)
        for at in range(leaving):
            @pl.when(q == at)
            def _():
                for b in range(blocks):
                    part = sums[:, b * width:(b + 1) * width]
                    sent_refs[at * blocks + b][...] = part.astype(jnp.bfloat16)

        @pl.when(q >= leaving)
        def _():
            for b in range(blocks):
                kept_ref[(q - leaving) * blocks + b] = sums[:, b * width:(b + 1) * width]

        return carry

    lax.fori_loop(0, groups, group, 0)


def branch_sums(mid, right, groups):
    pairs, depth, width = mid.shape
    total, _, inner, _ = right.shape
    blocks = total // groups
    leaving = (groups // 2 - 1) * blocks
    vmem = pl.BlockSpec(memory_space=pltpu.VMEM)
    hbm = pl.BlockSpec(memory_space=pltpu.HBM)
    return pl.pallas_call(
        functools.partial(branch_kernel, blocks),
        in_specs=[hbm, hbm],
        out_specs=[vmem] * (1 + leaving),
        out_shape=[
            jax.ShapeDtypeStruct((total - leaving, depth, width), jnp.float32),
        ] + [jax.ShapeDtypeStruct((depth, width), jnp.bfloat16)] * leaving,
        scratch_shapes=[
            pltpu.VMEM(mid.shape, mid.dtype),
            pltpu.VMEM((total, pairs, 2 * inner, width), right.dtype),
            pltpu.SemaphoreType.DMA((4,)),
            pltpu.SemaphoreType.DMA((groups,)),
        ],
        compiler_params=pltpu.CompilerParams(vmem_limit_bytes=52 * MIB),
        cost_estimate=pl.CostEstimate(
            flops=2 * depth * pairs * width * total * width, bytes_accessed=6 * MIB, transcendentals=0
        ),
        name="branch_sums",
    )(mid, right)


def close_kernel(count, *refs):
    *more, kept_ref, out_ref = refs
    stem_refs, got_refs = more[:count], more[count:]
    alone = kept_ref.shape[0] - len(got_refs)
    part = None
    at = 0
    for ref in stem_refs:
        for b in range(ref.shape[0]):
            block = ref[b]
            half = block.shape[-1] // 2
            rows = jnp.concatenate([block[:, :half], block[:, half:]], axis=0)
            sums = kept_ref[at]
            if at >= alone:
                sums += got_refs[at - alone][...].astype(jnp.float32)
            high = sums.astype(jnp.bfloat16)
            low = (sums - high.astype(jnp.float32)).astype(jnp.bfloat16)
            term = jnp.dot(rows, jnp.concatenate([high, low], axis=1), preferred_element_type=jnp.float32)
            part = term if part is None else part + term
            at += 1
    width = part.shape[1] // 2
    part = part[:, :width] + part[:, width:]
    half = part.shape[0] // 2
    total = part[:half] + turn(part[half:])
    if len(out_ref.shape) == 2:
        out_ref[...] = total
    else:
        cuts, copies, rows, _ = out_ref.shape
        for c in range(cuts):
            for s in range(copies):
                out_ref[c, s] = total[c * rows:(c + 1) * rows]


def close(stems, kept, got, cuts, copies):
    rows, width = stems[0].shape[1], kept.shape[2]
    whole_tiles = rows % (8 * cuts) == 0
    shape = (cuts, copies, rows // cuts, width) if whole_tiles else (rows, width)
    out = pl.pallas_call(
        functools.partial(close_kernel, len(stems)),
        out_shape=jax.ShapeDtypeStruct(shape, jnp.float32),
        compiler_params=pltpu.CompilerParams(vmem_limit_bytes=24 * MIB),
        cost_estimate=pl.CostEstimate(flops=8 * rows * kept.size, bytes_accessed=MIB, transcendentals=0),
        name="close",
    )(*stems, *got, kept)
    if whole_tiles:
        return out.reshape(cuts * copies, rows // cuts, width)
    out = out.reshape(cuts, 1, -1)
    return jnp.broadcast_to(out, (cuts, copies, out.shape[-1])).reshape(cuts * copies, -1)


def on_device(stem_tensor, mid_tensors, right_tensors):
    stems = lax.axis_size("stem")
    cuts = lax.axis_size("cuts")

    def swap(x, p):
        return lax.ppermute(x, "stem", [(s, s ^ p) for s in range(stems)])

    far = [swap(stem_tensor, p) for p in range(2, stems, 2)]
    pieces = [stem_tensor, swap(stem_tensor, 1)] + far
    kept, *sent = branch_sums(mid_tensors, right_tensors, stems)
    got = [swap(x, 1) for x in sent]
    spread = close(pieces, kept, got, cuts, stems)
    parts = lax.all_to_all(spread, ("cuts", "stem"), 0, 0, tiled=True)
    return jnp.sum(parts, axis=0).reshape(-1)


def solution(mesh):
    return jax.shard_map(
        on_device,
        mesh=mesh,
        in_specs=(
            P("stem", None, None),
            P(("cuts", "stem"), None, None),
            P(None, ("cuts", "stem"), None, None),
        ),
        out_specs=P("cuts"),
        check_vma=False,
    )
```

```python
import functools

import jax
import jax.numpy as jnp
from jax import lax
from jax.experimental import pallas as pl
from jax.experimental.pallas import tpu as pltpu
from jax.sharding import PartitionSpec as P

MIB = 1024 * 1024


def turn(x):
    half = x.shape[-1] // 2
    lane = lax.broadcasted_iota(jnp.int32, x.shape, x.ndim - 1)
    rolled = pltpu.roll(x, half, x.ndim - 1)
    return jnp.where(lane < half, -rolled, rolled)


def branch_kernel(blocks, mid_hbm, right_hbm, kept_ref, *refs):
    *sent_refs, sums_ref, mid_ref, right_ref, wide_ref, mid_sem, right_sem = refs
    width = mid_ref.shape[2]
    inner = right_ref.shape[3]
    groups = right_ref.shape[1] // blocks
    half = groups // 2
    chunks = mid_sem.shape[0]
    chunk = mid_ref.shape[0] // chunks
    steps = chunks * groups
    me = lax.axis_index("stem")

    def mid_copy(n):
        at = pl.ds(n * chunk, chunk)
        return pltpu.make_async_copy(mid_hbm.at[at], mid_ref.at[at], mid_sem.at[n])

    def right_copy(n):
        return pltpu.make_async_copy(right_hbm.at[:, pl.ds(n * chunk, chunk)], right_ref.at[n], right_sem.at[n])

    def widen(step):
        n, q = step // groups, step % groups
        p = jnp.where(q < half, 2 * q + 1, 2 * q - groups)
        slot = step % 2
        for b in range(blocks):
            cols = slice(b * width, (b + 1) * width)
            for j in range(chunk):
                w = right_ref[n, (me ^ p) * blocks + b, j]
                at = j * 2 * inner
                wide_ref[slot, at:at + inner, cols] = w
                wide_ref[slot, at + inner:at + 2 * inner, cols] = turn(w.astype(jnp.float32)).astype(w.dtype)

    for n in range(chunks):
        right_copy(n).start()
        mid_copy(n).start()
    sums_ref[...] = jnp.zeros_like(sums_ref)
    right_copy(0).wait()
    mid_copy(0).wait()
    widen(0)

    def multiply(step):
        n, q = step // groups, step % groups
        left = jnp.concatenate([mid_ref[n * chunk + j] for j in range(chunk)], axis=1)
        return q, jnp.dot(left, wide_ref[step % 2], preferred_element_type=jnp.float32)

    def advance(step, carry):
        @pl.when((step % groups == groups - 1) & (step < steps - 1))
        def _():
            right_copy(step // groups + 1).wait()
            mid_copy(step // groups + 1).wait()

        q, product = multiply(step)
        sums_ref[q] += product
        widen((step + 1) % steps)
        return carry

    lax.fori_loop(0, steps, advance, 0)
    for q in range(half):
        kept_ref[q] = sums_ref[q + half]
        for b in range(blocks):
            sent_refs[q * blocks + b][...] = sums_ref[q, :, b * width:(b + 1) * width].astype(jnp.bfloat16)


def branch_sums(mid, right, groups):
    pairs, depth, width = mid.shape
    total, _, inner, _ = right.shape
    blocks = total // groups
    chunks = 4
    vmem = pl.BlockSpec(memory_space=pltpu.VMEM)
    hbm = pl.BlockSpec(memory_space=pltpu.HBM)
    return pl.pallas_call(
        functools.partial(branch_kernel, blocks),
        in_specs=[hbm, hbm],
        out_specs=[vmem] * (1 + total // 2),
        out_shape=[
            jax.ShapeDtypeStruct((groups // 2, depth, blocks * width), jnp.float32),
        ] + [jax.ShapeDtypeStruct((depth, width), jnp.bfloat16)] * (total // 2),
        scratch_shapes=[
            pltpu.VMEM((groups, depth, blocks * width), jnp.float32),
            pltpu.VMEM(mid.shape, mid.dtype),
            pltpu.VMEM((chunks, total, pairs // chunks, inner, width), right.dtype),
            pltpu.VMEM((2, pairs // chunks * 2 * inner, blocks * width), right.dtype),
            pltpu.SemaphoreType.DMA((chunks,)),
            pltpu.SemaphoreType.DMA((chunks,)),
        ],
        compiler_params=pltpu.CompilerParams(vmem_limit_bytes=52 * MIB),
        cost_estimate=pl.CostEstimate(
            flops=2 * depth * pairs * width * total * width, bytes_accessed=6 * MIB, transcendentals=0
        ),
        name="branch_sums",
    )(mid, right)


def close_kernel(*refs):
    *more, sums_ref, out_ref = refs
    stem_refs, got_refs = more[:sums_ref.shape[0]], more[sums_ref.shape[0]:]
    part = None
    at = 0
    for q, ref in enumerate(stem_refs):
        for b in range(ref.shape[0]):
            block = ref[b]
            half = block.shape[-1] // 2
            rows = jnp.concatenate([block[:, :half], block[:, half:]], axis=0)
            width = got_refs[at].shape[1]
            sums = sums_ref[q, :, b * width:(b + 1) * width] + got_refs[at][...].astype(jnp.float32)
            high = sums.astype(jnp.bfloat16)
            low = (sums - high.astype(jnp.float32)).astype(jnp.bfloat16)
            term = jnp.dot(rows, jnp.concatenate([high, low], axis=1), preferred_element_type=jnp.float32)
            part = term if part is None else part + term
            at += 1
    width = part.shape[1] // 2
    part = part[:, :width] + part[:, width:]
    half = part.shape[0] // 2
    total = part[:half] + turn(part[half:])
    if len(out_ref.shape) == 2:
        out_ref[...] = total
    else:
        cuts, copies, rows, _ = out_ref.shape
        for c in range(cuts):
            for s in range(copies):
                out_ref[c, s] = total[c * rows:(c + 1) * rows]


def close(stems, sums, got, cuts, copies):
    rows, width = stems[0].shape[1], got[0].shape[1]
    whole_tiles = rows % (8 * cuts) == 0
    shape = (cuts, copies, rows // cuts, width) if whole_tiles else (rows, width)
    out = pl.pallas_call(
        close_kernel,
        out_shape=jax.ShapeDtypeStruct(shape, jnp.float32),
        compiler_params=pltpu.CompilerParams(vmem_limit_bytes=24 * MIB),
        cost_estimate=pl.CostEstimate(flops=8 * rows * sums.size, bytes_accessed=MIB, transcendentals=0),
        name="close",
    )(*stems, *got, sums)
    if whole_tiles:
        return out.reshape(cuts * copies, rows // cuts, width)
    out = out.reshape(cuts, 1, -1)
    return jnp.broadcast_to(out, (cuts, copies, out.shape[-1])).reshape(cuts * copies, -1)


def on_device(stem_tensor, mid_tensors, right_tensors):
    stems = lax.axis_size("stem")
    cuts = lax.axis_size("cuts")

    def swap(x, p):
        return lax.ppermute(x, "stem", [(s, s ^ p) for s in range(stems)])

    pieces = [stem_tensor] + [swap(stem_tensor, p) for p in range(2, stems, 2)]
    sums, *sent = branch_sums(mid_tensors, right_tensors, stems)
    got = [swap(x, 1) for x in sent]
    spread = close(pieces, sums, got, cuts, stems)
    parts = lax.all_to_all(spread, ("cuts", "stem"), 0, 0, tiled=True)
    return jnp.sum(parts, axis=0).reshape(-1)


def solution(mesh):
    return jax.shard_map(
        on_device,
        mesh=mesh,
        in_specs=(
            P("stem", None, None),
            P(("cuts", "stem"), None, None),
            P(None, ("cuts", "stem"), None, None),
        ),
        out_specs=P("cuts"),
        check_vma=False,
    )
```

```python
import functools

import jax
import jax.numpy as jnp
from jax import lax
from jax.experimental import pallas as pl
from jax.experimental.pallas import tpu as pltpu
from jax.sharding import PartitionSpec as P

MIB = 1024 * 1024


def turn(x):
    half = x.shape[-1] // 2
    lane = lax.broadcasted_iota(jnp.int32, x.shape, x.ndim - 1)
    rolled = pltpu.roll(x, half, x.ndim - 1)
    return jnp.where(lane < half, -rolled, rolled)


def branch_kernel(blocks, mid_hbm, right_hbm, kept_ref, *refs):
    *sent_refs, sums_ref, mid_ref, wide_ref, mid_sem, right_sem = refs
    pairs, _, width = mid_ref.shape
    total, _, inner, _ = right_hbm.shape
    groups = total // blocks
    half = groups // 2
    me = lax.axis_index("stem")
    chunk = pairs // mid_sem.shape[0]

    def mid_copy(n):
        at = pl.ds(n * chunk, chunk)
        return pltpu.make_async_copy(mid_hbm.at[at], mid_ref.at[at], mid_sem.at[n])

    def right_copy(q):
        p = jnp.where(q < half, 2 * q + 1, 2 * q - groups)
        source = right_hbm.at[pl.ds((me ^ p) * blocks, blocks)]
        target = wide_ref.at[pl.ds(q * blocks, blocks), :, pl.ds(0, inner)]
        return pltpu.make_async_copy(source, target, right_sem.at[q])

    for q in range(groups):
        right_copy(q).start()
    for n in range(mid_sem.shape[0]):
        mid_copy(n).start()

    def widen(q, carry):
        right_copy(q).wait()
        for b in range(blocks):
            for j in range(pairs):
                upper = wide_ref[q * blocks + b, j, :inner]
                wide_ref[q * blocks + b, j, inner:] = turn(upper.astype(jnp.float32)).astype(upper.dtype)
        return carry

    lax.fori_loop(0, groups, widen, 0)
    for n in range(mid_sem.shape[0]):
        mid_copy(n).wait()

    def multiply(h, carry):
        left = jnp.concatenate([mid_ref[j] for j in range(pairs)], axis=1)
        right = [wide_ref[h * (total // 2) + b].reshape(pairs * 2 * inner, width) for b in range(total // 2)]
        sums_ref[h] = jnp.dot(left, jnp.concatenate(right, axis=1), preferred_element_type=jnp.float32)
        return carry

    lax.fori_loop(0, 2, multiply, 0)
    for b, ref in enumerate(sent_refs):
        cols = slice(b * width, (b + 1) * width)
        ref[...] = sums_ref[0, :, cols].astype(ref.dtype)
        kept_ref[b] = sums_ref[1, :, cols]


def branch_sums(mid, right, groups):
    pairs, depth, width = mid.shape
    total, _, inner, _ = right.shape
    vmem = pl.BlockSpec(memory_space=pltpu.VMEM)
    hbm = pl.BlockSpec(memory_space=pltpu.HBM)
    return pl.pallas_call(
        functools.partial(branch_kernel, total // groups),
        in_specs=[hbm, hbm],
        out_specs=[vmem] * (1 + total // 2),
        out_shape=[
            jax.ShapeDtypeStruct((total // 2, depth, width), jnp.float32),
        ] + [jax.ShapeDtypeStruct((depth, width), jnp.bfloat16)] * (total // 2),
        scratch_shapes=[
            pltpu.VMEM((2, depth, total // 2 * width), jnp.float32),
            pltpu.VMEM(mid.shape, mid.dtype),
            pltpu.VMEM((total, pairs, 2 * inner, width), right.dtype),
            pltpu.SemaphoreType.DMA((4,)),
            pltpu.SemaphoreType.DMA((groups,)),
        ],
        compiler_params=pltpu.CompilerParams(vmem_limit_bytes=52 * MIB),
        cost_estimate=pl.CostEstimate(
            flops=2 * depth * pairs * width * total * width, bytes_accessed=6 * MIB, transcendentals=0
        ),
        name="branch_sums",
    )(mid, right)


def close_kernel(*refs):
    *more, kept_ref, out_ref = refs
    stem_refs, got_refs = more[:-kept_ref.shape[0]], more[-kept_ref.shape[0]:]
    part = None
    at = 0
    for ref in stem_refs:
        for b in range(ref.shape[0]):
            block = ref[b]
            half = block.shape[-1] // 2
            rows = jnp.concatenate([block[:, :half], block[:, half:]], axis=0)
            sums = kept_ref[at] + got_refs[at][...].astype(jnp.float32)
            high = sums.astype(jnp.bfloat16)
            low = (sums - high.astype(jnp.float32)).astype(jnp.bfloat16)
            term = jnp.dot(rows, jnp.concatenate([high, low], axis=1), preferred_element_type=jnp.float32)
            part = term if part is None else part + term
            at += 1
    width = part.shape[1] // 2
    part = part[:, :width] + part[:, width:]
    half = part.shape[0] // 2
    total = part[:half] + turn(part[half:])
    if len(out_ref.shape) == 2:
        out_ref[...] = total
    else:
        cuts, copies, rows, _ = out_ref.shape
        for c in range(cuts):
            for s in range(copies):
                out_ref[c, s] = total[c * rows:(c + 1) * rows]


def close(stems, kept, got, cuts, copies):
    rows, width = stems[0].shape[1], kept.shape[2]
    whole_tiles = rows % (8 * cuts) == 0
    shape = (cuts, copies, rows // cuts, width) if whole_tiles else (rows, width)
    out = pl.pallas_call(
        close_kernel,
        out_shape=jax.ShapeDtypeStruct(shape, jnp.float32),
        compiler_params=pltpu.CompilerParams(vmem_limit_bytes=24 * MIB),
        cost_estimate=pl.CostEstimate(flops=8 * rows * kept.size, bytes_accessed=MIB, transcendentals=0),
        name="close",
    )(*stems, *got, kept)
    if whole_tiles:
        return out.reshape(cuts * copies, rows // cuts, width)
    out = out.reshape(cuts, 1, -1)
    return jnp.broadcast_to(out, (cuts, copies, out.shape[-1])).reshape(cuts * copies, -1)


def on_device(stem_tensor, mid_tensors, right_tensors):
    stems = lax.axis_size("stem")
    cuts = lax.axis_size("cuts")

    def swap(x, p):
        return lax.ppermute(x, "stem", [(s, s ^ p) for s in range(stems)])

    pieces = [stem_tensor] + [swap(stem_tensor, p) for p in range(2, stems, 2)]
    kept, *sent = branch_sums(mid_tensors, right_tensors, stems)
    got = [swap(x, 1) for x in sent]
    spread = close(pieces, kept, got, cuts, stems)
    parts = lax.all_to_all(spread, ("cuts", "stem"), 0, 0, tiled=True)
    return jnp.sum(parts, axis=0).reshape(-1)


def solution(mesh):
    return jax.shard_map(
        on_device,
        mesh=mesh,
        in_specs=(
            P("stem", None, None),
            P(("cuts", "stem"), None, None),
            P(None, ("cuts", "stem"), None, None),
        ),
        out_specs=P("cuts"),
        check_vma=False,
    )
```

```python
import functools

import jax
import jax.numpy as jnp
from jax import lax
from jax.experimental import pallas as pl
from jax.experimental.pallas import tpu as pltpu
from jax.sharding import PartitionSpec as P

MIB = 1024 * 1024


def turn(x):
    half = x.shape[-1] // 2
    lane = lax.broadcasted_iota(jnp.int32, x.shape, x.ndim - 1)
    rolled = pltpu.roll(x, half, x.ndim - 1)
    return jnp.where(lane < half, -rolled, rolled)


def branch_kernel(blocks, mid_hbm, right_hbm, kept_ref, *refs):
    *sent_refs, sums_ref, mid_ref, wide_ref, mid_sem, right_sem = refs
    pairs, _, width = mid_ref.shape
    total, _, inner, _ = right_hbm.shape
    groups = total // blocks
    half = groups // 2
    me = lax.axis_index("stem")
    chunk = pairs // mid_sem.shape[0]

    def mid_copy(n):
        at = pl.ds(n * chunk, chunk)
        return pltpu.make_async_copy(mid_hbm.at[at], mid_ref.at[at], mid_sem.at[n])

    def right_copy(q):
        p = jnp.where(q < half, 2 * q + 1, 2 * q - groups)
        source = right_hbm.at[pl.ds((me ^ p) * blocks, blocks)]
        target = wide_ref.at[pl.ds(q * blocks, blocks), :, pl.ds(0, inner)]
        return pltpu.make_async_copy(source, target, right_sem.at[q])

    for q in range(groups):
        right_copy(q).start()
    for n in range(mid_sem.shape[0]):
        mid_copy(n).start()

    def widen(q, carry):
        right_copy(q).wait()
        for b in range(blocks):
            for j in range(pairs):
                upper = wide_ref[q * blocks + b, j, :inner]
                wide_ref[q * blocks + b, j, inner:] = turn(upper.astype(jnp.float32)).astype(upper.dtype)
        return carry

    lax.fori_loop(0, groups, widen, 0)
    for n in range(mid_sem.shape[0]):
        mid_copy(n).wait()

    def multiply(h, carry):
        left = jnp.concatenate([mid_ref[j] for j in range(pairs)], axis=1)
        right = [wide_ref[h * (total // 2) + b].reshape(pairs * 2 * inner, width) for b in range(total // 2)]
        sums_ref[h] = jnp.dot(left, jnp.concatenate(right, axis=1), preferred_element_type=jnp.float32)
        return carry

    lax.fori_loop(0, 2, multiply, 0)
    for b, ref in enumerate(sent_refs):
        cols = slice(b * width, (b + 1) * width)
        ref[...] = sums_ref[0, :, cols].astype(ref.dtype)
        kept_ref[b] = sums_ref[1, :, cols]


def branch_sums(mid, right, groups):
    pairs, depth, width = mid.shape
    total, _, inner, _ = right.shape
    vmem = pl.BlockSpec(memory_space=pltpu.VMEM)
    hbm = pl.BlockSpec(memory_space=pltpu.HBM)
    return pl.pallas_call(
        functools.partial(branch_kernel, total // groups),
        in_specs=[hbm, hbm],
        out_specs=[vmem] * (1 + total // 2),
        out_shape=[
            jax.ShapeDtypeStruct((total // 2, depth, width), jnp.float32),
        ] + [jax.ShapeDtypeStruct((depth, width), jnp.bfloat16)] * (total // 2),
        scratch_shapes=[
            pltpu.VMEM((2, depth, total // 2 * width), jnp.float32),
            pltpu.VMEM(mid.shape, mid.dtype),
            pltpu.VMEM((total, pairs, 2 * inner, width), right.dtype),
            pltpu.SemaphoreType.DMA((4,)),
            pltpu.SemaphoreType.DMA((groups,)),
        ],
        compiler_params=pltpu.CompilerParams(vmem_limit_bytes=52 * MIB),
        cost_estimate=pl.CostEstimate(
            flops=2 * depth * pairs * width * total * width, bytes_accessed=6 * MIB, transcendentals=0
        ),
        name="branch_sums",
    )(mid, right)


def close_kernel(*refs):
    *more, kept_ref, out_ref = refs
    stem_refs, got_refs = more[:-kept_ref.shape[0]], more[-kept_ref.shape[0]:]
    part = None
    at = 0
    for ref in stem_refs:
        for b in range(ref.shape[0]):
            block = ref[b]
            half = block.shape[-1] // 2
            rows = jnp.concatenate([block[:, :half], block[:, half:]], axis=0)
            sums = kept_ref[at] + got_refs[at][...].astype(jnp.float32)
            high = sums.astype(jnp.bfloat16)
            low = (sums - high.astype(jnp.float32)).astype(jnp.bfloat16)
            term = jnp.dot(rows, jnp.concatenate([high, low], axis=1), preferred_element_type=jnp.float32)
            part = term if part is None else part + term
            at += 1
    width = part.shape[1] // 2
    part = part[:, :width] + part[:, width:]
    half = part.shape[0] // 2
    out_ref[...] = part[:half] + turn(part[half:])


def close(stems, kept, got):
    rows, width = stems[0].shape[1], kept.shape[2]
    return pl.pallas_call(
        close_kernel,
        out_shape=jax.ShapeDtypeStruct((rows, width), jnp.float32),
        compiler_params=pltpu.CompilerParams(vmem_limit_bytes=24 * MIB),
        cost_estimate=pl.CostEstimate(flops=8 * rows * kept.size, bytes_accessed=MIB, transcendentals=0),
        name="close",
    )(*stems, *got, kept)


def deal(one, other, sections, places):
    rows, width = one.shape
    size = rows // sections
    count = len(places)

    def kernel(one_ref, other_ref, *out_refs):
        for place, out_ref in zip(places, out_refs):
            at = pl.ds(pl.multiple_of(place() * size, size), size)
            out_ref[...] = one_ref[at] + other_ref[at]

    return pl.pallas_call(
        kernel,
        out_shape=[jax.ShapeDtypeStruct((size, width), jnp.float32)] * count,
        compiler_params=pltpu.CompilerParams(vmem_limit_bytes=24 * MIB),
        cost_estimate=pl.CostEstimate(flops=2 * rows * width, bytes_accessed=8 * rows * width, transcendentals=0),
        name="deal",
    )(one, other)


def half_line(own, near, far):
    def kernel(own_ref, near_ref, far_ref, out_ref):
        odd = lax.axis_index("stem") % 2 == 1
        out_ref[...] = jnp.where(odd, own_ref[...], near_ref[...]) + far_ref[...]

    return pl.pallas_call(
        kernel,
        out_shape=jax.ShapeDtypeStruct(own.shape, own.dtype),
        compiler_params=pltpu.CompilerParams(vmem_limit_bytes=24 * MIB),
        cost_estimate=pl.CostEstimate(flops=2 * own.size, bytes_accessed=16 * own.size, transcendentals=0),
        name="half_line",
    )(own, near, far)


def on_device(stem_tensor, mid_tensors, right_tensors):
    stems = lax.axis_size("stem")
    cuts = lax.axis_size("cuts")

    def swap(x, p):
        return lax.ppermute(x, "stem", [(s, s ^ p) for s in range(stems)])

    pieces = [stem_tensor] + [swap(stem_tensor, p) for p in range(2, stems, 2)]
    kept, *sent = branch_sums(mid_tensors, right_tensors, stems)
    got = [swap(x, 1) for x in sent]
    partial_sum = close(pieces, kept, got)
    rows = partial_sum.shape[0]
    if cuts != 8 or stems != 4 or rows % 64:
        parts = partial_sum.reshape(cuts, 1, -1)
        parts = jnp.broadcast_to(parts, (cuts, stems, parts.shape[-1])).reshape(cuts * stems, -1)
        return jnp.sum(lax.all_to_all(parts, ("cuts", "stem"), 0, 0, tiled=True), axis=0)

    def send(x, mask):
        pairs = []
        for i in range(cuts):
            for j in range(stems):
                c, s = mask(j % 2)
                pairs.append((i * stems + j, (i ^ c) * stems + (j ^ s)))
        return lax.ppermute(x, ("cuts", "stem"), pairs)

    def plane():
        return lax.axis_index("cuts") // 2

    def column():
        return lax.axis_index("cuts") % 2

    chip = send(partial_sum, lambda core: (0, 1))
    own, near, far = deal(
        partial_sum, chip, 4, (plane, lambda: plane() ^ 1, lambda: plane() ^ (2 + lax.axis_index("stem") % 2))
    )
    near = send(near, lambda core: (2, 1))
    far = send(far, lambda core: (2 * (2 + core), 0))
    line = half_line(own, near, far)
    own, away = deal(line, send(line, lambda core: (0, 1)), 2, (column, lambda: column() ^ 1))
    total = own + send(away, lambda core: (1, 1)) + send(away, lambda core: (1, 3)) + send(own, lambda core: (0, 3))
    return total.reshape(-1)


def solution(mesh):
    return jax.shard_map(
        on_device,
        mesh=mesh,
        in_specs=(
            P("stem", None, None),
            P(("cuts", "stem"), None, None),
            P(None, ("cuts", "stem"), None, None),
        ),
        out_specs=P("cuts"),
        check_vma=False,
    )
```

```python
import functools

import jax
import jax.numpy as jnp
from jax import lax
from jax.experimental import pallas as pl
from jax.experimental.pallas import tpu as pltpu
from jax.sharding import PartitionSpec as P

MIB = 1024 * 1024


def turn(x):
    half = x.shape[-1] // 2
    lane = lax.broadcasted_iota(jnp.int32, x.shape, x.ndim - 1)
    rolled = pltpu.roll(x, half, x.ndim - 1)
    return jnp.where(lane < half, -rolled, rolled)


def branch_kernel(blocks, mid_hbm, right_hbm, kept_ref, *refs):
    *sent_refs, sums_ref, mid_ref, wide_ref, mid_sem, right_sem = refs
    pairs, _, width = mid_ref.shape
    total, _, inner, _ = right_hbm.shape
    groups = total // blocks
    half = groups // 2
    me = lax.axis_index("stem")
    chunk = pairs // mid_sem.shape[0]

    def mid_copy(n):
        at = pl.ds(n * chunk, chunk)
        return pltpu.make_async_copy(mid_hbm.at[at], mid_ref.at[at], mid_sem.at[n])

    def right_copy(q):
        p = jnp.where(q < half, 2 * q + 1, 2 * q - groups)
        source = right_hbm.at[pl.ds((me ^ p) * blocks, blocks)]
        target = wide_ref.at[pl.ds(q * blocks, blocks), :, pl.ds(0, inner)]
        return pltpu.make_async_copy(source, target, right_sem.at[q])

    for q in range(groups):
        right_copy(q).start()
    for n in range(mid_sem.shape[0]):
        mid_copy(n).start()

    def widen(q, carry):
        right_copy(q).wait()
        for b in range(blocks):
            for j in range(pairs):
                upper = wide_ref[q * blocks + b, j, :inner]
                wide_ref[q * blocks + b, j, inner:] = turn(upper.astype(jnp.float32)).astype(upper.dtype)
        return carry

    lax.fori_loop(0, groups, widen, 0)
    for n in range(mid_sem.shape[0]):
        mid_copy(n).wait()

    def multiply(h, carry):
        left = jnp.concatenate([mid_ref[j] for j in range(pairs)], axis=1)
        right = [wide_ref[h * (total // 2) + b].reshape(pairs * 2 * inner, width) for b in range(total // 2)]
        sums_ref[h] = jnp.dot(left, jnp.concatenate(right, axis=1), preferred_element_type=jnp.float32)
        return carry

    lax.fori_loop(0, 2, multiply, 0)
    for b, ref in enumerate(sent_refs):
        cols = slice(b * width, (b + 1) * width)
        ref[...] = sums_ref[0, :, cols].astype(ref.dtype)
        kept_ref[b] = sums_ref[1, :, cols]


def branch_sums(mid, right, groups):
    pairs, depth, width = mid.shape
    total, _, inner, _ = right.shape
    vmem = pl.BlockSpec(memory_space=pltpu.VMEM)
    hbm = pl.BlockSpec(memory_space=pltpu.HBM)
    return pl.pallas_call(
        functools.partial(branch_kernel, total // groups),
        in_specs=[hbm, hbm],
        out_specs=[vmem] * (1 + total // 2),
        out_shape=[
            jax.ShapeDtypeStruct((total // 2, depth, width), jnp.float32),
        ] + [jax.ShapeDtypeStruct((depth, width), jnp.bfloat16)] * (total // 2),
        scratch_shapes=[
            pltpu.VMEM((2, depth, total // 2 * width), jnp.float32),
            pltpu.VMEM(mid.shape, mid.dtype),
            pltpu.VMEM((total, pairs, 2 * inner, width), right.dtype),
            pltpu.SemaphoreType.DMA((4,)),
            pltpu.SemaphoreType.DMA((groups,)),
        ],
        compiler_params=pltpu.CompilerParams(vmem_limit_bytes=52 * MIB),
        cost_estimate=pl.CostEstimate(
            flops=2 * depth * pairs * width * total * width, bytes_accessed=6 * MIB, transcendentals=0
        ),
        name="branch_sums",
    )(mid, right)


def close_kernel(*refs):
    *more, kept_ref, out_ref = refs
    stem_refs, got_refs = more[:-kept_ref.shape[0]], more[-kept_ref.shape[0]:]
    part = None
    at = 0
    for ref in stem_refs:
        for b in range(ref.shape[0]):
            block = ref[b]
            half = block.shape[-1] // 2
            rows = jnp.concatenate([block[:, :half], block[:, half:]], axis=0)
            sums = kept_ref[at] + got_refs[at][...].astype(jnp.float32)
            high = sums.astype(jnp.bfloat16)
            low = (sums - high.astype(jnp.float32)).astype(jnp.bfloat16)
            term = jnp.dot(rows, jnp.concatenate([high, low], axis=1), preferred_element_type=jnp.float32)
            part = term if part is None else part + term
            at += 1
    width = part.shape[1] // 2
    part = part[:, :width] + part[:, width:]
    half = part.shape[0] // 2
    total = part[:half] + turn(part[half:])
    if len(out_ref.shape) == 2:
        out_ref[...] = total
    else:
        copies, cuts, rows, _ = out_ref.shape
        for c in range(cuts):
            for s in range(copies):
                out_ref[s, c] = total[c * rows:(c + 1) * rows]


def close(stems, kept, got, cuts, copies):
    rows, width = stems[0].shape[1], kept.shape[2]
    whole_tiles = rows % (8 * cuts) == 0
    shape = (copies, cuts, rows // cuts, width) if whole_tiles else (rows, width)
    out = pl.pallas_call(
        close_kernel,
        out_shape=jax.ShapeDtypeStruct(shape, jnp.float32),
        compiler_params=pltpu.CompilerParams(vmem_limit_bytes=24 * MIB),
        cost_estimate=pl.CostEstimate(flops=8 * rows * kept.size, bytes_accessed=MIB, transcendentals=0),
        name="close",
    )(*stems, *got, kept)
    if whole_tiles:
        return out.reshape(cuts * copies, rows // cuts, width)
    out = out.reshape(1, cuts, -1)
    return jnp.broadcast_to(out, (copies, cuts, out.shape[-1])).reshape(cuts * copies, -1)


def on_device(stem_tensor, mid_tensors, right_tensors):
    stems = lax.axis_size("stem")
    cuts = lax.axis_size("cuts")

    def swap(x, p):
        return lax.ppermute(x, "stem", [(s, s ^ p) for s in range(stems)])

    pieces = [stem_tensor] + [swap(stem_tensor, p) for p in range(2, stems, 2)]
    kept, *sent = branch_sums(mid_tensors, right_tensors, stems)
    got = [swap(x, 1) for x in sent]
    spread = close(pieces, kept, got, cuts, stems)
    parts = lax.all_to_all(spread, ("stem", "cuts"), 0, 0, tiled=True)
    return jnp.sum(parts, axis=0).reshape(-1)


def solution(mesh):
    return jax.shard_map(
        on_device,
        mesh=mesh,
        in_specs=(
            P("stem", None, None),
            P(("cuts", "stem"), None, None),
            P(None, ("cuts", "stem"), None, None),
        ),
        out_specs=P("cuts"),
        check_vma=False,
    )
```

```python
import functools

import jax
import jax.numpy as jnp
import numpy as np
from jax import lax
from jax.experimental import pallas as pl
from jax.experimental.pallas import tpu as pltpu
from jax.sharding import Mesh, PartitionSpec as P

CUTS = ("plane", "column")
STEM = ("side", "core")
ORDER = ("side", "core", "column", "plane")
MIB = 1024 * 1024


def turn(x):
    half = x.shape[-1] // 2
    lane = lax.broadcasted_iota(jnp.int32, x.shape, x.ndim - 1)
    rolled = pltpu.roll(x, half, x.ndim - 1)
    return jnp.where(lane < half, -rolled, rolled)


def branch_kernel(blocks, mid_hbm, right_hbm, kept_ref, *refs):
    *sent_refs, sums_ref, mid_ref, wide_ref, mid_sem, right_sem = refs
    pairs, _, width = mid_ref.shape
    total, _, inner, _ = right_hbm.shape
    groups = total // blocks
    half = groups // 2
    me = lax.axis_index("side") * lax.axis_size("core") + lax.axis_index("core")
    chunk = pairs // mid_sem.shape[0]

    def mid_copy(n):
        at = pl.ds(n * chunk, chunk)
        return pltpu.make_async_copy(mid_hbm.at[at], mid_ref.at[at], mid_sem.at[n])

    def right_copy(q):
        p = jnp.where(q < half, 2 * q + 1, 2 * q - groups)
        source = right_hbm.at[pl.ds((me ^ p) * blocks, blocks)]
        target = wide_ref.at[pl.ds(q * blocks, blocks), :, pl.ds(0, inner)]
        return pltpu.make_async_copy(source, target, right_sem.at[q])

    for q in range(groups):
        right_copy(q).start()
    for n in range(mid_sem.shape[0]):
        mid_copy(n).start()

    def widen(q, carry):
        right_copy(q).wait()
        for b in range(blocks):
            for j in range(pairs):
                upper = wide_ref[q * blocks + b, j, :inner]
                wide_ref[q * blocks + b, j, inner:] = turn(upper.astype(jnp.float32)).astype(upper.dtype)
        return carry

    lax.fori_loop(0, groups, widen, 0)
    for n in range(mid_sem.shape[0]):
        mid_copy(n).wait()

    def multiply(h, carry):
        left = jnp.concatenate([mid_ref[j] for j in range(pairs)], axis=1)
        right = [wide_ref[h * (total // 2) + b].reshape(pairs * 2 * inner, width) for b in range(total // 2)]
        sums_ref[h] = jnp.dot(left, jnp.concatenate(right, axis=1), preferred_element_type=jnp.float32)
        return carry

    lax.fori_loop(0, 2, multiply, 0)
    for b, ref in enumerate(sent_refs):
        cols = slice(b * width, (b + 1) * width)
        ref[...] = sums_ref[0, :, cols].astype(ref.dtype)
        kept_ref[b] = sums_ref[1, :, cols]


def branch_sums(mid, right, groups):
    pairs, depth, width = mid.shape
    total, _, inner, _ = right.shape
    vmem = pl.BlockSpec(memory_space=pltpu.VMEM)
    hbm = pl.BlockSpec(memory_space=pltpu.HBM)
    return pl.pallas_call(
        functools.partial(branch_kernel, total // groups),
        in_specs=[hbm, hbm],
        out_specs=[vmem] * (1 + total // 2),
        out_shape=[
            jax.ShapeDtypeStruct((total // 2, depth, width), jnp.float32),
        ] + [jax.ShapeDtypeStruct((depth, width), jnp.bfloat16)] * (total // 2),
        scratch_shapes=[
            pltpu.VMEM((2, depth, total // 2 * width), jnp.float32),
            pltpu.VMEM(mid.shape, mid.dtype),
            pltpu.VMEM((total, pairs, 2 * inner, width), right.dtype),
            pltpu.SemaphoreType.DMA((4,)),
            pltpu.SemaphoreType.DMA((groups,)),
        ],
        compiler_params=pltpu.CompilerParams(vmem_limit_bytes=52 * MIB),
        cost_estimate=pl.CostEstimate(
            flops=2 * depth * pairs * width * total * width, bytes_accessed=6 * MIB, transcendentals=0
        ),
        name="branch_sums",
    )(mid, right)


def close_kernel(targets, *refs):
    *more, kept_ref, out_ref = refs
    stem_refs, got_refs = more[:-kept_ref.shape[0]], more[-kept_ref.shape[0]:]
    part = None
    at = 0
    for ref in stem_refs:
        for b in range(ref.shape[0]):
            block = ref[b]
            half = block.shape[-1] // 2
            rows = jnp.concatenate([block[:, :half], block[:, half:]], axis=0)
            sums = kept_ref[at] + got_refs[at][...].astype(jnp.float32)
            high = sums.astype(jnp.bfloat16)
            low = (sums - high.astype(jnp.float32)).astype(jnp.bfloat16)
            term = jnp.dot(rows, jnp.concatenate([high, low], axis=1), preferred_element_type=jnp.float32)
            part = term if part is None else part + term
            at += 1
    width = part.shape[1] // 2
    part = part[:, :width] + part[:, width:]
    half = part.shape[0] // 2
    total = part[:half] + turn(part[half:])
    if targets is None:
        out_ref[...] = total
    else:
        rows = out_ref.shape[1]
        for at, c in enumerate(targets):
            out_ref[at] = total[c * rows:(c + 1) * rows]


def close(stems, kept, got):
    rows, width = stems[0].shape[1], kept.shape[2]
    cuts = lax.axis_size(CUTS)
    sizes = [lax.axis_size(name) for name in ORDER]
    places = np.arange(cuts).reshape([lax.axis_size(name) for name in CUTS])
    targets = [int(places[at[ORDER.index("plane")], at[ORDER.index("column")]]) for at in np.ndindex(*sizes)]
    whole_tiles = rows % (8 * cuts) == 0
    shape = (len(targets), rows // cuts, width) if whole_tiles else (rows, width)
    out = pl.pallas_call(
        functools.partial(close_kernel, targets if whole_tiles else None),
        out_shape=jax.ShapeDtypeStruct(shape, jnp.float32),
        compiler_params=pltpu.CompilerParams(vmem_limit_bytes=24 * MIB),
        cost_estimate=pl.CostEstimate(flops=8 * rows * kept.size, bytes_accessed=MIB, transcendentals=0),
        name="close",
    )(*stems, *got, kept)
    return out if whole_tiles else out.reshape(cuts, -1)[np.array(targets)]


def on_device(stem_tensor, mid_tensors, right_tensors):
    stems = lax.axis_size(STEM)

    def swap(x, p):
        return lax.ppermute(x, STEM, [(s, s ^ p) for s in range(stems)])

    pieces = [stem_tensor] + [swap(stem_tensor, p) for p in range(2, stems, 2)]
    kept, *sent = branch_sums(mid_tensors, right_tensors, stems)
    got = [swap(x, 1) for x in sent]
    spread = close(pieces, kept, got)
    parts = lax.all_to_all(spread, ORDER, 0, 0, tiled=True)
    return jnp.sum(parts, axis=0).reshape(-1)


def solution(mesh):
    cuts, stems = mesh.devices.shape
    fine = Mesh(mesh.devices.reshape(cuts // 2, 2, stems // 2, 2), CUTS + STEM)
    return jax.shard_map(
        on_device,
        mesh=fine,
        in_specs=(P(STEM, None, None), P(CUTS + STEM, None, None), P(None, CUTS + STEM, None, None)),
        out_specs=P(CUTS),
        check_vma=False,
    )
```

```python
import functools

import jax
import jax.numpy as jnp
import numpy as np
from jax import lax
from jax.experimental import pallas as pl
from jax.experimental.pallas import tpu as pltpu
from jax.sharding import Mesh, PartitionSpec as P

CUTS = ("plane", "column")
STEM = ("side", "core")
PLANE = ("side", "core", "column")
MIB = 1024 * 1024


def turn(x):
    half = x.shape[-1] // 2
    lane = lax.broadcasted_iota(jnp.int32, x.shape, x.ndim - 1)
    rolled = pltpu.roll(x, half, x.ndim - 1)
    return jnp.where(lane < half, -rolled, rolled)


def branch_kernel(blocks, mid_hbm, right_hbm, kept_ref, *refs):
    *sent_refs, sums_ref, mid_ref, wide_ref, mid_sem, right_sem = refs
    pairs, _, width = mid_ref.shape
    total, _, inner, _ = right_hbm.shape
    groups = total // blocks
    half = groups // 2
    me = lax.axis_index("side") * lax.axis_size("core") + lax.axis_index("core")
    chunk = pairs // mid_sem.shape[0]

    def mid_copy(n):
        at = pl.ds(n * chunk, chunk)
        return pltpu.make_async_copy(mid_hbm.at[at], mid_ref.at[at], mid_sem.at[n])

    def right_copy(q):
        p = jnp.where(q < half, 2 * q + 1, 2 * q - groups)
        source = right_hbm.at[pl.ds((me ^ p) * blocks, blocks)]
        target = wide_ref.at[pl.ds(q * blocks, blocks), :, pl.ds(0, inner)]
        return pltpu.make_async_copy(source, target, right_sem.at[q])

    for q in range(groups):
        right_copy(q).start()
    for n in range(mid_sem.shape[0]):
        mid_copy(n).start()

    def widen(q, carry):
        right_copy(q).wait()
        for b in range(blocks):
            for j in range(pairs):
                upper = wide_ref[q * blocks + b, j, :inner]
                wide_ref[q * blocks + b, j, inner:] = turn(upper.astype(jnp.float32)).astype(upper.dtype)
        return carry

    lax.fori_loop(0, groups, widen, 0)
    for n in range(mid_sem.shape[0]):
        mid_copy(n).wait()

    def multiply(h, carry):
        left = jnp.concatenate([mid_ref[j] for j in range(pairs)], axis=1)
        right = [wide_ref[h * (total // 2) + b].reshape(pairs * 2 * inner, width) for b in range(total // 2)]
        sums_ref[h] = jnp.dot(left, jnp.concatenate(right, axis=1), preferred_element_type=jnp.float32)
        return carry

    lax.fori_loop(0, 2, multiply, 0)
    for b, ref in enumerate(sent_refs):
        cols = slice(b * width, (b + 1) * width)
        ref[...] = sums_ref[0, :, cols].astype(ref.dtype)
        kept_ref[b] = sums_ref[1, :, cols]


def branch_sums(mid, right, groups):
    pairs, depth, width = mid.shape
    total, _, inner, _ = right.shape
    vmem = pl.BlockSpec(memory_space=pltpu.VMEM)
    hbm = pl.BlockSpec(memory_space=pltpu.HBM)
    return pl.pallas_call(
        functools.partial(branch_kernel, total // groups),
        in_specs=[hbm, hbm],
        out_specs=[vmem] * (1 + total // 2),
        out_shape=[
            jax.ShapeDtypeStruct((total // 2, depth, width), jnp.float32),
        ] + [jax.ShapeDtypeStruct((depth, width), jnp.bfloat16)] * (total // 2),
        scratch_shapes=[
            pltpu.VMEM((2, depth, total // 2 * width), jnp.float32),
            pltpu.VMEM(mid.shape, mid.dtype),
            pltpu.VMEM((total, pairs, 2 * inner, width), right.dtype),
            pltpu.SemaphoreType.DMA((4,)),
            pltpu.SemaphoreType.DMA((groups,)),
        ],
        compiler_params=pltpu.CompilerParams(vmem_limit_bytes=52 * MIB),
        cost_estimate=pl.CostEstimate(
            flops=2 * depth * pairs * width * total * width, bytes_accessed=6 * MIB, transcendentals=0
        ),
        name="branch_sums",
    )(mid, right)


def close_kernel(*refs):
    *more, kept_ref, out_ref = refs
    stem_refs, got_refs = more[:-kept_ref.shape[0]], more[-kept_ref.shape[0]:]
    part = None
    at = 0
    for ref in stem_refs:
        for b in range(ref.shape[0]):
            block = ref[b]
            half = block.shape[-1] // 2
            rows = jnp.concatenate([block[:, :half], block[:, half:]], axis=0)
            sums = kept_ref[at] + got_refs[at][...].astype(jnp.float32)
            high = sums.astype(jnp.bfloat16)
            low = (sums - high.astype(jnp.float32)).astype(jnp.bfloat16)
            term = jnp.dot(rows, jnp.concatenate([high, low], axis=1), preferred_element_type=jnp.float32)
            part = term if part is None else part + term
            at += 1
    width = part.shape[1] // 2
    part = part[:, :width] + part[:, width:]
    half = part.shape[0] // 2
    out_ref[...] = part[:half] + turn(part[half:])


def close(stems, kept, got):
    rows, width = stems[0].shape[1], kept.shape[2]
    return pl.pallas_call(
        close_kernel,
        out_shape=jax.ShapeDtypeStruct((rows, width), jnp.float32),
        compiler_params=pltpu.CompilerParams(vmem_limit_bytes=24 * MIB),
        cost_estimate=pl.CostEstimate(flops=8 * rows * kept.size, bytes_accessed=MIB, transcendentals=0),
        name="close",
    )(*stems, *got, kept)


def deal(one, other, sections, places):
    rows, width = one.shape
    size = rows // sections
    count = len(places)

    def kernel(one_ref, other_ref, *out_refs):
        for place, out_ref in zip(places, out_refs):
            at = pl.ds(pl.multiple_of(place() * size, size), size)
            out_ref[...] = one_ref[at] + other_ref[at]

    return pl.pallas_call(
        kernel,
        out_shape=[jax.ShapeDtypeStruct((size, width), jnp.float32)] * count,
        compiler_params=pltpu.CompilerParams(vmem_limit_bytes=24 * MIB),
        cost_estimate=pl.CostEstimate(flops=2 * rows * width, bytes_accessed=8 * rows * width, transcendentals=0),
        name="deal",
    )(one, other)


def half_line(own, near, far, columns):
    size = own.shape[0] // (max(columns) + 1)

    def kernel(own_ref, near_ref, far_ref, out_ref):
        odd = lax.axis_index("core") == 1
        total = jnp.where(odd, own_ref[...], near_ref[...]) + far_ref[...]
        for at, column in enumerate(columns):
            out_ref[at] = total[column * size:(column + 1) * size]

    return pl.pallas_call(
        kernel,
        out_shape=jax.ShapeDtypeStruct((len(columns), size, own.shape[1]), own.dtype),
        compiler_params=pltpu.CompilerParams(vmem_limit_bytes=24 * MIB),
        cost_estimate=pl.CostEstimate(flops=2 * own.size, bytes_accessed=32 * own.size, transcendentals=0),
        name="half_line",
    )(own, near, far)


def on_device(stem_tensor, mid_tensors, right_tensors):
    stems = lax.axis_size(STEM)

    def swap(x, p):
        return lax.ppermute(x, STEM, [(s, s ^ p) for s in range(stems)])

    pieces = [stem_tensor] + [swap(stem_tensor, p) for p in range(2, stems, 2)]
    kept, *sent = branch_sums(mid_tensors, right_tensors, stems)
    got = [swap(x, 1) for x in sent]
    partial_sum = close(pieces, kept, got)
    cuts = lax.axis_size(CUTS)
    if cuts != 8 or stems != 4 or partial_sum.shape[0] % 64:
        parts = partial_sum.reshape(1, cuts, -1)
        parts = jnp.broadcast_to(parts, (stems, cuts, parts.shape[-1])).reshape(cuts * stems, -1)
        return jnp.sum(lax.all_to_all(parts, STEM + CUTS, 0, 0, tiled=True), axis=0)

    def send(x, flips):
        pairs = []
        for i in range(cuts * stems):
            plane, core = flips(i % 2)
            pairs.append((i, i ^ (plane * 8 + core)))
        return lax.ppermute(x, CUTS + STEM, pairs)

    def plane():
        return lax.axis_index("plane")

    chip = send(partial_sum, lambda core: (0, 1))
    own, near, far = deal(
        partial_sum, chip, 4, (plane, lambda: plane() ^ 1, lambda: plane() ^ (2 + lax.axis_index("core")))
    )
    near = send(near, lambda core: (1, 1))
    far = send(far, lambda core: (2 + core, 0))
    parts = half_line(own, near, far, [at[2] for at in np.ndindex(2, 2, 2)])
    return jnp.sum(lax.all_to_all(parts, PLANE, 0, 0, tiled=True), axis=0).reshape(-1)


def solution(mesh):
    cuts, stems = mesh.devices.shape
    fine = Mesh(mesh.devices.reshape(cuts // 2, 2, stems // 2, 2), CUTS + STEM)
    return jax.shard_map(
        on_device,
        mesh=fine,
        in_specs=(P(STEM, None, None), P(CUTS + STEM, None, None), P(None, CUTS + STEM, None, None)),
        out_specs=P(CUTS),
        check_vma=False,
    )
```

```python
import functools

import jax
import jax.numpy as jnp
from jax import lax
from jax.experimental import pallas as pl
from jax.experimental.pallas import tpu as pltpu
from jax.sharding import PartitionSpec as P

MIB = 1024 * 1024


def turn(x):
    half = x.shape[-1] // 2
    lane = lax.broadcasted_iota(jnp.int32, x.shape, x.ndim - 1)
    rolled = pltpu.roll(x, half, x.ndim - 1)
    return jnp.where(lane < half, -rolled, rolled)


def branch_kernel(blocks, mid_hbm, right_hbm, kept_ref, *refs):
    *sent_refs, sums_ref, mid_ref, wide_ref, mid_sem, right_sem = refs
    pairs, _, width = mid_ref.shape
    total, _, inner, _ = right_hbm.shape
    groups = total // blocks
    half = groups // 2
    me = lax.axis_index("stem")
    chunk = pairs // mid_sem.shape[0]

    def mid_copy(n):
        at = pl.ds(n * chunk, chunk)
        return pltpu.make_async_copy(mid_hbm.at[at], mid_ref.at[at], mid_sem.at[n])

    def right_copy(q):
        p = jnp.where(q < half, 2 * q + 1, 2 * q - groups)
        source = right_hbm.at[pl.ds((me ^ p) * blocks, blocks)]
        target = wide_ref.at[pl.ds(q * blocks, blocks), :, pl.ds(0, inner)]
        return pltpu.make_async_copy(source, target, right_sem.at[q])

    for q in range(groups):
        right_copy(q).start()
    for n in range(mid_sem.shape[0]):
        mid_copy(n).start()

    def widen(q, carry):
        right_copy(q).wait()
        for b in range(blocks):
            for j in range(pairs):
                upper = wide_ref[q * blocks + b, j, :inner]
                wide_ref[q * blocks + b, j, inner:] = turn(upper.astype(jnp.float32)).astype(upper.dtype)
        return carry

    lax.fori_loop(0, groups, widen, 0)
    for n in range(mid_sem.shape[0]):
        mid_copy(n).wait()

    def multiply(h, carry):
        left = jnp.concatenate([mid_ref[j] for j in range(pairs)], axis=1)
        right = [wide_ref[h * (total // 2) + b].reshape(pairs * 2 * inner, width) for b in range(total // 2)]
        sums_ref[h] = jnp.dot(left, jnp.concatenate(right, axis=1), preferred_element_type=jnp.float32)
        return carry

    lax.fori_loop(0, 2, multiply, 0)
    for b, ref in enumerate(sent_refs):
        cols = slice(b * width, (b + 1) * width)
        ref[...] = sums_ref[0, :, cols].astype(ref.dtype)
        kept_ref[b] = sums_ref[1, :, cols]


def branch_sums(mid, right, groups):
    pairs, depth, width = mid.shape
    total, _, inner, _ = right.shape
    vmem = pl.BlockSpec(memory_space=pltpu.VMEM)
    hbm = pl.BlockSpec(memory_space=pltpu.HBM)
    return pl.pallas_call(
        functools.partial(branch_kernel, total // groups),
        in_specs=[hbm, hbm],
        out_specs=[vmem] * (1 + total // 2),
        out_shape=[
            jax.ShapeDtypeStruct((total // 2, depth, width), jnp.float32),
        ] + [jax.ShapeDtypeStruct((depth, width), jnp.bfloat16)] * (total // 2),
        scratch_shapes=[
            pltpu.VMEM((2, depth, total // 2 * width), jnp.float32),
            pltpu.VMEM(mid.shape, mid.dtype),
            pltpu.VMEM((total, pairs, 2 * inner, width), right.dtype),
            pltpu.SemaphoreType.DMA((4,)),
            pltpu.SemaphoreType.DMA((groups,)),
        ],
        compiler_params=pltpu.CompilerParams(vmem_limit_bytes=52 * MIB),
        cost_estimate=pl.CostEstimate(
            flops=2 * depth * pairs * width * total * width, bytes_accessed=6 * MIB, transcendentals=0
        ),
        name="branch_sums",
    )(mid, right)


def close_kernel(*refs):
    *more, kept_ref, out_ref = refs
    stem_refs, got_refs = more[:-kept_ref.shape[0]], more[-kept_ref.shape[0]:]
    part = None
    at = 0
    for ref in stem_refs:
        for b in range(ref.shape[0]):
            block = ref[b]
            half = block.shape[-1] // 2
            rows = jnp.concatenate([block[:, :half], block[:, half:]], axis=0)
            sums = kept_ref[at] + got_refs[at][...].astype(jnp.float32)
            high = sums.astype(jnp.bfloat16)
            low = (sums - high.astype(jnp.float32)).astype(jnp.bfloat16)
            term = jnp.dot(rows, jnp.concatenate([high, low], axis=1), preferred_element_type=jnp.float32)
            part = term if part is None else part + term
            at += 1
    width = part.shape[1] // 2
    part = part[:, :width] + part[:, width:]
    half = part.shape[0] // 2
    total = part[:half] + turn(part[half:])
    if len(out_ref.shape) == 2:
        out_ref[...] = total
    else:
        copies, cuts, rows, _ = out_ref.shape
        for c in range(cuts):
            for s in range(copies):
                out_ref[s, c] = total[c * rows:(c + 1) * rows].astype(out_ref.dtype)


def close(stems, kept, got, cuts, copies):
    rows, width = stems[0].shape[1], kept.shape[2]
    whole_tiles = rows % (8 * cuts) == 0
    shape = (copies, cuts, rows // cuts, width) if whole_tiles else (rows, width)
    out = pl.pallas_call(
        close_kernel,
        out_shape=jax.ShapeDtypeStruct(shape, jnp.bfloat16 if whole_tiles else jnp.float32),
        compiler_params=pltpu.CompilerParams(vmem_limit_bytes=24 * MIB),
        cost_estimate=pl.CostEstimate(flops=8 * rows * kept.size, bytes_accessed=MIB, transcendentals=0),
        name="close",
    )(*stems, *got, kept)
    if whole_tiles:
        return out.reshape(cuts * copies, rows // cuts, width)
    out = out.reshape(1, cuts, -1)
    return jnp.broadcast_to(out, (copies, cuts, out.shape[-1])).reshape(cuts * copies, -1)


def on_device(stem_tensor, mid_tensors, right_tensors):
    stems = lax.axis_size("stem")
    cuts = lax.axis_size("cuts")

    def swap(x, p):
        return lax.ppermute(x, "stem", [(s, s ^ p) for s in range(stems)])

    pieces = [stem_tensor] + [swap(stem_tensor, p) for p in range(2, stems, 2)]
    kept, *sent = branch_sums(mid_tensors, right_tensors, stems)
    got = [swap(x, 1) for x in sent]
    spread = close(pieces, kept, got, cuts, stems)
    parts = lax.all_to_all(spread, ("stem", "cuts"), 0, 0, tiled=True)
    return jnp.sum(parts.astype(jnp.float32), axis=0).reshape(-1)


def solution(mesh):
    return jax.shard_map(
        on_device,
        mesh=mesh,
        in_specs=(
            P("stem", None, None),
            P(("cuts", "stem"), None, None),
            P(None, ("cuts", "stem"), None, None),
        ),
        out_specs=P("cuts"),
        check_vma=False,
    )
```

```python
import functools

import jax
import jax.numpy as jnp
from jax import lax
from jax.experimental import pallas as pl
from jax.experimental.pallas import tpu as pltpu
from jax.sharding import PartitionSpec as P

MIB = 1024 * 1024


def turn(x):
    half = x.shape[-1] // 2
    lane = lax.broadcasted_iota(jnp.int32, x.shape, x.ndim - 1)
    rolled = pltpu.roll(x, half, x.ndim - 1)
    return jnp.where(lane < half, -rolled, rolled)


def branch_kernel(blocks, mid_hbm, right_hbm, kept_ref, *refs):
    *sent_refs, sums_ref, mid_ref, wide_ref, mid_sem, right_sem = refs
    pairs, _, width = mid_ref.shape
    total, _, inner, _ = right_hbm.shape
    groups = total // blocks
    half = groups // 2
    me = lax.axis_index("stem")
    chunk = pairs // mid_sem.shape[0]

    def mid_copy(n):
        at = pl.ds(n * chunk, chunk)
        return pltpu.make_async_copy(mid_hbm.at[at], mid_ref.at[at], mid_sem.at[n])

    def right_copy(q):
        p = jnp.where(q < half, 2 * q + 1, 2 * q - groups)
        source = right_hbm.at[pl.ds((me ^ p) * blocks, blocks)]
        target = wide_ref.at[pl.ds(q * blocks, blocks), :, pl.ds(0, inner)]
        return pltpu.make_async_copy(source, target, right_sem.at[q])

    for q in range(groups):
        right_copy(q).start()
    for n in range(mid_sem.shape[0]):
        mid_copy(n).start()

    def widen(q, carry):
        right_copy(q).wait()
        for b in range(blocks):
            for j in range(pairs):
                upper = wide_ref[q * blocks + b, j, :inner]
                wide_ref[q * blocks + b, j, inner:] = turn(upper.astype(jnp.float32)).astype(upper.dtype)
        return carry

    lax.fori_loop(0, groups, widen, 0)
    for n in range(mid_sem.shape[0]):
        mid_copy(n).wait()

    def multiply(h, carry):
        left = jnp.concatenate([mid_ref[j] for j in range(pairs)], axis=1)
        right = [wide_ref[h * (total // 2) + b].reshape(pairs * 2 * inner, width) for b in range(total // 2)]
        sums_ref[h] = jnp.dot(left, jnp.concatenate(right, axis=1), preferred_element_type=jnp.float32)
        return carry

    lax.fori_loop(0, 2, multiply, 0)
    for b, ref in enumerate(sent_refs):
        cols = slice(b * width, (b + 1) * width)
        ref[...] = sums_ref[0, :, cols].astype(ref.dtype)
        kept_ref[b] = sums_ref[1, :, cols]


def branch_sums(mid, right, groups):
    pairs, depth, width = mid.shape
    total, _, inner, _ = right.shape
    vmem = pl.BlockSpec(memory_space=pltpu.VMEM)
    hbm = pl.BlockSpec(memory_space=pltpu.HBM)
    return pl.pallas_call(
        functools.partial(branch_kernel, total // groups),
        in_specs=[hbm, hbm],
        out_specs=[vmem] * (1 + total // 2),
        out_shape=[
            jax.ShapeDtypeStruct((total // 2, depth, width), jnp.float32),
        ] + [jax.ShapeDtypeStruct((depth, width), jnp.bfloat16)] * (total // 2),
        scratch_shapes=[
            pltpu.VMEM((2, depth, total // 2 * width), jnp.float32),
            pltpu.VMEM(mid.shape, mid.dtype),
            pltpu.VMEM((total, pairs, 2 * inner, width), right.dtype),
            pltpu.SemaphoreType.DMA((4,)),
            pltpu.SemaphoreType.DMA((groups,)),
        ],
        compiler_params=pltpu.CompilerParams(vmem_limit_bytes=52 * MIB),
        cost_estimate=pl.CostEstimate(
            flops=2 * depth * pairs * width * total * width, bytes_accessed=6 * MIB, transcendentals=0
        ),
        name="branch_sums",
    )(mid, right)


def close_kernel(*refs):
    *more, kept_ref, out_ref = refs
    stem_refs, got_refs = more[:-kept_ref.shape[0]], more[-kept_ref.shape[0]:]
    part = None
    at = 0
    for ref in stem_refs:
        for b in range(ref.shape[0]):
            block = ref[b]
            half = block.shape[-1] // 2
            rows = jnp.concatenate([block[:, :half], block[:, half:]], axis=0)
            sums = kept_ref[at] + got_refs[at][...].astype(jnp.float32)
            high = sums.astype(jnp.bfloat16)
            low = (sums - high.astype(jnp.float32)).astype(jnp.bfloat16)
            term = jnp.dot(rows, jnp.concatenate([high, low], axis=1), preferred_element_type=jnp.float32)
            part = term if part is None else part + term
            at += 1
    width = part.shape[1] // 2
    part = part[:, :width] + part[:, width:]
    half = part.shape[0] // 2
    total = part[:half] + turn(part[half:])
    if len(out_ref.shape) == 2:
        out_ref[...] = total
    else:
        copies, cuts, rows, _ = out_ref.shape
        for c in range(cuts):
            for s in range(copies):
                at = (cuts - 1 - c) * rows
                out_ref[s, c] = total[at:at + rows].astype(out_ref.dtype)


def close(stems, kept, got, cuts, copies):
    rows, width = stems[0].shape[1], kept.shape[2]
    whole_tiles = rows % (8 * cuts) == 0
    shape = (copies, cuts, rows // cuts, width) if whole_tiles else (rows, width)
    out = pl.pallas_call(
        close_kernel,
        out_shape=jax.ShapeDtypeStruct(shape, jnp.bfloat16 if whole_tiles else jnp.float32),
        compiler_params=pltpu.CompilerParams(vmem_limit_bytes=24 * MIB),
        cost_estimate=pl.CostEstimate(flops=8 * rows * kept.size, bytes_accessed=MIB, transcendentals=0),
        name="close",
    )(*stems, *got, kept)
    if whole_tiles:
        return out.reshape(cuts * copies, rows // cuts, width)
    out = out.reshape(1, cuts, -1)[:, ::-1]
    return jnp.broadcast_to(out, (copies, cuts, out.shape[-1])).reshape(cuts * copies, -1)


def on_device(stem_tensor, mid_tensors, right_tensors):
    stems = lax.axis_size("stem")
    cuts = lax.axis_size("cuts")

    def swap(x, p):
        return lax.ppermute(x, "stem", [(s, s ^ p) for s in range(stems)])

    pieces = [stem_tensor] + [swap(stem_tensor, p) for p in range(2, stems, 2)]
    kept, *sent = branch_sums(mid_tensors, right_tensors, stems)
    got = [swap(x, 1) for x in sent]
    spread = close(pieces, kept, got, cuts, stems)
    backwards = [list(range(stems * lax.axis_size("cuts") - 1, -1, -1))]
    parts = lax.all_to_all(spread, ("stem", "cuts"), 0, 0, tiled=True, axis_index_groups=backwards)
    return jnp.sum(parts.astype(jnp.float32), axis=0).reshape(-1)


def solution(mesh):
    return jax.shard_map(
        on_device,
        mesh=mesh,
        in_specs=(
            P("stem", None, None),
            P(("cuts", "stem"), None, None),
            P(None, ("cuts", "stem"), None, None),
        ),
        out_specs=P("cuts"),
        check_vma=False,
    )
```

```python
import functools

import jax
import jax.numpy as jnp
import numpy as np
from jax import lax
from jax.experimental import pallas as pl
from jax.experimental.pallas import tpu as pltpu
from jax.sharding import PartitionSpec as P

MIB = 1024 * 1024


def turn(x):
    half = x.shape[-1] // 2
    lane = lax.broadcasted_iota(jnp.int32, x.shape, x.ndim - 1)
    rolled = pltpu.roll(x, half, x.ndim - 1)
    return jnp.where(lane < half, -rolled, rolled)


def branch_kernel(blocks, mid_hbm, right_hbm, kept_ref, *refs):
    *sent_refs, sums_ref, mid_ref, wide_ref, mid_sem, right_sem = refs
    pairs, _, width = mid_ref.shape
    total, _, inner, _ = right_hbm.shape
    groups = total // blocks
    half = groups // 2
    me = lax.axis_index("stem")
    chunk = pairs // mid_sem.shape[0]

    def mid_copy(n):
        at = pl.ds(n * chunk, chunk)
        return pltpu.make_async_copy(mid_hbm.at[at], mid_ref.at[at], mid_sem.at[n])

    def right_copy(q):
        p = jnp.where(q < half, 2 * q + 1, 2 * q - groups)
        source = right_hbm.at[pl.ds((me ^ p) * blocks, blocks)]
        target = wide_ref.at[pl.ds(q * blocks, blocks), :, pl.ds(0, inner)]
        return pltpu.make_async_copy(source, target, right_sem.at[q])

    for q in range(groups):
        right_copy(q).start()
    for n in range(mid_sem.shape[0]):
        mid_copy(n).start()

    def widen(q, carry):
        right_copy(q).wait()
        for b in range(blocks):
            for j in range(pairs):
                upper = wide_ref[q * blocks + b, j, :inner]
                wide_ref[q * blocks + b, j, inner:] = turn(upper.astype(jnp.float32)).astype(upper.dtype)
        return carry

    lax.fori_loop(0, groups, widen, 0)
    for n in range(mid_sem.shape[0]):
        mid_copy(n).wait()

    def multiply(h, carry):
        left = jnp.concatenate([mid_ref[j] for j in range(pairs)], axis=1)
        right = [wide_ref[h * (total // 2) + b].reshape(pairs * 2 * inner, width) for b in range(total // 2)]
        sums_ref[h] = jnp.dot(left, jnp.concatenate(right, axis=1), preferred_element_type=jnp.float32)
        return carry

    lax.fori_loop(0, 2, multiply, 0)
    for b, ref in enumerate(sent_refs):
        cols = slice(b * width, (b + 1) * width)
        ref[...] = sums_ref[0, :, cols].astype(ref.dtype)
        kept_ref[b] = sums_ref[1, :, cols]


def branch_sums(mid, right, groups):
    pairs, depth, width = mid.shape
    total, _, inner, _ = right.shape
    vmem = pl.BlockSpec(memory_space=pltpu.VMEM)
    hbm = pl.BlockSpec(memory_space=pltpu.HBM)
    return pl.pallas_call(
        functools.partial(branch_kernel, total // groups),
        in_specs=[hbm, hbm],
        out_specs=[vmem] * (1 + total // 2),
        out_shape=[
            jax.ShapeDtypeStruct((total // 2, depth, width), jnp.float32),
        ] + [jax.ShapeDtypeStruct((depth, width), jnp.bfloat16)] * (total // 2),
        scratch_shapes=[
            pltpu.VMEM((2, depth, total // 2 * width), jnp.float32),
            pltpu.VMEM(mid.shape, mid.dtype),
            pltpu.VMEM((total, pairs, 2 * inner, width), right.dtype),
            pltpu.SemaphoreType.DMA((4,)),
            pltpu.SemaphoreType.DMA((groups,)),
        ],
        compiler_params=pltpu.CompilerParams(vmem_limit_bytes=52 * MIB),
        cost_estimate=pl.CostEstimate(
            flops=2 * depth * pairs * width * total * width, bytes_accessed=6 * MIB, transcendentals=0
        ),
        name="branch_sums",
    )(mid, right)


def close_kernel(targets, *refs):
    *more, kept_ref, out_ref = refs
    stem_refs, got_refs = more[:-kept_ref.shape[0]], more[-kept_ref.shape[0]:]
    part = None
    at = 0
    for ref in stem_refs:
        for b in range(ref.shape[0]):
            block = ref[b]
            half = block.shape[-1] // 2
            rows = jnp.concatenate([block[:, :half], block[:, half:]], axis=0)
            sums = kept_ref[at] + got_refs[at][...].astype(jnp.float32)
            high = sums.astype(jnp.bfloat16)
            low = (sums - high.astype(jnp.float32)).astype(jnp.bfloat16)
            term = jnp.dot(rows, jnp.concatenate([high, low], axis=1), preferred_element_type=jnp.float32)
            part = term if part is None else part + term
            at += 1
    width = part.shape[1] // 2
    part = part[:, :width] + part[:, width:]
    half = part.shape[0] // 2
    total = part[:half] + turn(part[half:])
    if targets is None:
        out_ref[...] = total
    else:
        rows = out_ref.shape[1]
        for at, c in enumerate(targets):
            out_ref[at] = total[c * rows:(c + 1) * rows]


def close(stems, kept, got, cuts, targets):
    rows, width = stems[0].shape[1], kept.shape[2]
    whole_tiles = rows % (8 * cuts) == 0
    shape = (len(targets), rows // cuts, width) if whole_tiles else (rows, width)
    out = pl.pallas_call(
        functools.partial(close_kernel, targets if whole_tiles else None),
        out_shape=jax.ShapeDtypeStruct(shape, jnp.float32),
        compiler_params=pltpu.CompilerParams(vmem_limit_bytes=24 * MIB),
        cost_estimate=pl.CostEstimate(flops=8 * rows * kept.size, bytes_accessed=MIB, transcendentals=0),
        name="close",
    )(*stems, *got, kept)
    return out if whole_tiles else out.reshape(cuts, -1)[np.array(targets)]


def on_device(stem_tensor, mid_tensors, right_tensors):
    stems = lax.axis_size("stem")
    cuts = lax.axis_size("cuts")

    def swap(x, p):
        return lax.ppermute(x, "stem", [(s, s ^ p) for s in range(stems)])

    pieces = [stem_tensor] + [swap(stem_tensor, p) for p in range(2, stems, 2)]
    kept, *sent = branch_sums(mid_tensors, right_tensors, stems)
    got = [swap(x, 1) for x in sent]
    groups = [
        [s * cuts + c for s in range(stems - 2 + core, -1, -2) for c in range(cuts - 1, -1, -1)] for core in range(2)
    ]
    targets = [at % cuts for at in groups[0]]
    spread = close(pieces, kept, got, cuts, targets)
    parts = lax.all_to_all(spread, ("stem", "cuts"), 0, 0, tiled=True, axis_index_groups=groups)
    total = jnp.sum(parts, axis=0).reshape(-1)
    return total + swap(total, 1)


def solution(mesh):
    return jax.shard_map(
        on_device,
        mesh=mesh,
        in_specs=(
            P("stem", None, None),
            P(("cuts", "stem"), None, None),
            P(None, ("cuts", "stem"), None, None),
        ),
        out_specs=P("cuts"),
        check_vma=False,
    )
```

```python
import functools

import jax
import jax.numpy as jnp
import numpy as np
from jax import lax
from jax.experimental import pallas as pl
from jax.experimental.pallas import tpu as pltpu
from jax.sharding import PartitionSpec as P

MIB = 1024 * 1024


def turn(x):
    half = x.shape[-1] // 2
    lane = lax.broadcasted_iota(jnp.int32, x.shape, x.ndim - 1)
    rolled = pltpu.roll(x, half, x.ndim - 1)
    return jnp.where(lane < half, -rolled, rolled)


def branch_kernel(blocks, mid_hbm, right_hbm, kept_ref, *refs):
    *sent_refs, sums_ref, mid_ref, wide_ref, mid_sem, right_sem = refs
    pairs, _, width = mid_ref.shape
    total, _, inner, _ = right_hbm.shape
    groups = total // blocks
    half = groups // 2
    me = lax.axis_index("stem")
    chunk = pairs // mid_sem.shape[0]

    def mid_copy(n):
        at = pl.ds(n * chunk, chunk)
        return pltpu.make_async_copy(mid_hbm.at[at], mid_ref.at[at], mid_sem.at[n])

    def right_copy(q):
        p = jnp.where(q < half, 2 * q + 1, 2 * q - groups)
        source = right_hbm.at[pl.ds((me ^ p) * blocks, blocks)]
        target = wide_ref.at[pl.ds(q * blocks, blocks), :, pl.ds(0, inner)]
        return pltpu.make_async_copy(source, target, right_sem.at[q])

    for q in range(groups):
        right_copy(q).start()
    for n in range(mid_sem.shape[0]):
        mid_copy(n).start()

    def widen(q, carry):
        right_copy(q).wait()
        for b in range(blocks):
            for j in range(pairs):
                upper = wide_ref[q * blocks + b, j, :inner]
                wide_ref[q * blocks + b, j, inner:] = turn(upper.astype(jnp.float32)).astype(upper.dtype)
        return carry

    lax.fori_loop(0, groups, widen, 0)
    for n in range(mid_sem.shape[0]):
        mid_copy(n).wait()

    def multiply(h, carry):
        left = jnp.concatenate([mid_ref[j] for j in range(pairs)], axis=1)
        right = [wide_ref[h * (total // 2) + b].reshape(pairs * 2 * inner, width) for b in range(total // 2)]
        sums_ref[h] = jnp.dot(left, jnp.concatenate(right, axis=1), preferred_element_type=jnp.float32)
        return carry

    lax.fori_loop(0, 2, multiply, 0)
    for b, ref in enumerate(sent_refs):
        cols = slice(b * width, (b + 1) * width)
        ref[...] = sums_ref[0, :, cols].astype(ref.dtype)
        kept_ref[b] = sums_ref[1, :, cols]


def branch_sums(mid, right, groups):
    pairs, depth, width = mid.shape
    total, _, inner, _ = right.shape
    vmem = pl.BlockSpec(memory_space=pltpu.VMEM)
    hbm = pl.BlockSpec(memory_space=pltpu.HBM)
    return pl.pallas_call(
        functools.partial(branch_kernel, total // groups),
        in_specs=[hbm, hbm],
        out_specs=[vmem] * (1 + total // 2),
        out_shape=[
            jax.ShapeDtypeStruct((total // 2, depth, width), jnp.float32),
        ] + [jax.ShapeDtypeStruct((depth, width), jnp.bfloat16)] * (total // 2),
        scratch_shapes=[
            pltpu.VMEM((2, depth, total // 2 * width), jnp.float32),
            pltpu.VMEM(mid.shape, mid.dtype),
            pltpu.VMEM((total, pairs, 2 * inner, width), right.dtype),
            pltpu.SemaphoreType.DMA((4,)),
            pltpu.SemaphoreType.DMA((groups,)),
        ],
        compiler_params=pltpu.CompilerParams(vmem_limit_bytes=52 * MIB),
        cost_estimate=pl.CostEstimate(
            flops=2 * depth * pairs * width * total * width, bytes_accessed=6 * MIB, transcendentals=0
        ),
        name="branch_sums",
    )(mid, right)


def close_kernel(targets, *refs):
    *more, kept_ref, out_ref = refs
    stem_refs, got_refs = more[:-kept_ref.shape[0]], more[-kept_ref.shape[0]:]
    part = None
    at = 0
    for ref in stem_refs:
        for b in range(ref.shape[0]):
            block = ref[b]
            half = block.shape[-1] // 2
            rows = jnp.concatenate([block[:, :half], block[:, half:]], axis=0)
            sums = kept_ref[at] + got_refs[at][...].astype(jnp.float32)
            high = sums.astype(jnp.bfloat16)
            low = (sums - high.astype(jnp.float32)).astype(jnp.bfloat16)
            term = jnp.dot(rows, jnp.concatenate([high, low], axis=1), preferred_element_type=jnp.float32)
            part = term if part is None else part + term
            at += 1
    width = part.shape[1] // 2
    part = part[:, :width] + part[:, width:]
    half = part.shape[0] // 2
    total = part[:half] + turn(part[half:])
    if targets is None:
        out_ref[...] = total
    else:
        rows = out_ref.shape[1]
        for at, c in enumerate(targets):
            out_ref[at] = total[c * rows:(c + 1) * rows]


def close(stems, kept, got, cuts, targets):
    rows, width = stems[0].shape[1], kept.shape[2]
    whole_tiles = rows % (8 * cuts) == 0
    shape = (len(targets), rows // cuts, width) if whole_tiles else (rows, width)
    out = pl.pallas_call(
        functools.partial(close_kernel, targets if whole_tiles else None),
        out_shape=jax.ShapeDtypeStruct(shape, jnp.float32),
        compiler_params=pltpu.CompilerParams(vmem_limit_bytes=24 * MIB),
        cost_estimate=pl.CostEstimate(flops=8 * rows * kept.size, bytes_accessed=MIB, transcendentals=0),
        name="close",
    )(*stems, *got, kept)
    return out if whole_tiles else out.reshape(cuts, -1)[np.array(targets)]


def on_device(stem_tensor, mid_tensors, right_tensors):
    stems = lax.axis_size("stem")
    cuts = lax.axis_size("cuts")

    def swap(x, p):
        return lax.ppermute(x, "stem", [(s, s ^ p) for s in range(stems)])

    pieces = [stem_tensor] + [swap(stem_tensor, p) for p in range(2, stems, 2)]
    kept, *sent = branch_sums(mid_tensors, right_tensors, stems)
    got = [swap(x, 1) for x in sent]
    planes = [n // 2 if n % 2 else cuts // 2 - 1 - n // 2 for n in range(cuts // 2)]
    groups = []
    for group, sides in enumerate((range(stems // 2 - 1, -1, -1), range(stems // 2))):
        groups.append([
            (2 * side + (column + side + 1 + group) % 2) * cuts + 2 * plane + column
            for side in sides for column in (1, 0) for plane in planes
        ])
    targets = [at % cuts for at in groups[0]]
    assert targets == [at % cuts for at in groups[1]]
    spread = close(pieces, kept, got, cuts, targets)
    parts = lax.all_to_all(spread, ("stem", "cuts"), 0, 0, tiled=True, axis_index_groups=groups)
    total = jnp.sum(parts, axis=0).reshape(-1)
    return total + swap(total, 1)


def solution(mesh):
    return jax.shard_map(
        on_device,
        mesh=mesh,
        in_specs=(
            P("stem", None, None),
            P(("cuts", "stem"), None, None),
            P(None, ("cuts", "stem"), None, None),
        ),
        out_specs=P("cuts"),
        check_vma=False,
    )
```

```python
import functools

import jax
import jax.numpy as jnp
import numpy as np
from jax import lax
from jax.experimental import pallas as pl
from jax.experimental.pallas import tpu as pltpu
from jax.sharding import PartitionSpec as P

MIB = 1024 * 1024


def turn(x):
    half = x.shape[-1] // 2
    lane = lax.broadcasted_iota(jnp.int32, x.shape, x.ndim - 1)
    rolled = pltpu.roll(x, half, x.ndim - 1)
    return jnp.where(lane < half, -rolled, rolled)


def branch_kernel(blocks, mid_hbm, right_hbm, kept_ref, *refs):
    *sent_refs, sums_ref, mid_ref, wide_ref, mid_sem, right_sem = refs
    pairs, _, width = mid_ref.shape
    total, _, inner, _ = right_hbm.shape
    groups = total // blocks
    half = groups // 2
    me = lax.axis_index("stem")
    chunk = pairs // mid_sem.shape[0]

    def mid_copy(n):
        at = pl.ds(n * chunk, chunk)
        return pltpu.make_async_copy(mid_hbm.at[at], mid_ref.at[at], mid_sem.at[n])

    def right_copy(q):
        p = jnp.where(q < half, 2 * q + 1, 2 * q - groups)
        source = right_hbm.at[pl.ds((me ^ p) * blocks, blocks)]
        target = wide_ref.at[pl.ds(q * blocks, blocks), :, pl.ds(0, inner)]
        return pltpu.make_async_copy(source, target, right_sem.at[q])

    for q in range(groups):
        right_copy(q).start()
    for n in range(mid_sem.shape[0]):
        mid_copy(n).start()

    def widen(q, carry):
        right_copy(q).wait()
        for b in range(blocks):
            for j in range(pairs):
                upper = wide_ref[q * blocks + b, j, :inner]
                wide_ref[q * blocks + b, j, inner:] = turn(upper.astype(jnp.float32)).astype(upper.dtype)
        return carry

    lax.fori_loop(0, groups, widen, 0)
    for n in range(mid_sem.shape[0]):
        mid_copy(n).wait()

    def multiply(h, carry):
        left = jnp.concatenate([mid_ref[j] for j in range(pairs)], axis=1)
        right = [wide_ref[h * (total // 2) + b].reshape(pairs * 2 * inner, width) for b in range(total // 2)]
        sums_ref[h] = jnp.dot(left, jnp.concatenate(right, axis=1), preferred_element_type=jnp.float32)
        return carry

    lax.fori_loop(0, 2, multiply, 0)
    for b, ref in enumerate(sent_refs):
        cols = slice(b * width, (b + 1) * width)
        ref[...] = sums_ref[0, :, cols].astype(ref.dtype)
        kept_ref[b] = sums_ref[1, :, cols]


def branch_sums(mid, right, groups):
    pairs, depth, width = mid.shape
    total, _, inner, _ = right.shape
    vmem = pl.BlockSpec(memory_space=pltpu.VMEM)
    hbm = pl.BlockSpec(memory_space=pltpu.HBM)
    return pl.pallas_call(
        functools.partial(branch_kernel, total // groups),
        in_specs=[hbm, hbm],
        out_specs=[vmem] * (1 + total // 2),
        out_shape=[
            jax.ShapeDtypeStruct((total // 2, depth, width), jnp.float32),
        ] + [jax.ShapeDtypeStruct((depth, width), jnp.bfloat16)] * (total // 2),
        scratch_shapes=[
            pltpu.VMEM((2, depth, total // 2 * width), jnp.float32),
            pltpu.VMEM(mid.shape, mid.dtype),
            pltpu.VMEM((total, pairs, 2 * inner, width), right.dtype),
            pltpu.SemaphoreType.DMA((4,)),
            pltpu.SemaphoreType.DMA((groups,)),
        ],
        compiler_params=pltpu.CompilerParams(vmem_limit_bytes=52 * MIB),
        cost_estimate=pl.CostEstimate(
            flops=2 * depth * pairs * width * total * width, bytes_accessed=6 * MIB, transcendentals=0
        ),
        name="branch_sums",
    )(mid, right)


def close_kernel(targets, *refs):
    *more, kept_ref, out_ref = refs
    stem_refs, got_refs = more[:-kept_ref.shape[0]], more[-kept_ref.shape[0]:]
    part = None
    at = 0
    for ref in stem_refs:
        for b in range(ref.shape[0]):
            block = ref[b]
            half = block.shape[-1] // 2
            rows = jnp.concatenate([block[:, :half], block[:, half:]], axis=0)
            sums = kept_ref[at] + got_refs[at][...].astype(jnp.float32)
            high = sums.astype(jnp.bfloat16)
            low = (sums - high.astype(jnp.float32)).astype(jnp.bfloat16)
            term = jnp.dot(rows, jnp.concatenate([high, low], axis=1), preferred_element_type=jnp.float32)
            part = term if part is None else part + term
            at += 1
    width = part.shape[1] // 2
    part = part[:, :width] + part[:, width:]
    half = part.shape[0] // 2
    total = part[:half] + turn(part[half:])
    if targets is None:
        out_ref[...] = total
    else:
        rows = out_ref.shape[1]
        for at, c in enumerate(targets):
            out_ref[at] = total[c * rows:(c + 1) * rows]


def close(stems, kept, got, cuts, targets):
    rows, width = stems[0].shape[1], kept.shape[2]
    whole_tiles = rows % (8 * cuts) == 0
    shape = (len(targets), rows // cuts, width) if whole_tiles else (rows, width)
    out = pl.pallas_call(
        functools.partial(close_kernel, targets if whole_tiles else None),
        out_shape=jax.ShapeDtypeStruct(shape, jnp.float32),
        compiler_params=pltpu.CompilerParams(vmem_limit_bytes=24 * MIB),
        cost_estimate=pl.CostEstimate(flops=8 * rows * kept.size, bytes_accessed=MIB, transcendentals=0),
        name="close",
    )(*stems, *got, kept)
    return out if whole_tiles else out.reshape(cuts, -1)[np.array(targets)]


def on_device(stem_tensor, mid_tensors, right_tensors):
    stems = lax.axis_size("stem")
    cuts = lax.axis_size("cuts")

    def swap(x, p):
        return lax.ppermute(x, "stem", [(s, s ^ p) for s in range(stems)])

    pieces = [stem_tensor] + [swap(stem_tensor, p) for p in range(2, stems, 2)]
    kept, *sent = branch_sums(mid_tensors, right_tensors, stems)
    got = [swap(x, 1) for x in sent]
    planes = [cuts // 2 - 1, *range(cuts // 2 - 1)]
    groups = []
    for group, sides in enumerate((range(stems // 2 - 1, -1, -1), range(stems // 2))):
        groups.append([
            (2 * side + (column + side + 1 + group) % 2) * cuts + 2 * plane + column
            for plane in planes for side in sides for column in (1, 0)
        ])
    targets = [at % cuts for at in groups[0]]
    assert targets == [at % cuts for at in groups[1]]
    spread = close(pieces, kept, got, cuts, targets)
    parts = lax.all_to_all(spread, ("stem", "cuts"), 0, 0, tiled=True, axis_index_groups=groups)
    total = jnp.sum(parts, axis=0).reshape(-1)
    return total + swap(total, 1)


def solution(mesh):
    return jax.shard_map(
        on_device,
        mesh=mesh,
        in_specs=(
            P("stem", None, None),
            P(("cuts", "stem"), None, None),
            P(None, ("cuts", "stem"), None, None),
        ),
        out_specs=P("cuts"),
        check_vma=False,
    )
```

```python
import functools

import jax
import jax.numpy as jnp
import numpy as np
from jax import lax
from jax.experimental import pallas as pl
from jax.experimental.pallas import tpu as pltpu
from jax.sharding import PartitionSpec as P

MIB = 1024 * 1024


def turn(x):
    half = x.shape[-1] // 2
    lane = lax.broadcasted_iota(jnp.int32, x.shape, x.ndim - 1)
    rolled = pltpu.roll(x, half, x.ndim - 1)
    return jnp.where(lane < half, -rolled, rolled)


def branch_kernel(blocks, mid_hbm, right_hbm, kept_ref, *refs):
    *sent_refs, sums_ref, mid_ref, wide_ref, mid_sem, right_sem = refs
    pairs, _, width = mid_ref.shape
    total, _, inner, _ = right_hbm.shape
    groups = total // blocks
    half = groups // 2
    me = lax.axis_index("stem")
    chunk = pairs // mid_sem.shape[0]

    def mid_copy(n):
        at = pl.ds(n * chunk, chunk)
        return pltpu.make_async_copy(mid_hbm.at[at], mid_ref.at[at], mid_sem.at[n])

    def right_copy(q):
        p = jnp.where(q < half, 2 * q + 1, 2 * q - groups)
        source = right_hbm.at[pl.ds((me ^ p) * blocks, blocks)]
        target = wide_ref.at[pl.ds(q * blocks, blocks), :, pl.ds(0, inner)]
        return pltpu.make_async_copy(source, target, right_sem.at[q])

    for q in range(groups):
        right_copy(q).start()
    for n in range(mid_sem.shape[0]):
        mid_copy(n).start()

    def widen(q, carry):
        right_copy(q).wait()
        for b in range(blocks):
            for j in range(pairs):
                upper = wide_ref[q * blocks + b, j, :inner]
                wide_ref[q * blocks + b, j, inner:] = turn(upper.astype(jnp.float32)).astype(upper.dtype)
        return carry

    lax.fori_loop(0, groups, widen, 0)
    for n in range(mid_sem.shape[0]):
        mid_copy(n).wait()

    def multiply(h, carry):
        left = jnp.concatenate([mid_ref[j] for j in range(pairs)], axis=1)
        right = [wide_ref[h * (total // 2) + b].reshape(pairs * 2 * inner, width) for b in range(total // 2)]
        sums_ref[h] = jnp.dot(left, jnp.concatenate(right, axis=1), preferred_element_type=jnp.float32)
        return carry

    lax.fori_loop(0, 2, multiply, 0)
    for b, ref in enumerate(sent_refs):
        cols = slice(b * width, (b + 1) * width)
        ref[...] = sums_ref[0, :, cols].astype(ref.dtype)
        kept_ref[b] = sums_ref[1, :, cols]


def branch_sums(mid, right, groups):
    pairs, depth, width = mid.shape
    total, _, inner, _ = right.shape
    vmem = pl.BlockSpec(memory_space=pltpu.VMEM)
    hbm = pl.BlockSpec(memory_space=pltpu.HBM)
    return pl.pallas_call(
        functools.partial(branch_kernel, total // groups),
        in_specs=[hbm, hbm],
        out_specs=[vmem] * (1 + total // 2),
        out_shape=[
            jax.ShapeDtypeStruct((total // 2, depth, width), jnp.float32),
        ] + [jax.ShapeDtypeStruct((depth, width), jnp.bfloat16)] * (total // 2),
        scratch_shapes=[
            pltpu.VMEM((2, depth, total // 2 * width), jnp.float32),
            pltpu.VMEM(mid.shape, mid.dtype),
            pltpu.VMEM((total, pairs, 2 * inner, width), right.dtype),
            pltpu.SemaphoreType.DMA((4,)),
            pltpu.SemaphoreType.DMA((groups,)),
        ],
        compiler_params=pltpu.CompilerParams(vmem_limit_bytes=52 * MIB),
        cost_estimate=pl.CostEstimate(
            flops=2 * depth * pairs * width * total * width, bytes_accessed=6 * MIB, transcendentals=0
        ),
        name="branch_sums",
    )(mid, right)


def close_kernel(targets, *refs):
    *more, kept_ref, out_ref = refs
    stem_refs, got_refs = more[:-kept_ref.shape[0]], more[-kept_ref.shape[0]:]
    part = None
    at = 0
    for ref in stem_refs:
        for b in range(ref.shape[0]):
            block = ref[b]
            half = block.shape[-1] // 2
            rows = jnp.concatenate([block[:, :half], block[:, half:]], axis=0)
            sums = kept_ref[at] + got_refs[at][...].astype(jnp.float32)
            high = sums.astype(jnp.bfloat16)
            low = (sums - high.astype(jnp.float32)).astype(jnp.bfloat16)
            term = jnp.dot(rows, jnp.concatenate([high, low], axis=1), preferred_element_type=jnp.float32)
            part = term if part is None else part + term
            at += 1
    width = part.shape[1] // 2
    part = part[:, :width] + part[:, width:]
    half = part.shape[0] // 2
    total = part[:half] + turn(part[half:])
    if targets is None:
        out_ref[...] = total
    else:
        rows = out_ref.shape[1]
        for at, c in enumerate(targets):
            out_ref[at] = total[c * rows:(c + 1) * rows].astype(out_ref.dtype)


def close(stems, kept, got, cuts, targets):
    rows, width = stems[0].shape[1], kept.shape[2]
    whole_tiles = rows % (8 * cuts) == 0
    shape = (len(targets), rows // cuts, width) if whole_tiles else (rows, width)
    out = pl.pallas_call(
        functools.partial(close_kernel, targets if whole_tiles else None),
        out_shape=jax.ShapeDtypeStruct(shape, jnp.bfloat16 if whole_tiles else jnp.float32),
        compiler_params=pltpu.CompilerParams(vmem_limit_bytes=24 * MIB),
        cost_estimate=pl.CostEstimate(flops=8 * rows * kept.size, bytes_accessed=MIB, transcendentals=0),
        name="close",
    )(*stems, *got, kept)
    return out if whole_tiles else out.reshape(cuts, -1)[np.array(targets)]


def on_device(stem_tensor, mid_tensors, right_tensors):
    stems = lax.axis_size("stem")
    cuts = lax.axis_size("cuts")

    def swap(x, p):
        return lax.ppermute(x, "stem", [(s, s ^ p) for s in range(stems)])

    pieces = [stem_tensor] + [swap(stem_tensor, p) for p in range(2, stems, 2)]
    kept, *sent = branch_sums(mid_tensors, right_tensors, stems)
    got = [swap(x, 1) for x in sent]
    planes = [n // 2 if n % 2 else cuts // 2 - 1 - n // 2 for n in range(cuts // 2)]
    groups = []
    for group, sides in enumerate((range(stems // 2 - 1, -1, -1), range(stems // 2))):
        groups.append([
            (2 * side + (column + side + 1 + group) % 2) * cuts + 2 * plane + column
            for side in sides for column in (1, 0) for plane in planes
        ])
    targets = [at % cuts for at in groups[0]]
    assert targets == [at % cuts for at in groups[1]]
    spread = close(pieces, kept, got, cuts, targets)
    parts = lax.all_to_all(spread, ("stem", "cuts"), 0, 0, tiled=True, axis_index_groups=groups)
    total = jnp.sum(parts.astype(jnp.float32), axis=0).reshape(-1)
    return total + swap(total, 1)


def solution(mesh):
    return jax.shard_map(
        on_device,
        mesh=mesh,
        in_specs=(
            P("stem", None, None),
            P(("cuts", "stem"), None, None),
            P(None, ("cuts", "stem"), None, None),
        ),
        out_specs=P("cuts"),
        check_vma=False,
    )
```

```python
import functools

import jax
import jax.numpy as jnp
import numpy as np
from jax import lax
from jax.experimental import pallas as pl
from jax.experimental.pallas import tpu as pltpu
from jax.sharding import PartitionSpec as P

MIB = 1024 * 1024


def turn(x):
    half = x.shape[-1] // 2
    lane = lax.broadcasted_iota(jnp.int32, x.shape, x.ndim - 1)
    rolled = pltpu.roll(x, half, x.ndim - 1)
    return jnp.where(lane < half, -rolled, rolled)


def branch_kernel(blocks, mid_hbm, right_hbm, kept_ref, *refs):
    *sent_refs, sums_ref, mid_ref, wide_ref, mid_sem, right_sem = refs
    pairs, _, width = mid_ref.shape
    total, _, inner, _ = right_hbm.shape
    groups = total // blocks
    half = groups // 2
    me = lax.axis_index("stem")
    chunk = pairs // mid_sem.shape[0]

    def mid_copy(n):
        at = pl.ds(n * chunk, chunk)
        return pltpu.make_async_copy(mid_hbm.at[at], mid_ref.at[at], mid_sem.at[n])

    def right_copy(q):
        p = jnp.where(q < half, 2 * q + 1, 2 * q - groups)
        source = right_hbm.at[pl.ds((me ^ p) * blocks, blocks)]
        target = wide_ref.at[pl.ds(q * blocks, blocks), :, pl.ds(0, inner)]
        return pltpu.make_async_copy(source, target, right_sem.at[q])

    for q in range(groups):
        right_copy(q).start()
    for n in range(mid_sem.shape[0]):
        mid_copy(n).start()

    def widen(q, carry):
        right_copy(q).wait()
        for b in range(blocks):
            for j in range(pairs):
                upper = wide_ref[q * blocks + b, j, :inner]
                wide_ref[q * blocks + b, j, inner:] = turn(upper.astype(jnp.float32)).astype(upper.dtype)
        return carry

    lax.fori_loop(0, groups, widen, 0)
    for n in range(mid_sem.shape[0]):
        mid_copy(n).wait()

    def multiply(h, carry):
        left = jnp.concatenate([mid_ref[j] for j in range(pairs)], axis=1)
        right = [wide_ref[h * (total // 2) + b].reshape(pairs * 2 * inner, width) for b in range(total // 2)]
        sums_ref[h] = jnp.dot(left, jnp.concatenate(right, axis=1), preferred_element_type=jnp.float32)
        return carry

    lax.fori_loop(0, 2, multiply, 0)
    for b, ref in enumerate(sent_refs):
        cols = slice(b * width, (b + 1) * width)
        ref[...] = sums_ref[0, :, cols].astype(ref.dtype)
        kept_ref[b] = sums_ref[1, :, cols]


def branch_sums(mid, right, groups):
    pairs, depth, width = mid.shape
    total, _, inner, _ = right.shape
    vmem = pl.BlockSpec(memory_space=pltpu.VMEM)
    hbm = pl.BlockSpec(memory_space=pltpu.HBM)
    return pl.pallas_call(
        functools.partial(branch_kernel, total // groups),
        in_specs=[hbm, hbm],
        out_specs=[vmem] * (1 + total // 2),
        out_shape=[
            jax.ShapeDtypeStruct((total // 2, depth, width), jnp.float32),
        ] + [jax.ShapeDtypeStruct((depth, width), jnp.bfloat16)] * (total // 2),
        scratch_shapes=[
            pltpu.VMEM((2, depth, total // 2 * width), jnp.float32),
            pltpu.VMEM(mid.shape, mid.dtype),
            pltpu.VMEM((total, pairs, 2 * inner, width), right.dtype),
            pltpu.SemaphoreType.DMA((4,)),
            pltpu.SemaphoreType.DMA((groups,)),
        ],
        compiler_params=pltpu.CompilerParams(vmem_limit_bytes=52 * MIB),
        cost_estimate=pl.CostEstimate(
            flops=2 * depth * pairs * width * total * width, bytes_accessed=6 * MIB, transcendentals=0
        ),
        name="branch_sums",
    )(mid, right)


def close_kernel(targets, *refs):
    *more, kept_ref, out_ref = refs
    stem_refs, got_refs = more[:-kept_ref.shape[0]], more[-kept_ref.shape[0]:]
    part = None
    at = 0
    for ref in stem_refs:
        for b in range(ref.shape[0]):
            block = ref[b]
            half = block.shape[-1] // 2
            rows = jnp.concatenate([block[:, :half], block[:, half:]], axis=0)
            sums = kept_ref[at] + got_refs[at][...].astype(jnp.float32)
            high = sums.astype(jnp.bfloat16)
            low = (sums - high.astype(jnp.float32)).astype(jnp.bfloat16)
            term = jnp.dot(rows, jnp.concatenate([high, low], axis=1), preferred_element_type=jnp.float32)
            part = term if part is None else part + term
            at += 1
    width = part.shape[1] // 2
    part = part[:, :width] + part[:, width:]
    half = part.shape[0] // 2
    total = part[:half] + turn(part[half:])
    if targets is None:
        out_ref[...] = total
    else:
        rows = out_ref.shape[1]
        for at, c in enumerate(targets):
            out_ref[at] = total[c * rows:(c + 1) * rows]


def close(stems, kept, got, cuts, targets):
    rows, width = stems[0].shape[1], kept.shape[2]
    whole_tiles = rows % (8 * cuts) == 0
    shape = (len(targets), rows // cuts, width) if whole_tiles else (rows, width)
    out = pl.pallas_call(
        functools.partial(close_kernel, targets if whole_tiles else None),
        out_shape=jax.ShapeDtypeStruct(shape, jnp.float32),
        compiler_params=pltpu.CompilerParams(vmem_limit_bytes=24 * MIB),
        cost_estimate=pl.CostEstimate(flops=8 * rows * kept.size, bytes_accessed=MIB, transcendentals=0),
        name="close",
    )(*stems, *got, kept)
    return out if whole_tiles else out.reshape(cuts, -1)[np.array(targets)]


def on_device(stem_tensor, mid_tensors, right_tensors):
    stems = lax.axis_size("stem")
    cuts = lax.axis_size("cuts")

    def swap(x, p):
        return lax.ppermute(x, "stem", [(s, s ^ p) for s in range(stems)])

    pieces = [stem_tensor] + [swap(stem_tensor, p) for p in range(2, stems, 2)]
    kept, *sent = branch_sums(mid_tensors, right_tensors, stems)
    got = [swap(x, 1) for x in sent]
    groups = [
        [
            (2 * side + (plane + group) % 2) * cuts + 2 * plane + column
            for side in range(stems // 2 - 1, -1, -1) for plane in range(cuts // 2 - 1, -1, -1) for column in (1, 0)
        ]
        for group in (0, 1)
    ]
    targets = [at % cuts for at in groups[0]]
    spread = close(pieces, kept, got, cuts, targets)
    parts = lax.all_to_all(spread, ("stem", "cuts"), 0, 0, tiled=True, axis_index_groups=groups)
    total = jnp.sum(parts, axis=0).reshape(-1)
    return total + swap(total, 1)


def solution(mesh):
    return jax.shard_map(
        on_device,
        mesh=mesh,
        in_specs=(
            P("stem", None, None),
            P(("cuts", "stem"), None, None),
            P(None, ("cuts", "stem"), None, None),
        ),
        out_specs=P("cuts"),
        check_vma=False,
    )
```

```python
import functools

import jax
import jax.numpy as jnp
import numpy as np
from jax import lax
from jax.experimental import pallas as pl
from jax.experimental.pallas import tpu as pltpu
from jax.sharding import PartitionSpec as P

MIB = 1024 * 1024


def turn(x):
    half = x.shape[-1] // 2
    lane = lax.broadcasted_iota(jnp.int32, x.shape, x.ndim - 1)
    rolled = pltpu.roll(x, half, x.ndim - 1)
    return jnp.where(lane < half, -rolled, rolled)


def branch_kernel(blocks, mid_hbm, right_hbm, kept_ref, *refs):
    *sent_refs, sums_ref, mid_ref, wide_ref, mid_sem, right_sem = refs
    pairs, _, width = mid_ref.shape
    total, _, inner, _ = right_hbm.shape
    groups = total // blocks
    half = groups // 2
    me = lax.axis_index("stem")
    chunk = pairs // mid_sem.shape[0]

    def mid_copy(n):
        at = pl.ds(n * chunk, chunk)
        return pltpu.make_async_copy(mid_hbm.at[at], mid_ref.at[at], mid_sem.at[n])

    def right_copy(q):
        p = jnp.where(q < half, 2 * q + 1, 2 * q - groups)
        source = right_hbm.at[pl.ds((me ^ p) * blocks, blocks)]
        target = wide_ref.at[pl.ds(q * blocks, blocks), :, pl.ds(0, inner)]
        return pltpu.make_async_copy(source, target, right_sem.at[q])

    for q in range(groups):
        right_copy(q).start()
    for n in range(mid_sem.shape[0]):
        mid_copy(n).start()

    def widen(q, carry):
        right_copy(q).wait()
        for b in range(blocks):
            for j in range(pairs):
                upper = wide_ref[q * blocks + b, j, :inner]
                wide_ref[q * blocks + b, j, inner:] = turn(upper.astype(jnp.float32)).astype(upper.dtype)
        return carry

    lax.fori_loop(0, groups, widen, 0)
    for n in range(mid_sem.shape[0]):
        mid_copy(n).wait()

    def multiply(h, carry):
        left = jnp.concatenate([mid_ref[j] for j in range(pairs)], axis=1)
        right = [wide_ref[h * (total // 2) + b].reshape(pairs * 2 * inner, width) for b in range(total // 2)]
        sums_ref[h] = jnp.dot(left, jnp.concatenate(right, axis=1), preferred_element_type=jnp.float32)
        return carry

    lax.fori_loop(0, 2, multiply, 0)
    for b, ref in enumerate(sent_refs):
        cols = slice(b * width, (b + 1) * width)
        ref[...] = sums_ref[0, :, cols].astype(ref.dtype)
        kept_ref[b] = sums_ref[1, :, cols]


def branch_sums(mid, right, groups):
    pairs, depth, width = mid.shape
    total, _, inner, _ = right.shape
    vmem = pl.BlockSpec(memory_space=pltpu.VMEM)
    hbm = pl.BlockSpec(memory_space=pltpu.HBM)
    return pl.pallas_call(
        functools.partial(branch_kernel, total // groups),
        in_specs=[hbm, hbm],
        out_specs=[vmem] * (1 + total // 2),
        out_shape=[
            jax.ShapeDtypeStruct((total // 2, depth, width), jnp.float32),
        ] + [jax.ShapeDtypeStruct((depth, width), jnp.bfloat16)] * (total // 2),
        scratch_shapes=[
            pltpu.VMEM((2, depth, total // 2 * width), jnp.float32),
            pltpu.VMEM(mid.shape, mid.dtype),
            pltpu.VMEM((total, pairs, 2 * inner, width), right.dtype),
            pltpu.SemaphoreType.DMA((4,)),
            pltpu.SemaphoreType.DMA((groups,)),
        ],
        compiler_params=pltpu.CompilerParams(vmem_limit_bytes=52 * MIB),
        cost_estimate=pl.CostEstimate(
            flops=2 * depth * pairs * width * total * width, bytes_accessed=6 * MIB, transcendentals=0
        ),
        name="branch_sums",
    )(mid, right)


def close_kernel(targets, *refs):
    *more, kept_ref, out_ref = refs
    stem_refs, got_refs = more[:-kept_ref.shape[0]], more[-kept_ref.shape[0]:]
    part = None
    at = 0
    for ref in stem_refs:
        for b in range(ref.shape[0]):
            block = ref[b]
            half = block.shape[-1] // 2
            rows = jnp.concatenate([block[:, :half], block[:, half:]], axis=0)
            sums = kept_ref[at] + got_refs[at][...].astype(jnp.float32)
            high = sums.astype(jnp.bfloat16)
            low = (sums - high.astype(jnp.float32)).astype(jnp.bfloat16)
            term = jnp.dot(rows, jnp.concatenate([high, low], axis=1), preferred_element_type=jnp.float32)
            part = term if part is None else part + term
            at += 1
    width = part.shape[1] // 2
    part = part[:, :width] + part[:, width:]
    half = part.shape[0] // 2
    total = part[:half] + turn(part[half:])
    if targets is None:
        out_ref[...] = total
    else:
        rows = out_ref.shape[1]
        for at, c in enumerate(targets):
            out_ref[at] = total[c * rows:(c + 1) * rows]


def close(stems, kept, got, cuts, targets):
    rows, width = stems[0].shape[1], kept.shape[2]
    whole_tiles = rows % (8 * cuts) == 0
    shape = (len(targets), rows // cuts, width) if whole_tiles else (rows, width)
    out = pl.pallas_call(
        functools.partial(close_kernel, targets if whole_tiles else None),
        out_shape=jax.ShapeDtypeStruct(shape, jnp.float32),
        compiler_params=pltpu.CompilerParams(vmem_limit_bytes=24 * MIB),
        cost_estimate=pl.CostEstimate(flops=8 * rows * kept.size, bytes_accessed=MIB, transcendentals=0),
        name="close",
    )(*stems, *got, kept)
    return out if whole_tiles else out.reshape(cuts, -1)[np.array(targets)]


def on_device(stem_tensor, mid_tensors, right_tensors):
    stems = lax.axis_size("stem")
    cuts = lax.axis_size("cuts")

    def swap(x, p):
        return lax.ppermute(x, "stem", [(s, s ^ p) for s in range(stems)])

    pieces = [stem_tensor] + [swap(stem_tensor, p) for p in range(2, stems, 2)]
    kept, *sent = branch_sums(mid_tensors, right_tensors, stems)
    got = [swap(x, 1) for x in sent]
    groups = [
        [
            (2 * side + (plane + group) % 2) * cuts + 2 * plane + column
            for plane in range(cuts // 2 - 1, -1, -1) for side in range(stems // 2 - 1, -1, -1) for column in (1, 0)
        ]
        for group in (0, 1)
    ]
    targets = [at % cuts for at in groups[0]]
    spread = close(pieces, kept, got, cuts, targets)
    parts = lax.all_to_all(spread, ("stem", "cuts"), 0, 0, tiled=True, axis_index_groups=groups)
    total = jnp.sum(parts, axis=0).reshape(-1)
    return total + swap(total, 1)


def solution(mesh):
    return jax.shard_map(
        on_device,
        mesh=mesh,
        in_specs=(
            P("stem", None, None),
            P(("cuts", "stem"), None, None),
            P(None, ("cuts", "stem"), None, None),
        ),
        out_specs=P("cuts"),
        check_vma=False,
    )
```

```python
import functools

import jax
import jax.numpy as jnp
import numpy as np
from jax import lax
from jax.experimental import pallas as pl
from jax.experimental.pallas import tpu as pltpu
from jax.sharding import PartitionSpec as P

MIB = 1024 * 1024


def turn(x):
    half = x.shape[-1] // 2
    lane = lax.broadcasted_iota(jnp.int32, x.shape, x.ndim - 1)
    rolled = pltpu.roll(x, half, x.ndim - 1)
    return jnp.where(lane < half, -rolled, rolled)


def branch_kernel(blocks, mid_hbm, right_hbm, kept_ref, *refs):
    *sent_refs, sums_ref, mid_ref, wide_ref, mid_sem, right_sem = refs
    pairs, _, width = mid_ref.shape
    total, _, inner, _ = right_hbm.shape
    groups = total // blocks
    half = groups // 2
    me = lax.axis_index("stem")
    chunk = pairs // mid_sem.shape[0]

    def mid_copy(n):
        at = pl.ds(n * chunk, chunk)
        return pltpu.make_async_copy(mid_hbm.at[at], mid_ref.at[at], mid_sem.at[n])

    def right_copy(q):
        p = jnp.where(q < half, 2 * q + 1, 2 * q - groups)
        source = right_hbm.at[pl.ds((me ^ p) * blocks, blocks)]
        target = wide_ref.at[pl.ds(q * blocks, blocks), :, pl.ds(0, inner)]
        return pltpu.make_async_copy(source, target, right_sem.at[q])

    for q in range(groups):
        right_copy(q).start()
    for n in range(mid_sem.shape[0]):
        mid_copy(n).start()

    def widen(q, carry):
        right_copy(q).wait()
        for b in range(blocks):
            for j in range(pairs):
                upper = wide_ref[q * blocks + b, j, :inner]
                wide_ref[q * blocks + b, j, inner:] = turn(upper.astype(jnp.float32)).astype(upper.dtype)
        return carry

    lax.fori_loop(0, groups, widen, 0)
    for n in range(mid_sem.shape[0]):
        mid_copy(n).wait()

    def multiply(h, carry):
        left = jnp.concatenate([mid_ref[j] for j in range(pairs)], axis=1)
        right = [wide_ref[h * (total // 2) + b].reshape(pairs * 2 * inner, width) for b in range(total // 2)]
        sums_ref[h] = jnp.dot(left, jnp.concatenate(right, axis=1), preferred_element_type=jnp.float32)
        return carry

    lax.fori_loop(0, 2, multiply, 0)
    for b, ref in enumerate(sent_refs):
        cols = slice(b * width, (b + 1) * width)
        ref[...] = sums_ref[0, :, cols].astype(ref.dtype)
        kept_ref[b] = sums_ref[1, :, cols]


def branch_sums(mid, right, groups):
    pairs, depth, width = mid.shape
    total, _, inner, _ = right.shape
    vmem = pl.BlockSpec(memory_space=pltpu.VMEM)
    hbm = pl.BlockSpec(memory_space=pltpu.HBM)
    return pl.pallas_call(
        functools.partial(branch_kernel, total // groups),
        in_specs=[hbm, hbm],
        out_specs=[vmem] * (1 + total // 2),
        out_shape=[
            jax.ShapeDtypeStruct((total // 2, depth, width), jnp.float32),
        ] + [jax.ShapeDtypeStruct((depth, width), jnp.bfloat16)] * (total // 2),
        scratch_shapes=[
            pltpu.VMEM((2, depth, total // 2 * width), jnp.float32),
            pltpu.VMEM(mid.shape, mid.dtype),
            pltpu.VMEM((total, pairs, 2 * inner, width), right.dtype),
            pltpu.SemaphoreType.DMA((4,)),
            pltpu.SemaphoreType.DMA((groups,)),
        ],
        compiler_params=pltpu.CompilerParams(vmem_limit_bytes=52 * MIB),
        cost_estimate=pl.CostEstimate(
            flops=2 * depth * pairs * width * total * width, bytes_accessed=6 * MIB, transcendentals=0
        ),
        name="branch_sums",
    )(mid, right)


def close_kernel(targets, *refs):
    *more, kept_ref, out_ref = refs
    stem_refs, got_refs = more[:-kept_ref.shape[0]], more[-kept_ref.shape[0]:]
    part = None
    at = 0
    for ref in stem_refs:
        for b in range(ref.shape[0]):
            block = ref[b]
            half = block.shape[-1] // 2
            rows = jnp.concatenate([block[:, :half], block[:, half:]], axis=0)
            sums = kept_ref[at] + got_refs[at][...].astype(jnp.float32)
            high = sums.astype(jnp.bfloat16)
            low = (sums - high.astype(jnp.float32)).astype(jnp.bfloat16)
            term = jnp.dot(rows, jnp.concatenate([high, low], axis=1), preferred_element_type=jnp.float32)
            part = term if part is None else part + term
            at += 1
    width = part.shape[1] // 2
    part = part[:, :width] + part[:, width:]
    half = part.shape[0] // 2
    total = part[:half] + turn(part[half:])
    if targets is None:
        out_ref[...] = total
    else:
        rows = out_ref.shape[1]
        for at, c in enumerate(targets):
            out_ref[at] = total[c * rows:(c + 1) * rows]


def close(stems, kept, got, cuts, targets):
    rows, width = stems[0].shape[1], kept.shape[2]
    whole_tiles = rows % (8 * cuts) == 0
    shape = (len(targets), rows // cuts, width) if whole_tiles else (rows, width)
    out = pl.pallas_call(
        functools.partial(close_kernel, targets if whole_tiles else None),
        out_shape=jax.ShapeDtypeStruct(shape, jnp.float32),
        compiler_params=pltpu.CompilerParams(vmem_limit_bytes=24 * MIB),
        cost_estimate=pl.CostEstimate(flops=8 * rows * kept.size, bytes_accessed=MIB, transcendentals=0),
        name="close",
    )(*stems, *got, kept)
    return out if whole_tiles else out.reshape(cuts, -1)[np.array(targets)]


def on_device(stem_tensor, mid_tensors, right_tensors):
    stems = lax.axis_size("stem")
    cuts = lax.axis_size("cuts")

    def swap(x, p):
        return lax.ppermute(x, "stem", [(s, s ^ p) for s in range(stems)])

    pieces = [stem_tensor] + [swap(stem_tensor, p) for p in range(2, stems, 2)]
    kept, *sent = branch_sums(mid_tensors, right_tensors, stems)
    got = [swap(x, 1) for x in sent]
    groups = [
        [
            (2 * side + ((plane > 0) ^ group)) * cuts + 2 * plane + column
            for side in range(stems // 2 - 1, -1, -1) for plane in range(cuts // 2 - 1, -1, -1) for column in (1, 0)
        ]
        for group in (0, 1)
    ]
    targets = [at % cuts for at in groups[0]]
    spread = close(pieces, kept, got, cuts, targets)
    parts = lax.all_to_all(spread, ("stem", "cuts"), 0, 0, tiled=True, axis_index_groups=groups)
    total = jnp.sum(parts, axis=0).reshape(-1)
    return total + swap(total, 1)


def solution(mesh):
    return jax.shard_map(
        on_device,
        mesh=mesh,
        in_specs=(
            P("stem", None, None),
            P(("cuts", "stem"), None, None),
            P(None, ("cuts", "stem"), None, None),
        ),
        out_specs=P("cuts"),
        check_vma=False,
    )
```

```python
import functools

import jax
import jax.numpy as jnp
import numpy as np
from jax import lax
from jax.experimental import pallas as pl
from jax.experimental.pallas import tpu as pltpu
from jax.sharding import PartitionSpec as P

MIB = 1024 * 1024


def turn(x):
    half = x.shape[-1] // 2
    lane = lax.broadcasted_iota(jnp.int32, x.shape, x.ndim - 1)
    rolled = pltpu.roll(x, half, x.ndim - 1)
    return jnp.where(lane < half, -rolled, rolled)


def segments(blocks, depth, sizes):
    out, row = [], 0
    for piece, size in enumerate(sizes):
        end = row + size
        first = row
        while row < end:
            count = min(end, (row // depth + 1) * depth) - row
            out.append((row // depth, row % depth, piece, row - first, count))
            row += count
    return out


def piece_sizes(rows, count):
    size = -(-rows // (16 * count)) * 16
    return [min(size, rows - at) for at in range(0, rows, size)]


def branch_kernel(blocks, mid_hbm, right_hbm, kept_ref, *refs):
    *sent_refs, sums_ref, mid_ref, wide_ref, mid_sem, right_sem = refs
    pairs, _, width = mid_ref.shape
    total, _, inner, _ = right_hbm.shape
    groups = total // blocks
    half = groups // 2
    me = lax.axis_index("stem")
    chunk = pairs // mid_sem.shape[0]

    def mid_copy(n):
        at = pl.ds(n * chunk, chunk)
        return pltpu.make_async_copy(mid_hbm.at[at], mid_ref.at[at], mid_sem.at[n])

    def right_copy(q):
        p = jnp.where(q < half, 2 * q + 1, 2 * q - groups)
        source = right_hbm.at[pl.ds((me ^ p) * blocks, blocks)]
        target = wide_ref.at[pl.ds(q * blocks, blocks), :, pl.ds(0, inner)]
        return pltpu.make_async_copy(source, target, right_sem.at[q])

    for q in range(groups):
        right_copy(q).start()
    for n in range(mid_sem.shape[0]):
        mid_copy(n).start()

    def widen(q, carry):
        right_copy(q).wait()
        for b in range(blocks):
            for j in range(pairs):
                upper = wide_ref[q * blocks + b, j, :inner]
                wide_ref[q * blocks + b, j, inner:] = turn(upper.astype(jnp.float32)).astype(upper.dtype)
        return carry

    lax.fori_loop(0, groups, widen, 0)
    for n in range(mid_sem.shape[0]):
        mid_copy(n).wait()

    def multiply(h, carry):
        left = jnp.concatenate([mid_ref[j] for j in range(pairs)], axis=1)
        right = [wide_ref[h * (total // 2) + b].reshape(pairs * 2 * inner, width) for b in range(total // 2)]
        sums_ref[h] = jnp.dot(left, jnp.concatenate(right, axis=1), preferred_element_type=jnp.float32)
        return carry

    lax.fori_loop(0, 2, multiply, 0)
    sizes = [ref.shape[0] for ref in sent_refs]
    for b, row, piece, at, count in segments(total // 2, sums_ref.shape[1], sizes):
        part = sums_ref[0, row:row + count, b * width:(b + 1) * width]
        sent_refs[piece][at:at + count] = part.astype(jnp.bfloat16)
    for b in range(total // 2):
        kept_ref[b] = sums_ref[1, :, b * width:(b + 1) * width]


def branch_sums(mid, right, groups):
    pairs, depth, width = mid.shape
    total, _, inner, _ = right.shape
    sizes = piece_sizes(total // 2 * depth, 3)
    vmem = pl.BlockSpec(memory_space=pltpu.VMEM)
    hbm = pl.BlockSpec(memory_space=pltpu.HBM)
    return pl.pallas_call(
        functools.partial(branch_kernel, total // groups),
        in_specs=[hbm, hbm],
        out_specs=[vmem] * (1 + len(sizes)),
        out_shape=[
            jax.ShapeDtypeStruct((total // 2, depth, width), jnp.float32),
        ] + [jax.ShapeDtypeStruct((size, width), jnp.bfloat16) for size in sizes],
        scratch_shapes=[
            pltpu.VMEM((2, depth, total // 2 * width), jnp.float32),
            pltpu.VMEM(mid.shape, mid.dtype),
            pltpu.VMEM((total, pairs, 2 * inner, width), right.dtype),
            pltpu.SemaphoreType.DMA((4,)),
            pltpu.SemaphoreType.DMA((groups,)),
        ],
        compiler_params=pltpu.CompilerParams(vmem_limit_bytes=52 * MIB),
        cost_estimate=pl.CostEstimate(
            flops=2 * depth * pairs * width * total * width, bytes_accessed=6 * MIB, transcendentals=0
        ),
        name="branch_sums",
    )(mid, right)


def stacked(block):
    half = block.shape[-1] // 2
    return jnp.concatenate([block[:, :half], block[:, half:]], axis=0)


def fold_kernel(own_ref, kept_ref, *refs):
    *got_refs, part_ref, far_ref = refs
    blocks, depth, width = kept_ref.shape
    own = own_ref.shape[0]
    pieces = segments(blocks, depth, [ref.shape[0] for ref in got_refs])
    part = None
    for b in range(blocks):
        got = [got_refs[piece][at:at + count] for block, _, piece, at, count in pieces if block == b]
        sums = kept_ref[b] + jnp.concatenate(got, axis=0).astype(jnp.float32)
        high = sums.astype(jnp.bfloat16)
        low = (sums - high.astype(jnp.float32)).astype(jnp.bfloat16)
        both = jnp.concatenate([high, low], axis=1)
        if b < own:
            term = jnp.dot(stacked(own_ref[b]), both, preferred_element_type=jnp.float32)
            part = term if part is None else part + term
        else:
            far_ref[b - own] = both
    part_ref[...] = part


def fold(own, kept, got):
    count, rows, _ = own.shape
    blocks, depth, width = kept.shape
    return pl.pallas_call(
        fold_kernel,
        out_shape=[
            jax.ShapeDtypeStruct((2 * rows, 2 * width), jnp.float32),
            jax.ShapeDtypeStruct((blocks - count, depth, 2 * width), jnp.bfloat16),
        ],
        compiler_params=pltpu.CompilerParams(vmem_limit_bytes=24 * MIB),
        cost_estimate=pl.CostEstimate(flops=8 * rows * kept.size, bytes_accessed=MIB, transcendentals=0),
        name="fold",
    )(own, kept, *got)


def close_kernel(targets, *refs):
    *stem_refs, part_ref, far_ref, out_ref = refs
    part = part_ref[...]
    at = 0
    for ref in stem_refs:
        for b in range(ref.shape[0]):
            part += jnp.dot(stacked(ref[b]), far_ref[at], preferred_element_type=jnp.float32)
            at += 1
    width = part.shape[1] // 2
    part = part[:, :width] + part[:, width:]
    half = part.shape[0] // 2
    total = part[:half] + turn(part[half:])
    if targets is None:
        out_ref[...] = total
    else:
        rows = out_ref.shape[1]
        for at, c in enumerate(targets):
            out_ref[at] = total[c * rows:(c + 1) * rows]


def close(stems, part, far, cuts, targets):
    rows, width = part.shape[0] // 2, part.shape[1] // 2
    whole_tiles = rows % (8 * cuts) == 0
    shape = (len(targets), rows // cuts, width) if whole_tiles else (rows, width)
    out = pl.pallas_call(
        functools.partial(close_kernel, targets if whole_tiles else None),
        out_shape=jax.ShapeDtypeStruct(shape, jnp.float32),
        compiler_params=pltpu.CompilerParams(vmem_limit_bytes=24 * MIB),
        cost_estimate=pl.CostEstimate(flops=4 * rows * far.size, bytes_accessed=MIB, transcendentals=0),
        name="close",
    )(*stems, part, far)
    return out if whole_tiles else out.reshape(cuts, -1)[np.array(targets)]


def on_device(stem_tensor, mid_tensors, right_tensors):
    stems = lax.axis_size("stem")
    cuts = lax.axis_size("cuts")

    def swap(x, p):
        return lax.ppermute(x, "stem", [(s, s ^ p) for s in range(stems)])

    stems_far = [swap(stem_tensor, p) for p in range(2, stems, 2)]
    kept, *sent = branch_sums(mid_tensors, right_tensors, stems)
    got = [swap(x, 1) for x in sent]
    groups = [
        [
            (2 * side + (plane + group) % 2) * cuts + 2 * plane + column
            for side in range(stems // 2 - 1, -1, -1) for plane in range(cuts // 2 - 1, -1, -1) for column in (1, 0)
        ]
        for group in (0, 1)
    ]
    targets = [at % cuts for at in groups[0]]
    part, far = fold(stem_tensor, kept, got)
    spread = close(stems_far, part, far, cuts, targets)
    parts = lax.all_to_all(spread, ("stem", "cuts"), 0, 0, tiled=True, axis_index_groups=groups)
    total = jnp.sum(parts, axis=0).reshape(-1)
    return total + swap(total, 1)


def solution(mesh):
    return jax.shard_map(
        on_device,
        mesh=mesh,
        in_specs=(
            P("stem", None, None),
            P(("cuts", "stem"), None, None),
            P(None, ("cuts", "stem"), None, None),
        ),
        out_specs=P("cuts"),
        check_vma=False,
    )
```

```python
import functools

import jax
import jax.numpy as jnp
import numpy as np
from jax import lax
from jax.experimental import pallas as pl
from jax.experimental.pallas import tpu as pltpu
from jax.sharding import PartitionSpec as P

MIB = 1024 * 1024


def turn(x):
    half = x.shape[-1] // 2
    lane = lax.broadcasted_iota(jnp.int32, x.shape, x.ndim - 1)
    rolled = pltpu.roll(x, half, x.ndim - 1)
    return jnp.where(lane < half, -rolled, rolled)


def segments(blocks, depth, sizes):
    out, row = [], 0
    for piece, size in enumerate(sizes):
        end = row + size
        first = row
        while row < end:
            count = min(end, (row // depth + 1) * depth) - row
            out.append((row // depth, row % depth, piece, row - first, count))
            row += count
    return out


def piece_sizes(rows, count):
    size = -(-rows // (16 * count)) * 16
    return [min(size, rows - at) for at in range(0, rows, size)]


def branch_kernel(blocks, mid_hbm, right_hbm, kept_ref, *refs):
    *sent_refs, sums_ref, mid_ref, wide_ref, mid_sem, right_sem = refs
    pairs, _, width = mid_ref.shape
    total, _, inner, _ = right_hbm.shape
    groups = total // blocks
    half = groups // 2
    me = lax.axis_index("stem")
    chunk = pairs // mid_sem.shape[0]

    def mid_copy(n):
        at = pl.ds(n * chunk, chunk)
        return pltpu.make_async_copy(mid_hbm.at[at], mid_ref.at[at], mid_sem.at[n])

    def right_copy(q):
        stays = jnp.where(q < half, 0, 1)
        side = (me // 2) ^ (me % 2) ^ stays ^ 1
        source = right_hbm.at[pl.ds((2 * side + q % 2) * blocks, blocks)]
        target = wide_ref.at[pl.ds(q * blocks, blocks), :, pl.ds(0, inner)]
        return pltpu.make_async_copy(source, target, right_sem.at[q])

    for q in range(groups):
        right_copy(q).start()
    for n in range(mid_sem.shape[0]):
        mid_copy(n).start()

    def widen(q, carry):
        right_copy(q).wait()
        for b in range(blocks):
            for j in range(pairs):
                upper = wide_ref[q * blocks + b, j, :inner]
                wide_ref[q * blocks + b, j, inner:] = turn(upper.astype(jnp.float32)).astype(upper.dtype)
        return carry

    lax.fori_loop(0, groups, widen, 0)
    for n in range(mid_sem.shape[0]):
        mid_copy(n).wait()

    def multiply(h, carry):
        left = jnp.concatenate([mid_ref[j] for j in range(pairs)], axis=1)
        right = [wide_ref[h * (total // 2) + b].reshape(pairs * 2 * inner, width) for b in range(total // 2)]
        sums_ref[h] = jnp.dot(left, jnp.concatenate(right, axis=1), preferred_element_type=jnp.float32)
        return carry

    lax.fori_loop(0, 2, multiply, 0)
    sizes = [ref.shape[0] for ref in sent_refs]
    for b, row, piece, at, count in segments(total // 2, sums_ref.shape[1], sizes):
        part = sums_ref[0, row:row + count, b * width:(b + 1) * width]
        sent_refs[piece][at:at + count] = part.astype(jnp.bfloat16)
    for b in range(total // 2):
        kept_ref[b] = sums_ref[1, :, b * width:(b + 1) * width]


def branch_sums(mid, right, groups):
    pairs, depth, width = mid.shape
    total, _, inner, _ = right.shape
    sizes = piece_sizes(total // 2 * depth, 3)
    vmem = pl.BlockSpec(memory_space=pltpu.VMEM)
    hbm = pl.BlockSpec(memory_space=pltpu.HBM)
    return pl.pallas_call(
        functools.partial(branch_kernel, total // groups),
        in_specs=[hbm, hbm],
        out_specs=[vmem] * (1 + len(sizes)),
        out_shape=[
            jax.ShapeDtypeStruct((total // 2, depth, width), jnp.float32),
        ] + [jax.ShapeDtypeStruct((size, width), jnp.bfloat16) for size in sizes],
        scratch_shapes=[
            pltpu.VMEM((2, depth, total // 2 * width), jnp.float32),
            pltpu.VMEM(mid.shape, mid.dtype),
            pltpu.VMEM((total, pairs, 2 * inner, width), right.dtype),
            pltpu.SemaphoreType.DMA((4,)),
            pltpu.SemaphoreType.DMA((groups,)),
        ],
        compiler_params=pltpu.CompilerParams(vmem_limit_bytes=52 * MIB),
        cost_estimate=pl.CostEstimate(
            flops=2 * depth * pairs * width * total * width, bytes_accessed=6 * MIB, transcendentals=0
        ),
        name="branch_sums",
    )(mid, right)


def close_kernel(targets, *refs):
    own_ref, cross_ref, cycle_ref, *got_refs, kept_ref, out_ref = refs
    first_core = lax.axis_index("stem") % 2 == 0
    pieces = segments(kept_ref.shape[0], kept_ref.shape[1], [ref.shape[0] for ref in got_refs])
    part = None
    at = 0
    for when_first, when_second in ((own_ref, cycle_ref), (cycle_ref, cross_ref)):
        for b in range(own_ref.shape[0]):
            block = jnp.where(first_core, when_first[b], when_second[b])
            half = block.shape[-1] // 2
            rows = jnp.concatenate([block[:, :half], block[:, half:]], axis=0)
            got = [got_refs[piece][row:row + count] for block_at, _, piece, row, count in pieces if block_at == at]
            sums = kept_ref[at] + jnp.concatenate(got, axis=0).astype(jnp.float32)
            high = sums.astype(jnp.bfloat16)
            low = (sums - high.astype(jnp.float32)).astype(jnp.bfloat16)
            term = jnp.dot(rows, jnp.concatenate([high, low], axis=1), preferred_element_type=jnp.float32)
            part = term if part is None else part + term
            at += 1
    width = part.shape[1] // 2
    part = part[:, :width] + part[:, width:]
    half = part.shape[0] // 2
    total = part[:half] + turn(part[half:])
    if targets is None:
        out_ref[...] = total
    else:
        rows = out_ref.shape[1]
        for at, c in enumerate(targets):
            out_ref[at] = total[c * rows:(c + 1) * rows]


def close(stems, kept, got, cuts, targets):
    rows, width = stems[0].shape[1], kept.shape[2]
    whole_tiles = rows % (8 * cuts) == 0
    shape = (len(targets), rows // cuts, width) if whole_tiles else (rows, width)
    out = pl.pallas_call(
        functools.partial(close_kernel, targets if whole_tiles else None),
        out_shape=jax.ShapeDtypeStruct(shape, jnp.float32),
        compiler_params=pltpu.CompilerParams(vmem_limit_bytes=24 * MIB),
        cost_estimate=pl.CostEstimate(flops=8 * rows * kept.size, bytes_accessed=MIB, transcendentals=0),
        name="close",
    )(*stems, *got, kept)
    return out if whole_tiles else out.reshape(cuts, -1)[np.array(targets)]


def on_device(stem_tensor, mid_tensors, right_tensors):
    stems = lax.axis_size("stem")
    cuts = lax.axis_size("cuts")

    def swap(x, p):
        return lax.ppermute(x, "stem", [(s, s ^ p) for s in range(stems)])

    def route(target):
        pairs = []
        for at in np.ndindex(cuts, 2, 2):
            cut, side, core = target(*at)
            pairs.append((at[0] * 4 + at[1] * 2 + at[2], cut * 4 + side * 2 + core))
        return lax.ppermute(stem_tensor, ("cuts", "stem"), pairs)

    assert stems == 4
    cross = route(lambda cut, side, core: (cut, 1 - side, 1) if core else (cut ^ 1, side, 0))
    cycle = route(lambda cut, side, core: (cut, side, 0) if core else (cut, 1 - side, 1))
    pieces = [stem_tensor, cross, cycle]
    kept, *sent = branch_sums(mid_tensors, right_tensors, stems)
    got = [swap(x, 1) for x in sent]
    groups = [
        [
            (2 * side + (plane + group) % 2) * cuts + 2 * plane + column
            for side in range(stems // 2 - 1, -1, -1) for plane in range(cuts // 2 - 1, -1, -1) for column in (1, 0)
        ]
        for group in (0, 1)
    ]
    targets = [at % cuts for at in groups[0]]
    spread = close(pieces, kept, got, cuts, targets)
    parts = lax.all_to_all(spread, ("stem", "cuts"), 0, 0, tiled=True, axis_index_groups=groups)
    total = jnp.sum(parts, axis=0).reshape(-1)
    return total + swap(total, 1)


def solution(mesh):
    return jax.shard_map(
        on_device,
        mesh=mesh,
        in_specs=(
            P("stem", None, None),
            P(("cuts", "stem"), None, None),
            P(None, ("cuts", "stem"), None, None),
        ),
        out_specs=P("cuts"),
        check_vma=False,
    )
```

```python
import functools

import jax
import jax.numpy as jnp
import numpy as np
from jax import lax
from jax.experimental import pallas as pl
from jax.experimental.pallas import tpu as pltpu
from jax.sharding import PartitionSpec as P

MIB = 1024 * 1024
LEAVE_MIB = 48


def turn(x):
    half = x.shape[-1] // 2
    lane = lax.broadcasted_iota(jnp.int32, x.shape, x.ndim - 1)
    rolled = pltpu.roll(x, half, x.ndim - 1)
    return jnp.where(lane < half, -rolled, rolled)


def segments(blocks, depth, sizes):
    out, row = [], 0
    for piece, size in enumerate(sizes):
        end = row + size
        first = row
        while row < end:
            count = min(end, (row // depth + 1) * depth) - row
            out.append((row // depth, row % depth, piece, row - first, count))
            row += count
    return out


def piece_sizes(rows, count):
    size = -(-rows // (16 * count)) * 16
    return [min(size, rows - at) for at in range(0, rows, size)]


def product(mid_ref, wide_ref):
    pairs = mid_ref.shape[0]
    left = jnp.concatenate([mid_ref[j] for j in range(pairs)], axis=1)
    blocks, _, rows, width = wide_ref.shape
    right = [wide_ref[b].reshape(pairs * rows, width) for b in range(blocks)]
    return jnp.dot(left, jnp.concatenate(right, axis=1), preferred_element_type=jnp.float32)


def leave_kernel(blocks, mid_hbm, right_hbm, mid_ref, stay_ref, *refs):
    *sent_refs, leave_ref, mid_sem, right_sem = refs
    pairs, depth, width = mid_ref.shape
    total, _, inner, _ = right_hbm.shape
    groups = total // blocks
    half = groups // 2
    me = lax.axis_index("stem")
    chunk = pairs // mid_sem.shape[0]

    def mid_copy(n):
        at = pl.ds(n * chunk, chunk)
        return pltpu.make_async_copy(mid_hbm.at[at], mid_ref.at[at], mid_sem.at[n])

    def right_copy(q, wide_ref, stays):
        side = (me // 2) ^ (me % 2) ^ stays ^ 1
        source = right_hbm.at[pl.ds((2 * side + q) * blocks, blocks)]
        target = wide_ref.at[pl.ds(q * blocks, blocks), :, pl.ds(0, inner)]
        return pltpu.make_async_copy(source, target, right_sem.at[stays * half + q])

    for q in range(half):
        right_copy(q, leave_ref, 0).start()
    for n in range(mid_sem.shape[0]):
        mid_copy(n).start()
    for q in range(half):
        right_copy(q, stay_ref, 1).start()

    def widen(wide_ref, stays):
        def step(q, carry):
            right_copy(q, wide_ref, stays).wait()
            for b in range(blocks):
                for j in range(pairs):
                    upper = wide_ref[q * blocks + b, j, :inner]
                    wide_ref[q * blocks + b, j, inner:] = turn(upper.astype(jnp.float32)).astype(upper.dtype)
            return carry

        lax.fori_loop(0, half, step, 0)

    widen(leave_ref, 0)
    for n in range(mid_sem.shape[0]):
        mid_copy(n).wait()
    sums = product(mid_ref, leave_ref)
    sizes = [ref.shape[0] for ref in sent_refs]
    for b, row, piece, at, count in segments(total // 2, depth, sizes):
        part = sums[row:row + count, b * width:(b + 1) * width]
        sent_refs[piece][at:at + count] = part.astype(jnp.bfloat16)
    widen(stay_ref, 1)


def stay_kernel(mid_ref, wide_ref, kept_ref):
    sums = product(mid_ref, wide_ref)
    width = kept_ref.shape[2]
    for b in range(kept_ref.shape[0]):
        kept_ref[b] = sums[:, b * width:(b + 1) * width]


def branch_sums(mid, right, groups):
    pairs, depth, width = mid.shape
    total, _, inner, _ = right.shape
    half = total // 2
    sizes = piece_sizes(half * depth, 3)
    wide = (half, pairs, 2 * inner, width)
    vmem = pl.BlockSpec(memory_space=pltpu.VMEM)
    hbm = pl.BlockSpec(memory_space=pltpu.HBM)
    cost = pl.CostEstimate(
        flops=depth * pairs * width * total * width, bytes_accessed=4 * MIB, transcendentals=0
    )
    mid_here, wide_here, *sent = pl.pallas_call(
        functools.partial(leave_kernel, total // groups),
        in_specs=[hbm, hbm],
        out_specs=[vmem] * (2 + len(sizes)),
        out_shape=[
            jax.ShapeDtypeStruct(mid.shape, mid.dtype),
            jax.ShapeDtypeStruct(wide, right.dtype),
        ] + [jax.ShapeDtypeStruct((size, width), jnp.bfloat16) for size in sizes],
        scratch_shapes=[
            pltpu.VMEM(wide, right.dtype),
            pltpu.SemaphoreType.DMA((4,)),
            pltpu.SemaphoreType.DMA((groups,)),
        ],
        compiler_params=pltpu.CompilerParams(vmem_limit_bytes=LEAVE_MIB * MIB),
        cost_estimate=cost,
        name="leave",
    )(mid, right)
    kept = pl.pallas_call(
        stay_kernel,
        out_shape=jax.ShapeDtypeStruct((half, depth, width), jnp.float32),
        compiler_params=pltpu.CompilerParams(vmem_limit_bytes=24 * MIB),
        cost_estimate=cost,
        name="stay",
    )(mid_here, wide_here)
    return kept, *sent


def close_kernel(targets, *refs):
    own_ref, cross_ref, cycle_ref, *got_refs, kept_ref, out_ref = refs
    first_core = lax.axis_index("stem") % 2 == 0
    pieces = segments(kept_ref.shape[0], kept_ref.shape[1], [ref.shape[0] for ref in got_refs])
    part = None
    at = 0
    for when_first, when_second in ((own_ref, cycle_ref), (cycle_ref, cross_ref)):
        for b in range(own_ref.shape[0]):
            block = jnp.where(first_core, when_first[b], when_second[b])
            half = block.shape[-1] // 2
            rows = jnp.concatenate([block[:, :half], block[:, half:]], axis=0)
            got = [got_refs[piece][row:row + count] for block_at, _, piece, row, count in pieces if block_at == at]
            sums = kept_ref[at] + jnp.concatenate(got, axis=0).astype(jnp.float32)
            high = sums.astype(jnp.bfloat16)
            low = (sums - high.astype(jnp.float32)).astype(jnp.bfloat16)
            term = jnp.dot(rows, jnp.concatenate([high, low], axis=1), preferred_element_type=jnp.float32)
            part = term if part is None else part + term
            at += 1
    width = part.shape[1] // 2
    part = part[:, :width] + part[:, width:]
    half = part.shape[0] // 2
    total = part[:half] + turn(part[half:])
    if targets is None:
        out_ref[...] = total
    else:
        rows = out_ref.shape[1]
        for at, c in enumerate(targets):
            out_ref[at] = total[c * rows:(c + 1) * rows]


def close(stems, kept, got, cuts, targets):
    rows, width = stems[0].shape[1], kept.shape[2]
    whole_tiles = rows % (8 * cuts) == 0
    shape = (len(targets), rows // cuts, width) if whole_tiles else (rows, width)
    out = pl.pallas_call(
        functools.partial(close_kernel, targets if whole_tiles else None),
        out_shape=jax.ShapeDtypeStruct(shape, jnp.float32),
        compiler_params=pltpu.CompilerParams(vmem_limit_bytes=24 * MIB),
        cost_estimate=pl.CostEstimate(flops=8 * rows * kept.size, bytes_accessed=MIB, transcendentals=0),
        name="close",
    )(*stems, *got, kept)
    return out if whole_tiles else out.reshape(cuts, -1)[np.array(targets)]


def on_device(stem_tensor, mid_tensors, right_tensors):
    stems = lax.axis_size("stem")
    cuts = lax.axis_size("cuts")

    def swap(x, p):
        return lax.ppermute(x, "stem", [(s, s ^ p) for s in range(stems)])

    def route(target):
        pairs = []
        for at in np.ndindex(cuts, 2, 2):
            cut, side, core = target(*at)
            pairs.append((at[0] * 4 + at[1] * 2 + at[2], cut * 4 + side * 2 + core))
        return lax.ppermute(stem_tensor, ("cuts", "stem"), pairs)

    assert stems == 4
    cross = route(lambda cut, side, core: (cut, 1 - side, 1) if core else (cut ^ 1, side, 0))
    cycle = route(lambda cut, side, core: (cut, side, 0) if core else (cut, 1 - side, 1))
    pieces = [stem_tensor, cross, cycle]
    kept, *sent = branch_sums(mid_tensors, right_tensors, stems)
    got = [swap(x, 1) for x in sent]
    groups = [
        [
            (2 * side + (plane + group) % 2) * cuts + 2 * plane + column
            for side in range(stems // 2 - 1, -1, -1) for plane in range(cuts // 2 - 1, -1, -1) for column in (1, 0)
        ]
        for group in (0, 1)
    ]
    targets = [at % cuts for at in groups[0]]
    spread = close(pieces, kept, got, cuts, targets)
    parts = lax.all_to_all(spread, ("stem", "cuts"), 0, 0, tiled=True, axis_index_groups=groups)
    total = jnp.sum(parts, axis=0).reshape(-1)
    return total + swap(total, 1)


def solution(mesh):
    return jax.shard_map(
        on_device,
        mesh=mesh,
        in_specs=(
            P("stem", None, None),
            P(("cuts", "stem"), None, None),
            P(None, ("cuts", "stem"), None, None),
        ),
        out_specs=P("cuts"),
        check_vma=False,
    )
```

```python
import functools

import jax
import jax.numpy as jnp
import numpy as np
from jax import lax
from jax.experimental import pallas as pl
from jax.experimental.pallas import tpu as pltpu
from jax.sharding import PartitionSpec as P

MIB = 1024 * 1024
LEAVE_MIB = 48


def turn(x):
    half = x.shape[-1] // 2
    lane = lax.broadcasted_iota(jnp.int32, x.shape, x.ndim - 1)
    rolled = pltpu.roll(x, half, x.ndim - 1)
    return jnp.where(lane < half, -rolled, rolled)


def segments(blocks, depth, sizes):
    out, row = [], 0
    for piece, size in enumerate(sizes):
        end = row + size
        first = row
        while row < end:
            count = min(end, (row // depth + 1) * depth) - row
            out.append((row // depth, row % depth, piece, row - first, count))
            row += count
    return out


def piece_sizes(rows, count):
    size = -(-rows // (16 * count)) * 16
    return [min(size, rows - at) for at in range(0, rows, size)]


def product(mid_ref, wide_ref):
    pairs = mid_ref.shape[0]
    left = jnp.concatenate([mid_ref[j] for j in range(pairs)], axis=1)
    blocks, _, rows, width = wide_ref.shape
    right = [wide_ref[b].reshape(pairs * rows, width) for b in range(blocks)]
    return jnp.dot(left, jnp.concatenate(right, axis=1), preferred_element_type=jnp.float32)


def leave_kernel(blocks, mid_hbm, right_hbm, mid_ref, stay_ref, *refs):
    *sent_refs, leave_ref, mid_sem, right_sem = refs
    pairs, depth, width = mid_ref.shape
    total, _, inner, _ = right_hbm.shape
    groups = total // blocks
    half = groups // 2
    me = lax.axis_index("stem")
    chunk = pairs // mid_sem.shape[0]

    def mid_copy(n):
        at = pl.ds(n * chunk, chunk)
        return pltpu.make_async_copy(mid_hbm.at[at], mid_ref.at[at], mid_sem.at[n])

    def right_copy(q, wide_ref, stays):
        side = (me // 2) ^ (me % 2) ^ stays ^ 1
        source = right_hbm.at[pl.ds((2 * side + q) * blocks, blocks)]
        target = wide_ref.at[pl.ds(q * blocks, blocks), :, pl.ds(0, inner)]
        return pltpu.make_async_copy(source, target, right_sem.at[stays * half + q])

    for q in range(half):
        right_copy(q, leave_ref, 0).start()
    for n in range(mid_sem.shape[0]):
        mid_copy(n).start()
    for q in range(half):
        right_copy(q, stay_ref, 1).start()

    def widen(wide_ref, stays):
        def step(q, carry):
            right_copy(q, wide_ref, stays).wait()
            for b in range(blocks):
                for j in range(pairs):
                    upper = wide_ref[q * blocks + b, j, :inner]
                    wide_ref[q * blocks + b, j, inner:] = turn(upper.astype(jnp.float32)).astype(upper.dtype)
            return carry

        lax.fori_loop(0, half, step, 0)

    widen(leave_ref, 0)
    for n in range(mid_sem.shape[0]):
        mid_copy(n).wait()
    sums = product(mid_ref, leave_ref)
    sizes = [ref.shape[0] for ref in sent_refs]
    for b, row, piece, at, count in segments(total // 2, depth, sizes):
        part = sums[row:row + count, b * width:(b + 1) * width]
        sent_refs[piece][at:at + count] = part.astype(jnp.bfloat16)
    widen(stay_ref, 1)


def stay_kernel(mid_ref, wide_ref, kept_ref):
    sums = product(mid_ref, wide_ref)
    width = kept_ref.shape[2]
    for b in range(kept_ref.shape[0]):
        kept_ref[b] = sums[:, b * width:(b + 1) * width]


def branch_sums(mid, right, groups):
    pairs, depth, width = mid.shape
    total, _, inner, _ = right.shape
    half = total // 2
    sizes = piece_sizes(half * depth, 3)
    wide = (half, pairs, 2 * inner, width)
    vmem = pl.BlockSpec(memory_space=pltpu.VMEM)
    hbm = pl.BlockSpec(memory_space=pltpu.HBM)
    cost = pl.CostEstimate(
        flops=depth * pairs * width * total * width, bytes_accessed=4 * MIB, transcendentals=0
    )
    mid_here, wide_here, *sent = pl.pallas_call(
        functools.partial(leave_kernel, total // groups),
        in_specs=[hbm, hbm],
        out_specs=[vmem] * (2 + len(sizes)),
        out_shape=[
            jax.ShapeDtypeStruct(mid.shape, mid.dtype),
            jax.ShapeDtypeStruct(wide, right.dtype),
        ] + [jax.ShapeDtypeStruct((size, width), jnp.bfloat16) for size in sizes],
        scratch_shapes=[
            pltpu.VMEM(wide, right.dtype),
            pltpu.SemaphoreType.DMA((4,)),
            pltpu.SemaphoreType.DMA((groups,)),
        ],
        compiler_params=pltpu.CompilerParams(vmem_limit_bytes=LEAVE_MIB * MIB),
        cost_estimate=cost,
        name="leave",
    )(mid, right)
    kept = pl.pallas_call(
        stay_kernel,
        out_shape=jax.ShapeDtypeStruct((half, depth, width), jnp.float32),
        compiler_params=pltpu.CompilerParams(vmem_limit_bytes=24 * MIB),
        cost_estimate=cost,
        name="stay",
    )(mid_here, wide_here)
    return kept, *sent


def close_kernel(targets, *refs):
    own_ref, cross_ref, cycle_ref, *got_refs, kept_ref, out_ref = refs
    first_core = lax.axis_index("stem") % 2 == 0
    pieces = segments(kept_ref.shape[0], kept_ref.shape[1], [ref.shape[0] for ref in got_refs])
    part = None
    at = 0
    for when_first, when_second in ((own_ref, cycle_ref), (cycle_ref, cross_ref)):
        for b in range(own_ref.shape[0]):
            block = jnp.where(first_core, when_first[b], when_second[b])
            half = block.shape[-1] // 2
            rows = jnp.concatenate([block[:, :half], block[:, half:]], axis=0)
            got = [got_refs[piece][row:row + count] for block_at, _, piece, row, count in pieces if block_at == at]
            sums = kept_ref[at] + jnp.concatenate(got, axis=0).astype(jnp.float32)
            high = sums.astype(jnp.bfloat16)
            low = (sums - high.astype(jnp.float32)).astype(jnp.bfloat16)
            term = jnp.dot(rows, jnp.concatenate([high, low], axis=1), preferred_element_type=jnp.float32)
            part = term if part is None else part + term
            at += 1
    width = part.shape[1] // 2
    part = part[:, :width] + part[:, width:]
    half = part.shape[0] // 2
    total = part[:half] + turn(part[half:])
    if targets is None:
        out_ref[...] = total
    else:
        rows = out_ref.shape[1]
        for at, c in enumerate(targets):
            out_ref[at] = total[c * rows:(c + 1) * rows]


def close(stems, kept, got, cuts, targets):
    rows, width = stems[0].shape[1], kept.shape[2]
    whole_tiles = rows % (8 * cuts) == 0
    shape = (len(targets), rows // cuts, width) if whole_tiles else (rows, width)
    out = pl.pallas_call(
        functools.partial(close_kernel, targets if whole_tiles else None),
        out_shape=jax.ShapeDtypeStruct(shape, jnp.float32),
        compiler_params=pltpu.CompilerParams(vmem_limit_bytes=24 * MIB),
        cost_estimate=pl.CostEstimate(flops=8 * rows * kept.size, bytes_accessed=MIB, transcendentals=0),
        name="close",
    )(*stems, *got, kept)
    return out if whole_tiles else out.reshape(cuts, -1)[np.array(targets)]


def on_device(stem_tensor, mid_tensors, right_tensors):
    stems = lax.axis_size("stem")
    cuts = lax.axis_size("cuts")

    def swap(x, p):
        return lax.ppermute(x, "stem", [(s, s ^ p) for s in range(stems)])

    def route(target):
        pairs = []
        for at in np.ndindex(cuts, 2, 2):
            cut, side, core = target(*at)
            pairs.append((at[0] * 4 + at[1] * 2 + at[2], cut * 4 + side * 2 + core))
        return lax.ppermute(stem_tensor, ("cuts", "stem"), pairs)

    assert stems == 4
    cross = route(lambda cut, side, core: (cut, 1 - side, 1) if core else (cut ^ 1, side, 0))
    cycle = route(lambda cut, side, core: (cut, side, 0) if core else (cut, 1 - side, 1))
    pieces = [stem_tensor, cross, cycle]
    kept, *sent = branch_sums(mid_tensors, right_tensors, stems)
    got = [swap(x, 1) for x in sent]
    groups = [
        [
            (2 * side + group) * cuts + 2 * plane + column
            for side in range(stems // 2 - 1, -1, -1) for plane in range(cuts // 2 - 1, -1, -1) for column in (1, 0)
        ]
        for group in (0, 1)
    ]
    targets = [at % cuts for at in groups[0]]
    spread = close(pieces, kept, got, cuts, targets)
    parts = lax.all_to_all(spread, ("stem", "cuts"), 0, 0, tiled=True, axis_index_groups=groups)
    total = jnp.sum(parts, axis=0).reshape(-1)
    return total + swap(total, 1)


def solution(mesh):
    return jax.shard_map(
        on_device,
        mesh=mesh,
        in_specs=(
            P("stem", None, None),
            P(("cuts", "stem"), None, None),
            P(None, ("cuts", "stem"), None, None),
        ),
        out_specs=P("cuts"),
        check_vma=False,
    )
```

```python
import functools

import jax
import jax.numpy as jnp
import numpy as np
from jax import lax
from jax.experimental import pallas as pl
from jax.experimental.pallas import tpu as pltpu
from jax.sharding import PartitionSpec as P

MIB = 1024 * 1024
LEAVE_MIB = 48


def turn(x):
    half = x.shape[-1] // 2
    lane = lax.broadcasted_iota(jnp.int32, x.shape, x.ndim - 1)
    rolled = pltpu.roll(x, half, x.ndim - 1)
    return jnp.where(lane < half, -rolled, rolled)


def segments(blocks, depth, sizes):
    out, row = [], 0
    for piece, size in enumerate(sizes):
        end = row + size
        first = row
        while row < end:
            count = min(end, (row // depth + 1) * depth) - row
            out.append((row // depth, row % depth, piece, row - first, count))
            row += count
    return out


def piece_sizes(rows, count):
    size = -(-rows // (16 * count)) * 16
    return [min(size, rows - at) for at in range(0, rows, size)]


def product(mid_ref, wide_ref):
    pairs = mid_ref.shape[0]
    left = jnp.concatenate([mid_ref[j] for j in range(pairs)], axis=1)
    blocks, _, rows, width = wide_ref.shape
    right = [wide_ref[b].reshape(pairs * rows, width) for b in range(blocks)]
    return jnp.dot(left, jnp.concatenate(right, axis=1), preferred_element_type=jnp.float32)


def leave_kernel(blocks, mid_hbm, right_hbm, mid_ref, stay_ref, *refs):
    *sent_refs, leave_ref, mid_sem, right_sem = refs
    pairs, depth, width = mid_ref.shape
    total, _, inner, _ = right_hbm.shape
    groups = total // blocks
    half = groups // 2
    me = lax.axis_index("stem")
    chunk = pairs // mid_sem.shape[0]

    def mid_copy(n):
        at = pl.ds(n * chunk, chunk)
        return pltpu.make_async_copy(mid_hbm.at[at], mid_ref.at[at], mid_sem.at[n])

    def right_copy(q, wide_ref, stays):
        side = (me // 2) ^ (me % 2) ^ stays ^ 1
        source = right_hbm.at[pl.ds((2 * side + q) * blocks, blocks)]
        target = wide_ref.at[pl.ds(q * blocks, blocks), :, pl.ds(0, inner)]
        return pltpu.make_async_copy(source, target, right_sem.at[stays * half + q])

    for q in range(half):
        right_copy(q, leave_ref, 0).start()
    for n in range(mid_sem.shape[0]):
        mid_copy(n).start()
    for q in range(half):
        right_copy(q, stay_ref, 1).start()

    def widen(wide_ref, stays):
        def step(q, carry):
            right_copy(q, wide_ref, stays).wait()
            for b in range(blocks):
                for j in range(pairs):
                    upper = wide_ref[q * blocks + b, j, :inner]
                    wide_ref[q * blocks + b, j, inner:] = turn(upper.astype(jnp.float32)).astype(upper.dtype)
            return carry

        lax.fori_loop(0, half, step, 0)

    widen(leave_ref, 0)
    for n in range(mid_sem.shape[0]):
        mid_copy(n).wait()
    sums = product(mid_ref, leave_ref)
    sizes = [ref.shape[0] for ref in sent_refs]
    for b, row, piece, at, count in segments(total // 2, depth, sizes):
        part = sums[row:row + count, b * width:(b + 1) * width]
        sent_refs[piece][at:at + count] = part.astype(jnp.bfloat16)
    widen(stay_ref, 1)


def stay_kernel(mid_ref, wide_ref, kept_ref):
    sums = product(mid_ref, wide_ref)
    width = kept_ref.shape[2]
    for b in range(kept_ref.shape[0]):
        kept_ref[b] = sums[:, b * width:(b + 1) * width]


def branch_sums(mid, right, groups):
    pairs, depth, width = mid.shape
    total, _, inner, _ = right.shape
    half = total // 2
    sizes = piece_sizes(half * depth, 3)
    wide = (half, pairs, 2 * inner, width)
    vmem = pl.BlockSpec(memory_space=pltpu.VMEM)
    hbm = pl.BlockSpec(memory_space=pltpu.HBM)
    cost = pl.CostEstimate(
        flops=depth * pairs * width * total * width, bytes_accessed=4 * MIB, transcendentals=0
    )
    mid_here, wide_here, *sent = pl.pallas_call(
        functools.partial(leave_kernel, total // groups),
        in_specs=[hbm, hbm],
        out_specs=[vmem] * (2 + len(sizes)),
        out_shape=[
            jax.ShapeDtypeStruct(mid.shape, mid.dtype),
            jax.ShapeDtypeStruct(wide, right.dtype),
        ] + [jax.ShapeDtypeStruct((size, width), jnp.bfloat16) for size in sizes],
        scratch_shapes=[
            pltpu.VMEM(wide, right.dtype),
            pltpu.SemaphoreType.DMA((4,)),
            pltpu.SemaphoreType.DMA((groups,)),
        ],
        compiler_params=pltpu.CompilerParams(vmem_limit_bytes=LEAVE_MIB * MIB),
        cost_estimate=cost,
        name="leave",
    )(mid, right)
    kept = pl.pallas_call(
        stay_kernel,
        out_shape=jax.ShapeDtypeStruct((half, depth, width), jnp.float32),
        compiler_params=pltpu.CompilerParams(vmem_limit_bytes=24 * MIB),
        cost_estimate=cost,
        name="stay",
    )(mid_here, wide_here)
    return kept, *sent


def close_kernel(targets, *refs):
    own_ref, cross_ref, cycle_ref, *got_refs, kept_ref, out_ref = refs
    first_core = lax.axis_index("stem") % 2 == 0
    pieces = segments(kept_ref.shape[0], kept_ref.shape[1], [ref.shape[0] for ref in got_refs])
    part = None
    at = 0
    for when_first, when_second in ((own_ref, cycle_ref), (cycle_ref, cross_ref)):
        for b in range(own_ref.shape[0]):
            block = jnp.where(first_core, when_first[b], when_second[b])
            half = block.shape[-1] // 2
            rows = jnp.concatenate([block[:, :half], block[:, half:]], axis=0)
            got = [got_refs[piece][row:row + count] for block_at, _, piece, row, count in pieces if block_at == at]
            sums = kept_ref[at] + jnp.concatenate(got, axis=0).astype(jnp.float32)
            high = sums.astype(jnp.bfloat16)
            low = (sums - high.astype(jnp.float32)).astype(jnp.bfloat16)
            term = jnp.dot(rows, jnp.concatenate([high, low], axis=1), preferred_element_type=jnp.float32)
            part = term if part is None else part + term
            at += 1
    width = part.shape[1] // 2
    part = part[:, :width] + part[:, width:]
    half = part.shape[0] // 2
    total = part[:half] + turn(part[half:])
    if targets is None:
        out_ref[...] = total
    else:
        rows = out_ref.shape[1]
        for at, c in enumerate(targets):
            out_ref[at] = total[c * rows:(c + 1) * rows]


def close(stems, kept, got, cuts, targets):
    rows, width = stems[0].shape[1], kept.shape[2]
    whole_tiles = rows % (8 * cuts) == 0
    shape = (len(targets), rows // cuts, width) if whole_tiles else (rows, width)
    out = pl.pallas_call(
        functools.partial(close_kernel, targets if whole_tiles else None),
        out_shape=jax.ShapeDtypeStruct(shape, jnp.float32),
        compiler_params=pltpu.CompilerParams(vmem_limit_bytes=24 * MIB),
        cost_estimate=pl.CostEstimate(flops=8 * rows * kept.size, bytes_accessed=MIB, transcendentals=0),
        name="close",
    )(*stems, *got, kept)
    return out if whole_tiles else out.reshape(cuts, -1)[np.array(targets)]


def on_device(stem_tensor, mid_tensors, right_tensors):
    stems = lax.axis_size("stem")
    cuts = lax.axis_size("cuts")

    def swap(x, p):
        return lax.ppermute(x, "stem", [(s, s ^ p) for s in range(stems)])

    def route(target):
        pairs = []
        for at in np.ndindex(cuts, 2, 2):
            cut, side, core = target(*at)
            pairs.append((at[0] * 4 + at[1] * 2 + at[2], cut * 4 + side * 2 + core))
        return lax.ppermute(stem_tensor, ("cuts", "stem"), pairs)

    assert stems == 4
    cross = route(lambda cut, side, core: (cut, 1 - side, 1) if core else (cut ^ 2, side, 0))
    cycle = route(lambda cut, side, core: (cut, side, 0) if core else (cut, 1 - side, 1))
    pieces = [stem_tensor, cross, cycle]
    kept, *sent = branch_sums(mid_tensors, right_tensors, stems)
    got = [swap(x, 1) for x in sent]
    groups = [
        [
            (2 * side + group) * cuts + 2 * plane + column
            for side in range(stems // 2 - 1, -1, -1) for plane in range(cuts // 2 - 1, -1, -1) for column in (1, 0)
        ]
        for group in (0, 1)
    ]
    targets = [at % cuts for at in groups[0]]
    spread = close(pieces, kept, got, cuts, targets)
    parts = lax.all_to_all(spread, ("stem", "cuts"), 0, 0, tiled=True, axis_index_groups=groups)
    total = jnp.sum(parts, axis=0).reshape(-1)
    return total + swap(total, 1)


def solution(mesh):
    return jax.shard_map(
        on_device,
        mesh=mesh,
        in_specs=(
            P("stem", None, None),
            P(("cuts", "stem"), None, None),
            P(None, ("cuts", "stem"), None, None),
        ),
        out_specs=P("cuts"),
        check_vma=False,
    )
```

```python
import functools

import jax
import jax.numpy as jnp
import numpy as np
from jax import lax
from jax.experimental import pallas as pl
from jax.experimental.pallas import tpu as pltpu
from jax.sharding import PartitionSpec as P

MIB = 1024 * 1024
LEAVE_MIB = 48


def turn(x):
    half = x.shape[-1] // 2
    lane = lax.broadcasted_iota(jnp.int32, x.shape, x.ndim - 1)
    rolled = pltpu.roll(x, half, x.ndim - 1)
    return jnp.where(lane < half, -rolled, rolled)


def segments(blocks, depth, sizes):
    out, row = [], 0
    for piece, size in enumerate(sizes):
        end = row + size
        first = row
        while row < end:
            count = min(end, (row // depth + 1) * depth) - row
            out.append((row // depth, row % depth, piece, row - first, count))
            row += count
    return out


def piece_sizes(rows, count):
    size = -(-rows // (16 * count)) * 16
    return [min(size, rows - at) for at in range(0, rows, size)]


def product(mid_ref, wide_ref):
    pairs = mid_ref.shape[0]
    left = jnp.concatenate([mid_ref[j] for j in range(pairs)], axis=1)
    blocks, _, rows, width = wide_ref.shape
    right = [wide_ref[b].reshape(pairs * rows, width) for b in range(blocks)]
    return jnp.dot(left, jnp.concatenate(right, axis=1), preferred_element_type=jnp.float32)


def leave_kernel(blocks, mid_hbm, right_hbm, mid_ref, stay_ref, *refs):
    *sent_refs, leave_ref, mid_sem, right_sem = refs
    pairs, depth, width = mid_ref.shape
    total, _, inner, _ = right_hbm.shape
    groups = total // blocks
    half = groups // 2
    me = lax.axis_index("stem")
    chunk = pairs // mid_sem.shape[0]

    def mid_copy(n):
        at = pl.ds(n * chunk, chunk)
        return pltpu.make_async_copy(mid_hbm.at[at], mid_ref.at[at], mid_sem.at[n])

    def right_copy(q, wide_ref, stays):
        side = (me // 2) ^ (me % 2) ^ stays ^ 1
        source = right_hbm.at[pl.ds((2 * side + q) * blocks, blocks)]
        target = wide_ref.at[pl.ds(q * blocks, blocks), :, pl.ds(0, inner)]
        return pltpu.make_async_copy(source, target, right_sem.at[stays * half + q])

    for q in range(half):
        right_copy(q, leave_ref, 0).start()
    for n in range(mid_sem.shape[0]):
        mid_copy(n).start()
    for q in range(half):
        right_copy(q, stay_ref, 1).start()

    def widen(wide_ref, stays):
        def step(q, carry):
            right_copy(q, wide_ref, stays).wait()
            for b in range(blocks):
                for j in range(pairs):
                    upper = wide_ref[q * blocks + b, j, :inner]
                    wide_ref[q * blocks + b, j, inner:] = turn(upper.astype(jnp.float32)).astype(upper.dtype)
            return carry

        lax.fori_loop(0, half, step, 0)

    widen(leave_ref, 0)
    for n in range(mid_sem.shape[0]):
        mid_copy(n).wait()
    sums = product(mid_ref, leave_ref)
    sizes = [ref.shape[0] for ref in sent_refs]
    for b, row, piece, at, count in segments(total // 2, depth, sizes):
        part = sums[row:row + count, b * width:(b + 1) * width]
        sent_refs[piece][at:at + count] = part.astype(jnp.bfloat16)
    widen(stay_ref, 1)


def stay_kernel(mid_ref, wide_ref, kept_ref):
    sums = product(mid_ref, wide_ref)
    width = kept_ref.shape[2]
    for b in range(kept_ref.shape[0]):
        kept_ref[b] = sums[:, b * width:(b + 1) * width]


def branch_sums(mid, right, groups):
    pairs, depth, width = mid.shape
    total, _, inner, _ = right.shape
    half = total // 2
    sizes = piece_sizes(half * depth, 3)
    wide = (half, pairs, 2 * inner, width)
    vmem = pl.BlockSpec(memory_space=pltpu.VMEM)
    hbm = pl.BlockSpec(memory_space=pltpu.HBM)
    cost = pl.CostEstimate(
        flops=depth * pairs * width * total * width, bytes_accessed=4 * MIB, transcendentals=0
    )
    mid_here, wide_here, *sent = pl.pallas_call(
        functools.partial(leave_kernel, total // groups),
        in_specs=[hbm, hbm],
        out_specs=[vmem] * (2 + len(sizes)),
        out_shape=[
            jax.ShapeDtypeStruct(mid.shape, mid.dtype),
            jax.ShapeDtypeStruct(wide, right.dtype),
        ] + [jax.ShapeDtypeStruct((size, width), jnp.bfloat16) for size in sizes],
        scratch_shapes=[
            pltpu.VMEM(wide, right.dtype),
            pltpu.SemaphoreType.DMA((4,)),
            pltpu.SemaphoreType.DMA((groups,)),
        ],
        compiler_params=pltpu.CompilerParams(vmem_limit_bytes=LEAVE_MIB * MIB),
        cost_estimate=cost,
        name="leave",
    )(mid, right)
    kept = pl.pallas_call(
        stay_kernel,
        out_shape=jax.ShapeDtypeStruct((half, depth, width), jnp.float32),
        compiler_params=pltpu.CompilerParams(vmem_limit_bytes=24 * MIB),
        cost_estimate=cost,
        name="stay",
    )(mid_here, wide_here)
    return kept, *sent


def close_kernel(targets, *refs):
    own_ref, cross_ref, cycle_ref, *got_refs, kept_ref, out_ref = refs
    first_core = lax.axis_index("stem") % 2 == 0
    pieces = segments(kept_ref.shape[0], kept_ref.shape[1], [ref.shape[0] for ref in got_refs])
    part = None
    at = 0
    for when_first, when_second in ((own_ref, cycle_ref), (cycle_ref, cross_ref)):
        for b in range(own_ref.shape[0]):
            block = jnp.where(first_core, when_first[b], when_second[b])
            half = block.shape[-1] // 2
            rows = jnp.concatenate([block[:, :half], block[:, half:]], axis=0)
            got = [got_refs[piece][row:row + count] for block_at, _, piece, row, count in pieces if block_at == at]
            sums = kept_ref[at] + jnp.concatenate(got, axis=0).astype(jnp.float32)
            high = sums.astype(jnp.bfloat16)
            low = (sums - high.astype(jnp.float32)).astype(jnp.bfloat16)
            term = jnp.dot(rows, jnp.concatenate([high, low], axis=1), preferred_element_type=jnp.float32)
            part = term if part is None else part + term
            at += 1
    width = part.shape[1] // 2
    part = part[:, :width] + part[:, width:]
    half = part.shape[0] // 2
    total = part[:half] + turn(part[half:])
    if targets is None:
        out_ref[...] = total
    else:
        rows = out_ref.shape[1]
        for at, c in enumerate(targets):
            out_ref[at] = total[c * rows:(c + 1) * rows].astype(out_ref.dtype)


def close(stems, kept, got, cuts, targets):
    rows, width = stems[0].shape[1], kept.shape[2]
    whole_tiles = rows % (8 * cuts) == 0
    shape = (len(targets), rows // cuts, width) if whole_tiles else (rows, width)
    out = pl.pallas_call(
        functools.partial(close_kernel, targets if whole_tiles else None),
        out_shape=jax.ShapeDtypeStruct(shape, jnp.bfloat16 if whole_tiles else jnp.float32),
        compiler_params=pltpu.CompilerParams(vmem_limit_bytes=24 * MIB),
        cost_estimate=pl.CostEstimate(flops=8 * rows * kept.size, bytes_accessed=MIB, transcendentals=0),
        name="close",
    )(*stems, *got, kept)
    return out if whole_tiles else out.reshape(cuts, -1)[np.array(targets)]


def on_device(stem_tensor, mid_tensors, right_tensors):
    stems = lax.axis_size("stem")
    cuts = lax.axis_size("cuts")

    def swap(x, p):
        return lax.ppermute(x, "stem", [(s, s ^ p) for s in range(stems)])

    def route(target):
        pairs = []
        for at in np.ndindex(cuts, 2, 2):
            cut, side, core = target(*at)
            pairs.append((at[0] * 4 + at[1] * 2 + at[2], cut * 4 + side * 2 + core))
        return lax.ppermute(stem_tensor, ("cuts", "stem"), pairs)

    assert stems == 4
    cross = route(lambda cut, side, core: (cut, 1 - side, 1) if core else (cut ^ 2, side, 0))
    cycle = route(lambda cut, side, core: (cut, side, 0) if core else (cut, 1 - side, 1))
    pieces = [stem_tensor, cross, cycle]
    kept, *sent = branch_sums(mid_tensors, right_tensors, stems)
    got = [swap(x, 1) for x in sent]
    groups = [
        [
            (2 * side + group) * cuts + 2 * plane + column
            for side in range(stems // 2 - 1, -1, -1) for plane in range(cuts // 2 - 1, -1, -1) for column in (1, 0)
        ]
        for group in (0, 1)
    ]
    targets = [at % cuts for at in groups[0]]
    spread = close(pieces, kept, got, cuts, targets)
    parts = lax.all_to_all(spread, ("stem", "cuts"), 0, 0, tiled=True, axis_index_groups=groups)
    total = jnp.sum(parts.astype(jnp.float32), axis=0).reshape(-1)
    return total + swap(total, 1)


def solution(mesh):
    return jax.shard_map(
        on_device,
        mesh=mesh,
        in_specs=(
            P("stem", None, None),
            P(("cuts", "stem"), None, None),
            P(None, ("cuts", "stem"), None, None),
        ),
        out_specs=P("cuts"),
        check_vma=False,
    )
```

```python
import functools

import jax
import jax.numpy as jnp
import numpy as np
from jax import lax
from jax.experimental import pallas as pl
from jax.experimental.pallas import tpu as pltpu
from jax.sharding import PartitionSpec as P

MIB = 1024 * 1024
LEAVE_MIB = 48


def turn(x):
    half = x.shape[-1] // 2
    lane = lax.broadcasted_iota(jnp.int32, x.shape, x.ndim - 1)
    rolled = pltpu.roll(x, half, x.ndim - 1)
    return jnp.where(lane < half, -rolled, rolled)


def segments(blocks, depth, sizes):
    out, row = [], 0
    for piece, size in enumerate(sizes):
        end = row + size
        first = row
        while row < end:
            count = min(end, (row // depth + 1) * depth) - row
            out.append((row // depth, row % depth, piece, row - first, count))
            row += count
    return out


def piece_sizes(rows, count):
    size = -(-rows // (16 * count)) * 16
    return [min(size, rows - at) for at in range(0, rows, size)]


def product(mid_ref, wide_ref):
    pairs = mid_ref.shape[0]
    left = jnp.concatenate([mid_ref[j] for j in range(pairs)], axis=1)
    blocks, _, rows, width = wide_ref.shape
    right = [wide_ref[b].reshape(pairs * rows, width) for b in range(blocks)]
    return jnp.dot(left, jnp.concatenate(right, axis=1), preferred_element_type=jnp.float32)


def leave_kernel(blocks, mid_hbm, right_hbm, mid_ref, stay_ref, *refs):
    *sent_refs, leave_ref, mid_sem, right_sem = refs
    pairs, depth, width = mid_ref.shape
    total, _, inner, _ = right_hbm.shape
    groups = total // blocks
    half = groups // 2
    me = lax.axis_index("stem")
    chunk = pairs // mid_sem.shape[0]

    def mid_copy(n):
        at = pl.ds(n * chunk, chunk)
        return pltpu.make_async_copy(mid_hbm.at[at], mid_ref.at[at], mid_sem.at[n])

    def right_copy(q, wide_ref, stays):
        side = (me // 2) ^ (me % 2) ^ stays ^ 1
        source = right_hbm.at[pl.ds((2 * side + q) * blocks, blocks)]
        target = wide_ref.at[pl.ds(q * blocks, blocks), :, pl.ds(0, inner)]
        return pltpu.make_async_copy(source, target, right_sem.at[stays * half + q])

    for q in range(half):
        right_copy(q, leave_ref, 0).start()
    for n in range(mid_sem.shape[0]):
        mid_copy(n).start()
    for q in range(half):
        right_copy(q, stay_ref, 1).start()

    def widen(wide_ref, stays):
        def step(q, carry):
            right_copy(q, wide_ref, stays).wait()
            for b in range(blocks):
                for j in range(pairs):
                    upper = wide_ref[q * blocks + b, j, :inner]
                    wide_ref[q * blocks + b, j, inner:] = turn(upper.astype(jnp.float32)).astype(upper.dtype)
            return carry

        lax.fori_loop(0, half, step, 0)

    widen(leave_ref, 0)
    for n in range(mid_sem.shape[0]):
        mid_copy(n).wait()
    sums = product(mid_ref, leave_ref)
    sizes = [ref.shape[0] for ref in sent_refs]
    for b, row, piece, at, count in segments(total // 2, depth, sizes):
        part = sums[row:row + count, b * width:(b + 1) * width]
        sent_refs[piece][at:at + count] = part.astype(jnp.bfloat16)
    widen(stay_ref, 1)


def stay_kernel(mid_ref, wide_ref, kept_ref):
    sums = product(mid_ref, wide_ref)
    width = kept_ref.shape[2]
    for b in range(kept_ref.shape[0]):
        kept_ref[b] = sums[:, b * width:(b + 1) * width]


def branch_sums(mid, right, groups):
    pairs, depth, width = mid.shape
    total, _, inner, _ = right.shape
    half = total // 2
    sizes = piece_sizes(half * depth, 3)
    wide = (half, pairs, 2 * inner, width)
    vmem = pl.BlockSpec(memory_space=pltpu.VMEM)
    hbm = pl.BlockSpec(memory_space=pltpu.HBM)
    cost = pl.CostEstimate(
        flops=depth * pairs * width * total * width, bytes_accessed=4 * MIB, transcendentals=0
    )
    mid_here, wide_here, *sent = pl.pallas_call(
        functools.partial(leave_kernel, total // groups),
        in_specs=[hbm, hbm],
        out_specs=[vmem] * (2 + len(sizes)),
        out_shape=[
            jax.ShapeDtypeStruct(mid.shape, mid.dtype),
            jax.ShapeDtypeStruct(wide, right.dtype),
        ] + [jax.ShapeDtypeStruct((size, width), jnp.bfloat16) for size in sizes],
        scratch_shapes=[
            pltpu.VMEM(wide, right.dtype),
            pltpu.SemaphoreType.DMA((4,)),
            pltpu.SemaphoreType.DMA((groups,)),
        ],
        compiler_params=pltpu.CompilerParams(vmem_limit_bytes=LEAVE_MIB * MIB),
        cost_estimate=cost,
        name="leave",
    )(mid, right)
    kept = pl.pallas_call(
        stay_kernel,
        out_shape=jax.ShapeDtypeStruct((half, depth, width), jnp.float32),
        compiler_params=pltpu.CompilerParams(vmem_limit_bytes=24 * MIB),
        cost_estimate=cost,
        name="stay",
    )(mid_here, wide_here)
    return kept, *sent


def close_kernel(targets, *refs):
    own_ref, cycle_ref, cross_ref, *got_refs, kept_ref, out_ref = refs
    first_core = lax.axis_index("stem") % 2 == 0
    pieces = segments(kept_ref.shape[0], kept_ref.shape[1], [ref.shape[0] for ref in got_refs])
    part = None
    at = 0
    for when_first, when_second in ((own_ref, cycle_ref), (cycle_ref, cross_ref)):
        for b in range(own_ref.shape[0]):
            block = jnp.where(first_core, when_first[b], when_second[b])
            half = block.shape[-1] // 2
            rows = jnp.concatenate([block[:, :half], block[:, half:]], axis=0)
            got = [got_refs[piece][row:row + count] for block_at, _, piece, row, count in pieces if block_at == at]
            sums = kept_ref[at] + jnp.concatenate(got, axis=0).astype(jnp.float32)
            high = sums.astype(jnp.bfloat16)
            low = (sums - high.astype(jnp.float32)).astype(jnp.bfloat16)
            term = jnp.dot(rows, jnp.concatenate([high, low], axis=1), preferred_element_type=jnp.float32)
            part = term if part is None else part + term
            at += 1
    width = part.shape[1] // 2
    part = part[:, :width] + part[:, width:]
    half = part.shape[0] // 2
    total = part[:half] + turn(part[half:])
    if targets is None:
        out_ref[...] = total
    else:
        rows = out_ref.shape[1]
        for at, c in enumerate(targets):
            out_ref[at] = total[c * rows:(c + 1) * rows].astype(out_ref.dtype)


def close(stems, kept, got, cuts, targets):
    rows, width = stems[0].shape[1], kept.shape[2]
    whole_tiles = rows % (8 * cuts) == 0
    shape = (len(targets), rows // cuts, width) if whole_tiles else (rows, width)
    out = pl.pallas_call(
        functools.partial(close_kernel, targets if whole_tiles else None),
        out_shape=jax.ShapeDtypeStruct(shape, jnp.bfloat16 if whole_tiles else jnp.float32),
        compiler_params=pltpu.CompilerParams(vmem_limit_bytes=24 * MIB),
        cost_estimate=pl.CostEstimate(flops=8 * rows * kept.size, bytes_accessed=MIB, transcendentals=0),
        name="close",
    )(*stems, *got, kept)
    return out if whole_tiles else out.reshape(cuts, -1)[np.array(targets)]


def on_device(stem_tensor, mid_tensors, right_tensors):
    stems = lax.axis_size("stem")
    cuts = lax.axis_size("cuts")

    def swap(x, p):
        return lax.ppermute(x, "stem", [(s, s ^ p) for s in range(stems)])

    def route(target):
        pairs = []
        for at in np.ndindex(cuts, 2, 2):
            cut, side, core = target(*at)
            pairs.append((at[0] * 4 + at[1] * 2 + at[2], cut * 4 + side * 2 + core))
        return lax.ppermute(stem_tensor, ("cuts", "stem"), pairs)

    assert stems == 4
    cycle = route(lambda cut, side, core: (cut, side, 0) if core else (cut, 1 - side, 1))
    cross = route(lambda cut, side, core: (cut, 1 - side, 1) if core else (cut ^ 2, side, 0))
    pieces = [stem_tensor, cycle, cross]
    kept, *sent = branch_sums(mid_tensors, right_tensors, stems)
    got = [swap(x, 1) for x in sent]
    groups = [
        [
            (2 * side + (plane + group) % 2) * cuts + 2 * plane + column
            for side in range(stems // 2 - 1, -1, -1) for plane in range(cuts // 2 - 1, -1, -1) for column in (1, 0)
        ]
        for group in (0, 1)
    ]
    targets = [at % cuts for at in groups[0]]
    spread = close(pieces, kept, got, cuts, targets)
    parts = lax.all_to_all(spread, ("stem", "cuts"), 0, 0, tiled=True, axis_index_groups=groups)
    total = jnp.sum(parts.astype(jnp.float32), axis=0).reshape(-1)
    return total + swap(total, 1)


def solution(mesh):
    return jax.shard_map(
        on_device,
        mesh=mesh,
        in_specs=(
            P("stem", None, None),
            P(("cuts", "stem"), None, None),
            P(None, ("cuts", "stem"), None, None),
        ),
        out_specs=P("cuts"),
        check_vma=False,
    )
```

```python
import functools

import jax
import jax.numpy as jnp
import numpy as np
from jax import lax
from jax.experimental import pallas as pl
from jax.experimental.pallas import tpu as pltpu
from jax.sharding import PartitionSpec as P

MIB = 1024 * 1024
LEAVE_MIB = 48


def turn(x):
    half = x.shape[-1] // 2
    lane = lax.broadcasted_iota(jnp.int32, x.shape, x.ndim - 1)
    rolled = pltpu.roll(x, half, x.ndim - 1)
    return jnp.where(lane < half, -rolled, rolled)


def segments(blocks, depth, sizes):
    out, row = [], 0
    for piece, size in enumerate(sizes):
        end = row + size
        first = row
        while row < end:
            count = min(end, (row // depth + 1) * depth) - row
            out.append((row // depth, row % depth, piece, row - first, count))
            row += count
    return out


def piece_sizes(rows, count):
    size = -(-rows // (16 * count)) * 16
    return [min(size, rows - at) for at in range(0, rows, size)]


def product(mid_ref, wide_ref):
    pairs = mid_ref.shape[0]
    left = jnp.concatenate([mid_ref[j] for j in range(pairs)], axis=1)
    blocks, _, rows, width = wide_ref.shape
    right = [wide_ref[b].reshape(pairs * rows, width) for b in range(blocks)]
    return jnp.dot(left, jnp.concatenate(right, axis=1), preferred_element_type=jnp.float32)


def leave_kernel(blocks, mid_hbm, right_hbm, mid_ref, stay_ref, *refs):
    *sent_refs, leave_ref, mid_sem, right_sem = refs
    pairs, depth, width = mid_ref.shape
    total, _, inner, _ = right_hbm.shape
    groups = total // blocks
    half = groups // 2
    me = lax.axis_index("stem")
    chunk = pairs // mid_sem.shape[0]

    def mid_copy(n):
        at = pl.ds(n * chunk, chunk)
        return pltpu.make_async_copy(mid_hbm.at[at], mid_ref.at[at], mid_sem.at[n])

    def right_copy(q, wide_ref, stays):
        side = (me // 2) ^ (me % 2) ^ stays ^ 1
        source = right_hbm.at[pl.ds((2 * side + q) * blocks, blocks)]
        target = wide_ref.at[pl.ds(q * blocks, blocks), :, pl.ds(0, inner)]
        return pltpu.make_async_copy(source, target, right_sem.at[stays * half + q])

    for q in range(half):
        right_copy(q, leave_ref, 0).start()
    for n in range(mid_sem.shape[0]):
        mid_copy(n).start()
    for q in range(half):
        right_copy(q, stay_ref, 1).start()

    def widen(wide_ref, stays):
        def step(q, carry):
            right_copy(q, wide_ref, stays).wait()
            for b in range(blocks):
                for j in range(pairs):
                    upper = wide_ref[q * blocks + b, j, :inner]
                    wide_ref[q * blocks + b, j, inner:] = turn(upper.astype(jnp.float32)).astype(upper.dtype)
            return carry

        lax.fori_loop(0, half, step, 0)

    widen(leave_ref, 0)
    for n in range(mid_sem.shape[0]):
        mid_copy(n).wait()
    sums = product(mid_ref, leave_ref)
    sizes = [ref.shape[0] for ref in sent_refs]
    for b, row, piece, at, count in segments(total // 2, depth, sizes):
        part = sums[row:row + count, b * width:(b + 1) * width]
        sent_refs[piece][at:at + count] = part.astype(jnp.bfloat16)
    widen(stay_ref, 1)


def stay_kernel(mid_ref, wide_ref, kept_ref):
    sums = product(mid_ref, wide_ref)
    width = kept_ref.shape[2]
    for b in range(kept_ref.shape[0]):
        kept_ref[b] = sums[:, b * width:(b + 1) * width]


def branch_sums(mid, right, groups):
    pairs, depth, width = mid.shape
    total, _, inner, _ = right.shape
    half = total // 2
    sizes = piece_sizes(half * depth, 3)
    wide = (half, pairs, 2 * inner, width)
    vmem = pl.BlockSpec(memory_space=pltpu.VMEM)
    hbm = pl.BlockSpec(memory_space=pltpu.HBM)
    cost = pl.CostEstimate(
        flops=depth * pairs * width * total * width, bytes_accessed=4 * MIB, transcendentals=0
    )
    mid_here, wide_here, *sent = pl.pallas_call(
        functools.partial(leave_kernel, total // groups),
        in_specs=[hbm, hbm],
        out_specs=[vmem] * (2 + len(sizes)),
        out_shape=[
            jax.ShapeDtypeStruct(mid.shape, mid.dtype),
            jax.ShapeDtypeStruct(wide, right.dtype),
        ] + [jax.ShapeDtypeStruct((size, width), jnp.bfloat16) for size in sizes],
        scratch_shapes=[
            pltpu.VMEM(wide, right.dtype),
            pltpu.SemaphoreType.DMA((4,)),
            pltpu.SemaphoreType.DMA((groups,)),
        ],
        compiler_params=pltpu.CompilerParams(vmem_limit_bytes=LEAVE_MIB * MIB),
        cost_estimate=cost,
        name="leave",
    )(mid, right)
    kept = pl.pallas_call(
        stay_kernel,
        out_shape=jax.ShapeDtypeStruct((half, depth, width), jnp.float32),
        compiler_params=pltpu.CompilerParams(vmem_limit_bytes=24 * MIB),
        cost_estimate=cost,
        name="stay",
    )(mid_here, wide_here)
    return kept, *sent


def close_kernel(targets, *refs):
    own_ref, cross_ref, cycle_ref, *got_refs, kept_ref, out_ref = refs
    first_core = lax.axis_index("stem") % 2 == 0
    pieces = segments(kept_ref.shape[0], kept_ref.shape[1], [ref.shape[0] for ref in got_refs])
    part = None
    at = 0
    for when_first, when_second in ((own_ref, cycle_ref), (cycle_ref, cross_ref)):
        for b in range(own_ref.shape[0]):
            block = jnp.where(first_core, when_first[b], when_second[b])
            half = block.shape[-1] // 2
            rows = jnp.concatenate([block[:, :half], block[:, half:]], axis=0)
            got = [got_refs[piece][row:row + count] for block_at, _, piece, row, count in pieces if block_at == at]
            sums = kept_ref[at] + jnp.concatenate(got, axis=0).astype(jnp.float32)
            high = sums.astype(jnp.bfloat16)
            low = (sums - high.astype(jnp.float32)).astype(jnp.bfloat16)
            term = jnp.dot(rows, jnp.concatenate([high, low], axis=1), preferred_element_type=jnp.float32)
            part = term if part is None else part + term
            at += 1
    width = part.shape[1] // 2
    part = part[:, :width] + part[:, width:]
    half = part.shape[0] // 2
    total = part[:half] + turn(part[half:])
    if targets is None:
        out_ref[...] = total
    else:
        rows = out_ref.shape[1]
        for at, c in enumerate(targets):
            out_ref[at] = total[c * rows:(c + 1) * rows].astype(out_ref.dtype)


def close(stems, kept, got, cuts, targets):
    rows, width = stems[0].shape[1], kept.shape[2]
    whole_tiles = rows % (8 * cuts) == 0
    shape = (len(targets), rows // cuts, width) if whole_tiles else (rows, width)
    out = pl.pallas_call(
        functools.partial(close_kernel, targets if whole_tiles else None),
        out_shape=jax.ShapeDtypeStruct(shape, jnp.bfloat16 if whole_tiles else jnp.float32),
        compiler_params=pltpu.CompilerParams(vmem_limit_bytes=24 * MIB),
        cost_estimate=pl.CostEstimate(flops=8 * rows * kept.size, bytes_accessed=MIB, transcendentals=0),
        name="close",
    )(*stems, *got, kept)
    return out if whole_tiles else out.reshape(cuts, -1)[np.array(targets)]


def on_device(stem_tensor, mid_tensors, right_tensors):
    stems = lax.axis_size("stem")
    cuts = lax.axis_size("cuts")

    def swap(x, p):
        return lax.ppermute(x, "stem", [(s, s ^ p) for s in range(stems)])

    def route(target):
        pairs = []
        for at in np.ndindex(cuts, 2, 2):
            cut, side, core = target(*at)
            pairs.append((at[0] * 4 + at[1] * 2 + at[2], cut * 4 + side * 2 + core))
        return lax.ppermute(stem_tensor, ("cuts", "stem"), pairs)

    assert stems == 4
    cross = route(lambda cut, side, core: (cut, 1 - side, 1) if core else (cut ^ 2, side, 0))
    cycle = route(lambda cut, side, core: (cut, side, 0) if core else (cut, 1 - side, 1))
    pieces = [stem_tensor, cross, cycle]
    kept, *sent = branch_sums(mid_tensors, right_tensors, stems)
    got = [swap(x, 1) for x in sent]
    groups = [
        [
            (2 * side + (plane + group) % 2) * cuts + 2 * plane + column
            for side in range(stems // 2 - 1, -1, -1) for plane in range(cuts // 2 - 1, -1, -1) for column in (1, 0)
        ]
        for group in (0, 1)
    ]
    targets = [at % cuts for at in groups[0]]
    spread = close(pieces, kept, got, cuts, targets)
    parts = lax.all_to_all(spread, ("stem", "cuts"), 0, 0, tiled=True, axis_index_groups=groups)
    total = jnp.sum(parts.astype(jnp.float32), axis=0).reshape(-1)
    return total + swap(total, 1)


def solution(mesh):
    return jax.shard_map(
        on_device,
        mesh=mesh,
        in_specs=(
            P("stem", None, None),
            P(("cuts", "stem"), None, None),
            P(None, ("cuts", "stem"), None, None),
        ),
        out_specs=P("cuts"),
        check_vma=False,
    )
```

```python
import functools

import jax
import jax.numpy as jnp
import numpy as np
from jax import lax
from jax.experimental import pallas as pl
from jax.experimental.pallas import tpu as pltpu
from jax.sharding import PartitionSpec as P

MIB = 1024 * 1024
LEAVE_MIB = 48


def turn(x):
    half = x.shape[-1] // 2
    lane = lax.broadcasted_iota(jnp.int32, x.shape, x.ndim - 1)
    rolled = pltpu.roll(x, half, x.ndim - 1)
    return jnp.where(lane < half, -rolled, rolled)


def segments(blocks, depth, sizes):
    out, row = [], 0
    for piece, size in enumerate(sizes):
        end = row + size
        first = row
        while row < end:
            count = min(end, (row // depth + 1) * depth) - row
            out.append((row // depth, row % depth, piece, row - first, count))
            row += count
    return out


def piece_sizes(rows, count):
    size = -(-rows // (16 * count)) * 16
    return [min(size, rows - at) for at in range(0, rows, size)]


def product(mid_ref, wide_ref):
    pairs = mid_ref.shape[0]
    left = jnp.concatenate([mid_ref[j] for j in range(pairs)], axis=1)
    blocks, _, rows, width = wide_ref.shape
    right = [wide_ref[b].reshape(pairs * rows, width) for b in range(blocks)]
    return jnp.dot(left, jnp.concatenate(right, axis=1), preferred_element_type=jnp.float32)


def leave_kernel(blocks, mid_hbm, right_hbm, mid_ref, stay_ref, *refs):
    *sent_refs, leave_ref, mid_sem, right_sem = refs
    pairs, depth, width = mid_ref.shape
    total, _, inner, _ = right_hbm.shape
    groups = total // blocks
    half = groups // 2
    me = lax.axis_index("stem")
    chunk = pairs // mid_sem.shape[0]

    def mid_copy(n):
        at = pl.ds(n * chunk, chunk)
        return pltpu.make_async_copy(mid_hbm.at[at], mid_ref.at[at], mid_sem.at[n])

    def right_copy(q, wide_ref, stays):
        side = (me // 2) ^ (me % 2) ^ stays ^ 1
        source = right_hbm.at[pl.ds((2 * side + q) * blocks, blocks)]
        target = wide_ref.at[pl.ds(q * blocks, blocks), :, pl.ds(0, inner)]
        return pltpu.make_async_copy(source, target, right_sem.at[stays * half + q])

    for q in range(half):
        right_copy(q, leave_ref, 0).start()
    for n in range(mid_sem.shape[0]):
        mid_copy(n).start()
    for q in range(half):
        right_copy(q, stay_ref, 1).start()

    def widen(wide_ref, stays):
        def step(q, carry):
            right_copy(q, wide_ref, stays).wait()
            for b in range(blocks):
                for j in range(pairs):
                    upper = wide_ref[q * blocks + b, j, :inner]
                    wide_ref[q * blocks + b, j, inner:] = turn(upper.astype(jnp.float32)).astype(upper.dtype)
            return carry

        lax.fori_loop(0, half, step, 0)

    widen(leave_ref, 0)
    for n in range(mid_sem.shape[0]):
        mid_copy(n).wait()
    sums = product(mid_ref, leave_ref)
    sizes = [ref.shape[0] for ref in sent_refs]
    for b, row, piece, at, count in segments(total // 2, depth, sizes):
        part = sums[row:row + count, b * width:(b + 1) * width]
        sent_refs[piece][at:at + count] = part.astype(jnp.bfloat16)
    widen(stay_ref, 1)


def stay_kernel(mid_ref, wide_ref, kept_ref):
    sums = product(mid_ref, wide_ref)
    width = kept_ref.shape[2]
    for b in range(kept_ref.shape[0]):
        kept_ref[b] = sums[:, b * width:(b + 1) * width]


def branch_sums(mid, right, groups):
    pairs, depth, width = mid.shape
    total, _, inner, _ = right.shape
    half = total // 2
    sizes = piece_sizes(half * depth, 3)
    wide = (half, pairs, 2 * inner, width)
    vmem = pl.BlockSpec(memory_space=pltpu.VMEM)
    hbm = pl.BlockSpec(memory_space=pltpu.HBM)
    cost = pl.CostEstimate(
        flops=depth * pairs * width * total * width, bytes_accessed=4 * MIB, transcendentals=0
    )
    mid_here, wide_here, *sent = pl.pallas_call(
        functools.partial(leave_kernel, total // groups),
        in_specs=[hbm, hbm],
        out_specs=[vmem] * (2 + len(sizes)),
        out_shape=[
            jax.ShapeDtypeStruct(mid.shape, mid.dtype),
            jax.ShapeDtypeStruct(wide, right.dtype),
        ] + [jax.ShapeDtypeStruct((size, width), jnp.bfloat16) for size in sizes],
        scratch_shapes=[
            pltpu.VMEM(wide, right.dtype),
            pltpu.SemaphoreType.DMA((4,)),
            pltpu.SemaphoreType.DMA((groups,)),
        ],
        compiler_params=pltpu.CompilerParams(vmem_limit_bytes=LEAVE_MIB * MIB),
        cost_estimate=cost,
        name="leave",
    )(mid, right)
    kept = pl.pallas_call(
        stay_kernel,
        out_shape=jax.ShapeDtypeStruct((half, depth, width), jnp.float32),
        compiler_params=pltpu.CompilerParams(vmem_limit_bytes=24 * MIB),
        cost_estimate=cost,
        name="stay",
    )(mid_here, wide_here)
    return kept, *sent


def stacked(block):
    half = block.shape[-1] // 2
    return jnp.concatenate([block[:, :half], block[:, half:]], axis=0)


def fold_kernel(own_ref, cycle_ref, kept_ref, *refs):
    *got_refs, part_ref, far_ref = refs
    blocks, depth, width = kept_ref.shape
    own = own_ref.shape[0]
    first_core = lax.axis_index("stem") % 2 == 0
    pieces = segments(blocks, depth, [ref.shape[0] for ref in got_refs])
    part = None
    for b in range(blocks):
        got = [got_refs[piece][at:at + count] for block, _, piece, at, count in pieces if block == b]
        sums = kept_ref[b] + jnp.concatenate(got, axis=0).astype(jnp.float32)
        high = sums.astype(jnp.bfloat16)
        low = (sums - high.astype(jnp.float32)).astype(jnp.bfloat16)
        both = jnp.concatenate([high, low], axis=1)
        if b < own:
            term = jnp.dot(stacked(jnp.where(first_core, own_ref[b], cycle_ref[b])), both, preferred_element_type=jnp.float32)
            part = term if part is None else part + term
        else:
            far_ref[b - own] = both
    part_ref[...] = part


def fold(own, cycle, kept, got):
    count, rows, _ = own.shape
    blocks, depth, width = kept.shape
    return pl.pallas_call(
        fold_kernel,
        out_shape=[
            jax.ShapeDtypeStruct((2 * rows, 2 * width), jnp.float32),
            jax.ShapeDtypeStruct((blocks - count, depth, 2 * width), jnp.bfloat16),
        ],
        compiler_params=pltpu.CompilerParams(vmem_limit_bytes=24 * MIB),
        cost_estimate=pl.CostEstimate(flops=8 * rows * kept.size, bytes_accessed=MIB, transcendentals=0),
        name="fold",
    )(own, cycle, kept, *got)


def close_kernel(targets, *refs):
    cycle_ref, cross_ref, part_ref, far_ref, out_ref = refs
    first_core = lax.axis_index("stem") % 2 == 0
    part = part_ref[...]
    for b in range(far_ref.shape[0]):
        block = jnp.where(first_core, cycle_ref[b], cross_ref[b])
        part += jnp.dot(stacked(block), far_ref[b], preferred_element_type=jnp.float32)
    width = part.shape[1] // 2
    part = part[:, :width] + part[:, width:]
    half = part.shape[0] // 2
    total = part[:half] + turn(part[half:])
    if targets is None:
        out_ref[...] = total
    else:
        rows = out_ref.shape[1]
        for at, c in enumerate(targets):
            out_ref[at] = total[c * rows:(c + 1) * rows].astype(out_ref.dtype)


def close(stems, part, far, cuts, targets):
    rows, width = part.shape[0] // 2, part.shape[1] // 2
    whole_tiles = rows % (8 * cuts) == 0
    shape = (len(targets), rows // cuts, width) if whole_tiles else (rows, width)
    out = pl.pallas_call(
        functools.partial(close_kernel, targets if whole_tiles else None),
        out_shape=jax.ShapeDtypeStruct(shape, jnp.bfloat16 if whole_tiles else jnp.float32),
        compiler_params=pltpu.CompilerParams(vmem_limit_bytes=24 * MIB),
        cost_estimate=pl.CostEstimate(flops=4 * rows * far.size, bytes_accessed=MIB, transcendentals=0),
        name="close",
    )(*stems, part, far)
    return out if whole_tiles else out.reshape(cuts, -1)[np.array(targets)]


def on_device(stem_tensor, mid_tensors, right_tensors):
    stems = lax.axis_size("stem")
    cuts = lax.axis_size("cuts")

    def swap(x, p):
        return lax.ppermute(x, "stem", [(s, s ^ p) for s in range(stems)])

    def route(target):
        pairs = []
        for at in np.ndindex(cuts, 2, 2):
            cut, side, core = target(*at)
            pairs.append((at[0] * 4 + at[1] * 2 + at[2], cut * 4 + side * 2 + core))
        return lax.ppermute(stem_tensor, ("cuts", "stem"), pairs)

    assert stems == 4
    cross = route(lambda cut, side, core: (cut, 1 - side, 1) if core else (cut ^ 2, side, 0))
    cycle = route(lambda cut, side, core: (cut, side, 0) if core else (cut, 1 - side, 1))
    kept, *sent = branch_sums(mid_tensors, right_tensors, stems)
    got = [swap(x, 1) for x in sent]
    groups = [
        [
            (2 * side + group) * cuts + 2 * plane + column
            for side in range(stems // 2 - 1, -1, -1) for plane in range(cuts // 2 - 1, -1, -1) for column in (1, 0)
        ]
        for group in (0, 1)
    ]
    targets = [at % cuts for at in groups[0]]
    part, far = fold(stem_tensor, cycle, kept, got)
    spread = close([cycle, cross], part, far, cuts, targets)
    parts = lax.all_to_all(spread, ("stem", "cuts"), 0, 0, tiled=True, axis_index_groups=groups)
    total = jnp.sum(parts.astype(jnp.float32), axis=0).reshape(-1)
    return total + swap(total, 1)


def solution(mesh):
    return jax.shard_map(
        on_device,
        mesh=mesh,
        in_specs=(
            P("stem", None, None),
            P(("cuts", "stem"), None, None),
            P(None, ("cuts", "stem"), None, None),
        ),
        out_specs=P("cuts"),
        check_vma=False,
    )
```

```python
import functools

import jax
import jax.numpy as jnp
import numpy as np
from jax import lax
from jax.experimental import pallas as pl
from jax.experimental.pallas import tpu as pltpu
from jax.sharding import PartitionSpec as P

MIB = 1024 * 1024
LEAVE_MIB = 49


def turn(x):
    half = x.shape[-1] // 2
    lane = lax.broadcasted_iota(jnp.int32, x.shape, x.ndim - 1)
    rolled = pltpu.roll(x, half, x.ndim - 1)
    return jnp.where(lane < half, -rolled, rolled)


def segments(blocks, depth, sizes):
    out, row = [], 0
    for piece, size in enumerate(sizes):
        end = row + size
        first = row
        while row < end:
            count = min(end, (row // depth + 1) * depth) - row
            out.append((row // depth, row % depth, piece, row - first, count))
            row += count
    return out


def piece_sizes(rows, count):
    size = -(-rows // (16 * count)) * 16
    return [min(size, rows - at) for at in range(0, rows, size)]


def product(mid_ref, wide_ref):
    pairs = mid_ref.shape[0]
    left = jnp.concatenate([mid_ref[j] for j in range(pairs)], axis=1)
    blocks, _, rows, width = wide_ref.shape
    if rows == width:
        right = [wide_ref[b].reshape(pairs * rows, width) for b in range(blocks)]
    else:
        right = []
        for b in range(blocks):
            both = []
            for j in range(pairs):
                upper = wide_ref[b, j]
                both += [upper, turn(upper.astype(jnp.float32)).astype(upper.dtype)]
            right.append(jnp.concatenate(both, axis=0))
    return jnp.dot(left, jnp.concatenate(right, axis=1), preferred_element_type=jnp.float32)


def leave_kernel(blocks, mid_hbm, right_hbm, mid_ref, stay_ref, *refs):
    *sent_refs, leave_ref, mid_sem, right_sem = refs
    pairs, depth, width = mid_ref.shape
    total, _, inner, _ = right_hbm.shape
    groups = total // blocks
    half = groups // 2
    me = lax.axis_index("stem")
    chunk = pairs // mid_sem.shape[0]

    def mid_copy(n):
        at = pl.ds(n * chunk, chunk)
        return pltpu.make_async_copy(mid_hbm.at[at], mid_ref.at[at], mid_sem.at[n])

    def right_copy(q, wide_ref, stays):
        side = (me // 2) ^ (me % 2) ^ stays ^ 1
        source = right_hbm.at[pl.ds((2 * side + q) * blocks, blocks)]
        target = wide_ref.at[pl.ds(q * blocks, blocks), :, pl.ds(0, inner)]
        return pltpu.make_async_copy(source, target, right_sem.at[stays * half + q])

    for q in range(half):
        right_copy(q, leave_ref, 0).start()
    for n in range(mid_sem.shape[0]):
        mid_copy(n).start()
    for q in range(half):
        right_copy(q, stay_ref, 1).start()

    def widen(wide_ref, stays):
        def step(q, carry):
            right_copy(q, wide_ref, stays).wait()
            for b in range(blocks):
                for j in range(pairs):
                    upper = wide_ref[q * blocks + b, j, :inner]
                    wide_ref[q * blocks + b, j, inner:] = turn(upper.astype(jnp.float32)).astype(upper.dtype)
            return carry

        lax.fori_loop(0, half, step, 0)

    widen(leave_ref, 0)
    for n in range(mid_sem.shape[0]):
        mid_copy(n).wait()
    sums = product(mid_ref, leave_ref)
    sizes = [ref.shape[0] for ref in sent_refs]
    for b, row, piece, at, count in segments(total // 2, depth, sizes):
        part = sums[row:row + count, b * width:(b + 1) * width]
        sent_refs[piece][at:at + count] = part.astype(jnp.bfloat16)
    for q in range(half):
        right_copy(q, stay_ref, 1).wait()


def stay_kernel(mid_ref, wide_ref, kept_ref):
    sums = product(mid_ref, wide_ref)
    width = kept_ref.shape[2]
    for b in range(kept_ref.shape[0]):
        kept_ref[b] = sums[:, b * width:(b + 1) * width]


def branch_sums(mid, right, groups):
    pairs, depth, width = mid.shape
    total, _, inner, _ = right.shape
    half = total // 2
    sizes = piece_sizes(half * depth, 3)
    wide = (half, pairs, 2 * inner, width)
    vmem = pl.BlockSpec(memory_space=pltpu.VMEM)
    hbm = pl.BlockSpec(memory_space=pltpu.HBM)
    cost = pl.CostEstimate(
        flops=depth * pairs * width * total * width, bytes_accessed=4 * MIB, transcendentals=0
    )
    mid_here, wide_here, *sent = pl.pallas_call(
        functools.partial(leave_kernel, total // groups),
        in_specs=[hbm, hbm],
        out_specs=[vmem] * (2 + len(sizes)),
        out_shape=[
            jax.ShapeDtypeStruct(mid.shape, mid.dtype),
            jax.ShapeDtypeStruct((half, pairs, inner, width), right.dtype),
        ] + [jax.ShapeDtypeStruct((size, width), jnp.bfloat16) for size in sizes],
        scratch_shapes=[
            pltpu.VMEM(wide, right.dtype),
            pltpu.SemaphoreType.DMA((4,)),
            pltpu.SemaphoreType.DMA((groups,)),
        ],
        compiler_params=pltpu.CompilerParams(vmem_limit_bytes=LEAVE_MIB * MIB),
        cost_estimate=cost,
        name="leave",
    )(mid, right)
    kept = pl.pallas_call(
        stay_kernel,
        out_shape=jax.ShapeDtypeStruct((half, depth, width), jnp.float32),
        compiler_params=pltpu.CompilerParams(vmem_limit_bytes=24 * MIB),
        cost_estimate=cost,
        name="stay",
    )(mid_here, wide_here)
    return kept, *sent


def close_kernel(targets, *refs):
    own_ref, cross_ref, cycle_ref, *got_refs, kept_ref, out_ref = refs
    first_core = lax.axis_index("stem") % 2 == 0
    pieces = segments(kept_ref.shape[0], kept_ref.shape[1], [ref.shape[0] for ref in got_refs])
    part = None
    at = 0
    for when_first, when_second in ((own_ref, cycle_ref), (cycle_ref, cross_ref)):
        for b in range(own_ref.shape[0]):
            block = jnp.where(first_core, when_first[b], when_second[b])
            half = block.shape[-1] // 2
            rows = jnp.concatenate([block[:, :half], block[:, half:]], axis=0)
            got = [got_refs[piece][row:row + count] for block_at, _, piece, row, count in pieces if block_at == at]
            sums = kept_ref[at] + jnp.concatenate(got, axis=0).astype(jnp.float32)
            high = sums.astype(jnp.bfloat16)
            low = (sums - high.astype(jnp.float32)).astype(jnp.bfloat16)
            term = jnp.dot(rows, jnp.concatenate([high, low], axis=1), preferred_element_type=jnp.float32)
            part = term if part is None else part + term
            at += 1
    width = part.shape[1] // 2
    part = part[:, :width] + part[:, width:]
    half = part.shape[0] // 2
    total = part[:half] + turn(part[half:])
    if targets is None:
        out_ref[...] = total
    else:
        rows = out_ref.shape[1]
        for at, c in enumerate(targets):
            out_ref[at] = total[c * rows:(c + 1) * rows].astype(out_ref.dtype)


def close(stems, kept, got, cuts, targets):
    rows, width = stems[0].shape[1], kept.shape[2]
    whole_tiles = rows % (8 * cuts) == 0
    shape = (len(targets), rows // cuts, width) if whole_tiles else (rows, width)
    out = pl.pallas_call(
        functools.partial(close_kernel, targets if whole_tiles else None),
        out_shape=jax.ShapeDtypeStruct(shape, jnp.bfloat16 if whole_tiles else jnp.float32),
        compiler_params=pltpu.CompilerParams(vmem_limit_bytes=24 * MIB),
        cost_estimate=pl.CostEstimate(flops=8 * rows * kept.size, bytes_accessed=MIB, transcendentals=0),
        name="close",
    )(*stems, *got, kept)
    return out if whole_tiles else out.reshape(cuts, -1)[np.array(targets)]


def on_device(stem_tensor, mid_tensors, right_tensors):
    stems = lax.axis_size("stem")
    cuts = lax.axis_size("cuts")

    def swap(x, p):
        return lax.ppermute(x, "stem", [(s, s ^ p) for s in range(stems)])

    def route(target):
        pairs = []
        for at in np.ndindex(cuts, 2, 2):
            cut, side, core = target(*at)
            pairs.append((at[0] * 4 + at[1] * 2 + at[2], cut * 4 + side * 2 + core))
        return lax.ppermute(stem_tensor, ("cuts", "stem"), pairs)

    assert stems == 4
    cross = route(lambda cut, side, core: (cut, 1 - side, 1) if core else (cut ^ 2, side, 0))
    cycle = route(lambda cut, side, core: (cut, side, 0) if core else (cut, 1 - side, 1))
    pieces = [stem_tensor, cross, cycle]
    kept, *sent = branch_sums(mid_tensors, right_tensors, stems)
    got = [swap(x, 1) for x in sent]
    groups = [
        [
            (2 * side + group) * cuts + 2 * plane + column
            for side in range(stems // 2 - 1, -1, -1) for plane in range(cuts // 2 - 1, -1, -1) for column in (1, 0)
        ]
        for group in (0, 1)
    ]
    targets = [at % cuts for at in groups[0]]
    spread = close(pieces, kept, got, cuts, targets)
    parts = lax.all_to_all(spread, ("stem", "cuts"), 0, 0, tiled=True, axis_index_groups=groups)
    total = jnp.sum(parts.astype(jnp.float32), axis=0).reshape(-1)
    return total + swap(total, 1)


def solution(mesh):
    return jax.shard_map(
        on_device,
        mesh=mesh,
        in_specs=(
            P("stem", None, None),
            P(("cuts", "stem"), None, None),
            P(None, ("cuts", "stem"), None, None),
        ),
        out_specs=P("cuts"),
        check_vma=False,
    )
```

```python
import functools

import jax
import jax.numpy as jnp
import numpy as np
from jax import lax
from jax.experimental import pallas as pl
from jax.experimental.pallas import tpu as pltpu
from jax.sharding import PartitionSpec as P

MIB = 1024 * 1024
LEAVE_MIB = 49


def turn(x):
    half = x.shape[-1] // 2
    lane = lax.broadcasted_iota(jnp.int32, x.shape, x.ndim - 1)
    rolled = pltpu.roll(x, half, x.ndim - 1)
    return jnp.where(lane < half, -rolled, rolled)


def segments(blocks, depth, sizes):
    out, row = [], 0
    for piece, size in enumerate(sizes):
        end = row + size
        first = row
        while row < end:
            count = min(end, (row // depth + 1) * depth) - row
            out.append((row // depth, row % depth, piece, row - first, count))
            row += count
    return out


def piece_sizes(rows, count):
    size = -(-rows // (16 * count)) * 16
    return [min(size, rows - at) for at in range(0, rows, size)]


def product(mid_ref, wide_ref):
    pairs = mid_ref.shape[0]
    left = jnp.concatenate([mid_ref[j] for j in range(pairs)], axis=1)
    blocks, _, rows, width = wide_ref.shape
    if rows == width:
        right = [wide_ref[b].reshape(pairs * rows, width) for b in range(blocks)]
    else:
        right = []
        for b in range(blocks):
            both = []
            for j in range(pairs):
                upper = wide_ref[b, j]
                both += [upper, turn(upper.astype(jnp.float32)).astype(upper.dtype)]
            right.append(jnp.concatenate(both, axis=0))
    return jnp.dot(left, jnp.concatenate(right, axis=1), preferred_element_type=jnp.float32)


def leave_kernel(blocks, mid_hbm, right_hbm, mid_ref, stay_ref, *refs):
    *sent_refs, leave_ref, mid_sem, right_sem = refs
    pairs, depth, width = mid_ref.shape
    total, _, inner, _ = right_hbm.shape
    groups = total // blocks
    half = groups // 2
    me = lax.axis_index("stem")
    chunk = pairs // mid_sem.shape[0]

    def mid_copy(n):
        at = pl.ds(n * chunk, chunk)
        return pltpu.make_async_copy(mid_hbm.at[at], mid_ref.at[at], mid_sem.at[n])

    def right_copy(q, wide_ref, stays):
        side = (me // 2) ^ (me % 2) ^ stays ^ 1
        source = right_hbm.at[pl.ds((2 * side + q) * blocks, blocks)]
        target = wide_ref.at[pl.ds(q * blocks, blocks), :, pl.ds(0, inner)]
        return pltpu.make_async_copy(source, target, right_sem.at[stays * half + q])

    for q in range(half):
        right_copy(q, leave_ref, 0).start()
    for n in range(mid_sem.shape[0]):
        mid_copy(n).start()
    for q in range(half):
        right_copy(q, stay_ref, 1).start()

    def widen(wide_ref, stays):
        def step(q, carry):
            right_copy(q, wide_ref, stays).wait()
            for b in range(blocks):
                for j in range(pairs):
                    upper = wide_ref[q * blocks + b, j, :inner]
                    wide_ref[q * blocks + b, j, inner:] = turn(upper.astype(jnp.float32)).astype(upper.dtype)
            return carry

        lax.fori_loop(0, half, step, 0)

    widen(leave_ref, 0)
    for n in range(mid_sem.shape[0]):
        mid_copy(n).wait()
    sums = product(mid_ref, leave_ref)
    sizes = [ref.shape[0] for ref in sent_refs]
    for b, row, piece, at, count in segments(total // 2, depth, sizes):
        part = sums[row:row + count, b * width:(b + 1) * width]
        sent_refs[piece][at:at + count] = part.astype(jnp.bfloat16)
    for q in range(half):
        right_copy(q, stay_ref, 1).wait()


def stay_kernel(mid_ref, wide_ref, kept_ref):
    sums = product(mid_ref, wide_ref)
    width = kept_ref.shape[2]
    for b in range(kept_ref.shape[0]):
        kept_ref[b] = sums[:, b * width:(b + 1) * width]


def branch_sums(mid, right, groups):
    pairs, depth, width = mid.shape
    total, _, inner, _ = right.shape
    half = total // 2
    sizes = piece_sizes(half * depth, 3)
    wide = (half, pairs, 2 * inner, width)
    vmem = pl.BlockSpec(memory_space=pltpu.VMEM)
    hbm = pl.BlockSpec(memory_space=pltpu.HBM)
    cost = pl.CostEstimate(
        flops=depth * pairs * width * total * width, bytes_accessed=4 * MIB, transcendentals=0
    )
    mid_here, wide_here, *sent = pl.pallas_call(
        functools.partial(leave_kernel, total // groups),
        in_specs=[hbm, hbm],
        out_specs=[vmem] * (2 + len(sizes)),
        out_shape=[
            jax.ShapeDtypeStruct(mid.shape, mid.dtype),
            jax.ShapeDtypeStruct((half, pairs, inner, width), right.dtype),
        ] + [jax.ShapeDtypeStruct((size, width), jnp.bfloat16) for size in sizes],
        scratch_shapes=[
            pltpu.VMEM(wide, right.dtype),
            pltpu.SemaphoreType.DMA((4,)),
            pltpu.SemaphoreType.DMA((groups,)),
        ],
        compiler_params=pltpu.CompilerParams(vmem_limit_bytes=LEAVE_MIB * MIB),
        cost_estimate=cost,
        name="leave",
    )(mid, right)
    kept = pl.pallas_call(
        stay_kernel,
        out_shape=jax.ShapeDtypeStruct((half, depth, width), jnp.float32),
        compiler_params=pltpu.CompilerParams(vmem_limit_bytes=24 * MIB),
        cost_estimate=cost,
        name="stay",
    )(mid_here, wide_here)
    return kept, *sent


def close_kernel(targets, *refs):
    own_ref, cross_ref, cycle_ref, *got_refs, kept_ref, out_ref = refs
    first_core = lax.axis_index("stem") % 2 == 0
    pieces = segments(kept_ref.shape[0], kept_ref.shape[1], [ref.shape[0] for ref in got_refs])
    part = None
    at = 0
    for when_first, when_second in ((own_ref, cycle_ref), (cycle_ref, cross_ref)):
        for b in range(own_ref.shape[0]):
            block = jnp.where(first_core, when_first[b], when_second[b])
            half = block.shape[-1] // 2
            rows = jnp.concatenate([block[:, :half], block[:, half:]], axis=0)
            got = [got_refs[piece][row:row + count] for block_at, _, piece, row, count in pieces if block_at == at]
            sums = kept_ref[at] + jnp.concatenate(got, axis=0).astype(jnp.float32)
            high = sums.astype(jnp.bfloat16)
            low = (sums - high.astype(jnp.float32)).astype(jnp.bfloat16)
            term = jnp.dot(rows, jnp.concatenate([high, low], axis=1), preferred_element_type=jnp.float32)
            part = term if part is None else part + term
            at += 1
    width = part.shape[1] // 2
    part = part[:, :width] + part[:, width:]
    half = part.shape[0] // 2
    total = part[:half] + turn(part[half:])
    if targets is None:
        out_ref[...] = total
    else:
        rows = out_ref.shape[1]
        for at, c in enumerate(targets):
            out_ref[at] = total[c * rows:(c + 1) * rows].astype(out_ref.dtype)


def close(stems, kept, got, cuts, targets):
    rows, width = stems[0].shape[1], kept.shape[2]
    whole_tiles = rows % (8 * cuts) == 0
    shape = (len(targets), rows // cuts, width) if whole_tiles else (rows, width)
    out = pl.pallas_call(
        functools.partial(close_kernel, targets if whole_tiles else None),
        out_shape=jax.ShapeDtypeStruct(shape, jnp.bfloat16 if whole_tiles else jnp.float32),
        compiler_params=pltpu.CompilerParams(vmem_limit_bytes=24 * MIB),
        cost_estimate=pl.CostEstimate(flops=8 * rows * kept.size, bytes_accessed=MIB, transcendentals=0),
        name="close",
    )(*stems, *got, kept)
    return out if whole_tiles else out.reshape(cuts, -1)[np.array(targets)]


def on_device(stem_tensor, mid_tensors, right_tensors):
    stems = lax.axis_size("stem")
    cuts = lax.axis_size("cuts")

    def swap(x, p):
        return lax.ppermute(x, "stem", [(s, s ^ p) for s in range(stems)])

    def route(target):
        pairs = []
        for at in np.ndindex(cuts, 2, 2):
            cut, side, core = target(*at)
            pairs.append((at[0] * 4 + at[1] * 2 + at[2], cut * 4 + side * 2 + core))
        return lax.ppermute(stem_tensor, ("cuts", "stem"), pairs)

    assert stems == 4
    cross = route(lambda cut, side, core: (cut, 1 - side, 1) if core else (cut ^ 2, side, 0))
    cycle = route(lambda cut, side, core: (cut, side, 0) if core else (cut, 1 - side, 1))
    pieces = [stem_tensor, cross, cycle]
    kept, *sent = branch_sums(mid_tensors, right_tensors, stems)
    got = [swap(x, 1) for x in sent]
    groups = [
        [
            (2 * side + group) * cuts + 2 * plane + column
            for side in range(stems // 2 - 1, -1, -1) for column in (1, 0) for plane in range(cuts // 2 - 1, -1, -1)
        ]
        for group in (0, 1)
    ]
    targets = [at % cuts for at in groups[0]]
    spread = close(pieces, kept, got, cuts, targets)
    parts = lax.all_to_all(spread, ("stem", "cuts"), 0, 0, tiled=True, axis_index_groups=groups)
    total = jnp.sum(parts.astype(jnp.float32), axis=0).reshape(-1)
    return total + swap(total, 1)


def solution(mesh):
    return jax.shard_map(
        on_device,
        mesh=mesh,
        in_specs=(
            P("stem", None, None),
            P(("cuts", "stem"), None, None),
            P(None, ("cuts", "stem"), None, None),
        ),
        out_specs=P("cuts"),
        check_vma=False,
    )
```

```python
import functools

import jax
import jax.numpy as jnp
import numpy as np
from jax import lax
from jax.experimental import pallas as pl
from jax.experimental.pallas import tpu as pltpu
from jax.sharding import PartitionSpec as P

MIB = 1024 * 1024
LEAVE_MIB = 49


def turn(x):
    half = x.shape[-1] // 2
    lane = lax.broadcasted_iota(jnp.int32, x.shape, x.ndim - 1)
    rolled = pltpu.roll(x, half, x.ndim - 1)
    return jnp.where(lane < half, -rolled, rolled)


def segments(blocks, depth, sizes):
    out, row = [], 0
    for piece, size in enumerate(sizes):
        end = row + size
        first = row
        while row < end:
            count = min(end, (row // depth + 1) * depth) - row
            out.append((row // depth, row % depth, piece, row - first, count))
            row += count
    return out


def piece_sizes(rows, count):
    size = -(-rows // (16 * count)) * 16
    return [min(size, rows - at) for at in range(0, rows, size)]


def product(mid_ref, wide_ref):
    pairs = mid_ref.shape[0]
    left = jnp.concatenate([mid_ref[j] for j in range(pairs)], axis=1)
    blocks, _, rows, width = wide_ref.shape
    if rows == width:
        right = [wide_ref[b].reshape(pairs * rows, width) for b in range(blocks)]
    else:
        right = []
        for b in range(blocks):
            both = []
            for j in range(pairs):
                upper = wide_ref[b, j]
                both += [upper, turn(upper.astype(jnp.float32)).astype(upper.dtype)]
            right.append(jnp.concatenate(both, axis=0))
    return jnp.dot(left, jnp.concatenate(right, axis=1), preferred_element_type=jnp.float32)


def leave_kernel(blocks, mid_hbm, right_hbm, mid_ref, stay_ref, *refs):
    *sent_refs, leave_ref, mid_sem, right_sem = refs
    pairs, depth, width = mid_ref.shape
    total, _, inner, _ = right_hbm.shape
    groups = total // blocks
    half = groups // 2
    me = lax.axis_index("stem")
    chunk = pairs // mid_sem.shape[0]

    def mid_copy(n):
        at = pl.ds(n * chunk, chunk)
        return pltpu.make_async_copy(mid_hbm.at[at], mid_ref.at[at], mid_sem.at[n])

    def right_copy(q, wide_ref, stays):
        side = (me // 2) ^ (me % 2) ^ stays ^ 1
        source = right_hbm.at[pl.ds((2 * side + q) * blocks, blocks)]
        target = wide_ref.at[pl.ds(q * blocks, blocks), :, pl.ds(0, inner)]
        return pltpu.make_async_copy(source, target, right_sem.at[stays * half + q])

    for q in range(half):
        right_copy(q, leave_ref, 0).start()
    for n in range(mid_sem.shape[0]):
        mid_copy(n).start()
    for q in range(half):
        right_copy(q, stay_ref, 1).start()

    def widen(wide_ref, stays):
        def step(q, carry):
            right_copy(q, wide_ref, stays).wait()
            for b in range(blocks):
                for j in range(pairs):
                    upper = wide_ref[q * blocks + b, j, :inner]
                    wide_ref[q * blocks + b, j, inner:] = turn(upper.astype(jnp.float32)).astype(upper.dtype)
            return carry

        lax.fori_loop(0, half, step, 0)

    widen(leave_ref, 0)
    for n in range(mid_sem.shape[0]):
        mid_copy(n).wait()
    sums = product(mid_ref, leave_ref)
    sizes = [ref.shape[0] for ref in sent_refs]
    for b, row, piece, at, count in segments(total // 2, depth, sizes):
        part = sums[row:row + count, b * width:(b + 1) * width]
        sent_refs[piece][at:at + count] = part.astype(jnp.bfloat16)
    for q in range(half):
        right_copy(q, stay_ref, 1).wait()


def stay_kernel(mid_ref, wide_ref, kept_ref):
    sums = product(mid_ref, wide_ref)
    width = kept_ref.shape[2]
    for b in range(kept_ref.shape[0]):
        kept_ref[b] = sums[:, b * width:(b + 1) * width]


def branch_sums(mid, right, groups):
    pairs, depth, width = mid.shape
    total, _, inner, _ = right.shape
    half = total // 2
    sizes = piece_sizes(half * depth, 3)
    wide = (half, pairs, 2 * inner, width)
    vmem = pl.BlockSpec(memory_space=pltpu.VMEM)
    hbm = pl.BlockSpec(memory_space=pltpu.HBM)
    cost = pl.CostEstimate(
        flops=depth * pairs * width * total * width, bytes_accessed=4 * MIB, transcendentals=0
    )
    mid_here, wide_here, *sent = pl.pallas_call(
        functools.partial(leave_kernel, total // groups),
        in_specs=[hbm, hbm],
        out_specs=[vmem] * (2 + len(sizes)),
        out_shape=[
            jax.ShapeDtypeStruct(mid.shape, mid.dtype),
            jax.ShapeDtypeStruct((half, pairs, inner, width), right.dtype),
        ] + [jax.ShapeDtypeStruct((size, width), jnp.bfloat16) for size in sizes],
        scratch_shapes=[
            pltpu.VMEM(wide, right.dtype),
            pltpu.SemaphoreType.DMA((4,)),
            pltpu.SemaphoreType.DMA((groups,)),
        ],
        compiler_params=pltpu.CompilerParams(vmem_limit_bytes=LEAVE_MIB * MIB),
        cost_estimate=cost,
        name="leave",
    )(mid, right)
    kept = pl.pallas_call(
        stay_kernel,
        out_shape=jax.ShapeDtypeStruct((half, depth, width), jnp.float32),
        compiler_params=pltpu.CompilerParams(vmem_limit_bytes=24 * MIB),
        cost_estimate=cost,
        name="stay",
    )(mid_here, wide_here)
    return kept, *sent


def close_kernel(targets, *refs):
    own_ref, cross_ref, cycle_ref, *got_refs, kept_ref, out_ref = refs
    first_core = lax.axis_index("stem") % 2 == 0
    pieces = segments(kept_ref.shape[0], kept_ref.shape[1], [ref.shape[0] for ref in got_refs])
    part = None
    at = 0
    for when_first, when_second in ((own_ref, cycle_ref), (cycle_ref, cross_ref)):
        for b in range(own_ref.shape[0]):
            block = jnp.where(first_core, when_first[b], when_second[b])
            half = block.shape[-1] // 2
            rows = jnp.concatenate([block[:, :half], block[:, half:]], axis=0)
            got = [got_refs[piece][row:row + count] for block_at, _, piece, row, count in pieces if block_at == at]
            sums = kept_ref[at] + jnp.concatenate(got, axis=0).astype(jnp.float32)
            high = sums.astype(jnp.bfloat16)
            low = (sums - high.astype(jnp.float32)).astype(jnp.bfloat16)
            term = jnp.dot(rows, jnp.concatenate([high, low], axis=1), preferred_element_type=jnp.float32)
            part = term if part is None else part + term
            at += 1
    width = part.shape[1] // 2
    part = part[:, :width] + part[:, width:]
    half = part.shape[0] // 2
    total = part[:half] + turn(part[half:])
    if targets is None:
        out_ref[...] = total
    else:
        rows = out_ref.shape[1]
        for at, c in enumerate(targets):
            out_ref[at] = total[c * rows:(c + 1) * rows]


def close(stems, kept, got, cuts, targets):
    rows, width = stems[0].shape[1], kept.shape[2]
    whole_tiles = rows % (8 * cuts) == 0
    shape = (len(targets), rows // cuts, width) if whole_tiles else (rows, width)
    out = pl.pallas_call(
        functools.partial(close_kernel, targets if whole_tiles else None),
        out_shape=jax.ShapeDtypeStruct(shape, jnp.float32),
        compiler_params=pltpu.CompilerParams(vmem_limit_bytes=24 * MIB),
        cost_estimate=pl.CostEstimate(flops=8 * rows * kept.size, bytes_accessed=MIB, transcendentals=0),
        name="close",
    )(*stems, *got, kept)
    return out if whole_tiles else out.reshape(cuts, -1)[np.array(targets)]


def on_device(stem_tensor, mid_tensors, right_tensors):
    stems = lax.axis_size("stem")
    cuts = lax.axis_size("cuts")

    def swap(x, p):
        return lax.ppermute(x, "stem", [(s, s ^ p) for s in range(stems)])

    def route(target):
        pairs = []
        for at in np.ndindex(cuts, 2, 2):
            cut, side, core = target(*at)
            pairs.append((at[0] * 4 + at[1] * 2 + at[2], cut * 4 + side * 2 + core))
        return lax.ppermute(stem_tensor, ("cuts", "stem"), pairs)

    assert stems == 4
    cross = route(lambda cut, side, core: (cut, 1 - side, 1) if core else (cut ^ 2, side, 0))
    cycle = route(lambda cut, side, core: (cut, side, 0) if core else (cut, 1 - side, 1))
    pieces = [stem_tensor, cross, cycle]
    kept, *sent = branch_sums(mid_tensors, right_tensors, stems)
    got = [swap(x, 1) for x in sent]
    groups = [
        [
            (2 * side + group) * cuts + 2 * plane + column
            for side in range(stems // 2 - 1, -1, -1) for plane in range(cuts // 2 - 1, -1, -1) for column in (1, 0)
        ]
        for group in (0, 1)
    ]
    targets = [at % cuts for at in groups[0]]
    spread = close(pieces, kept, got, cuts, targets)
    parts = lax.all_to_all(spread, ("stem", "cuts"), 0, 0, tiled=True, axis_index_groups=groups)
    total = jnp.sum(parts, axis=0).reshape(-1)
    return total + swap(total, 1)


def solution(mesh):
    return jax.shard_map(
        on_device,
        mesh=mesh,
        in_specs=(
            P("stem", None, None),
            P(("cuts", "stem"), None, None),
            P(None, ("cuts", "stem"), None, None),
        ),
        out_specs=P("cuts"),
        check_vma=False,
    )
```
